32 devices in a mesh: dp: 4 (over y, x), context: 2 (over core), tensor: 4 (over z).
Axes of the slice: x: 2, y: 2, z: 4, core: 2. Of those that a mesh axis runs over, the one named last changes fastest.
Arguments:
- inputs: bfloat16 [4096, 2048], P(('dp', 'context')), may hold values from -6 to 6
- cotangent: bfloat16 [4096, 2048], P(('dp', 'context')), may hold values from -6 to 6
- doc_lengths: int32 [4, 8], P('dp'), may hold values from 1 to 512, 1024 in all within a row
- gain_attn: float32 [2048], P(('dp', 'context')), may hold values from 0.5 to 1.5
- w_query: float32 [2048, 2048], P(('dp', 'context'), 'tensor'), may hold values from -0.125 to 0.125
- w_key: float32 [2048, 512], P(('dp', 'context'), 'tensor'), may hold values from -0.125 to 0.125
- w_value: float32 [2048, 512], P(('dp', 'context'), 'tensor'), may hold values from -0.125 to 0.125
- w_out: float32 [2048, 2048], P('tensor', ('dp', 'context')), may hold values from -0.375 to 0.375
- gain_mlp: float32 [2048], P(('dp', 'context')), may hold values from 0.5 to 1.5
- w_gate: float32 [2048, 8192], P(('dp', 'context'), 'tensor'), may hold values from -0.125 to 0.125
- w_up: float32 [2048, 8192], P(('dp', 'context'), 'tensor'), may hold values from -0.125 to 0.125
- w_down: float32 [8192, 2048], P('tensor', ('dp', 'context')), may hold values from -0.0625 to 0.0625
Outputs:
- activations: bfloat16 [4096, 2048], P(('dp', 'context'))
- input_grad: float32 [4096, 2048], P(('dp', 'context'))
- grad_gain_attn: float32 [2048], P(('dp', 'context'))
- grad_query: float32 [2048, 2048], P(('dp', 'context'), 'tensor')
- grad_key: float32 [2048, 512], P(('dp', 'context'), 'tensor')
- grad_value: float32 [2048, 512], P(('dp', 'context'), 'tensor')
- grad_out: float32 [2048, 2048], P('tensor', ('dp', 'context'))
- grad_gain_mlp: float32 [2048], P(('dp', 'context'))
- grad_gate: float32 [2048, 8192], P(('dp', 'context'), 'tensor')
- grad_up: float32 [2048, 8192], P(('dp', 'context'), 'tensor')
- grad_down: float32 [8192, 2048], P('tensor', ('dp', 'context'))
The draws below stay inside these ranges and needn't reach their ends.
Inputs may be any that keep to these rules, and one draw needn't show every extreme that they name: `doc_lengths`: each row lists the lengths of one sequence's 8 documents in order; they sum to 1024, and the longest is exactly 512.
All inputs are finite; a program needn't handle non-finite values.
Results may differ from the reference program's by a relative error of at most 0.014.
The reference program's roundings to bfloat16 on the way count: a program that leaves them out, or rounds other values in their place, can miss the bound.
Values may be sent and summed in bfloat16 or wider, within the bound.
A program may use at most 256 MiB of HBM per device.

```python
import math
import jax
import jax.numpy as jnp
import numpy as np
from jax import lax

D = 2048
H = 32
KV = 8
HD = 64
FF = 8192
NDOC = 8
SEQ_LEN = 1024
SEQS = 4
TOKENS = 4096


def level_of(rng, shape, pieces, smallest, top_value):
    loudness = 1.0
    for dim, shards_of in pieces:
        draws = jax.random.uniform(jax.random.fold_in(jax.random.fold_in(rng, 6), dim), (shards_of,), jnp.float32, smallest / len(pieces), top_value / len(pieces))
        loudness = loudness * jnp.repeat(jnp.exp(draws), shape[dim] // shards_of).reshape((-1,) + (1,) * (len(shape) - 1 - dim))
    return loudness


def profile(number_of, total, bound, skew):
    weights = [(1 << 20) // math.isqrt(grade ** skew) + 1 for grade in range(2, number_of + 1)]
    rest, given = total - bound - (number_of - 1), [1] * (number_of - 1)
    while rest > 0:
        movable = [i for i in range(number_of - 1) if given[i] < bound]
        mass, left = sum([weights[i] for i in movable]), rest
        for i in movable:
            extra = min(bound - given[i], max(1, left * weights[i] // mass), rest)
            given[i] = given[i] + extra
            rest = rest - extra
    return np.array([bound] + given)


def ragged(rng, amount, total, bound, slope):
    if amount == 2:
        one = jax.random.randint(rng, (), max(1, total - bound), min(bound, total - 1) + 1)
        return jnp.stack([one, total - one])
    sizes = jnp.asarray(profile(amount, total, bound, slope), jnp.int32)
    couples = (amount - 1) // 2
    donor, taker = sizes[1:1 + 2 * couples:2], sizes[2:2 + 2 * couples:2]
    slack = jnp.minimum(donor - 1, bound - taker)
    moved = jax.random.randint(jax.random.fold_in(rng, 1), (couples,), 0, 1 << 20) % (slack + 1)
    sizes = sizes.at[1:1 + 2 * couples:2].set(donor - moved).at[2:2 + 2 * couples:2].set(taker + moved)
    return sizes[jax.random.permutation(jax.random.fold_in(rng, 2), amount)]


def normal_values(key, dims, spread, most, split=(), kind=jnp.bfloat16):
    factor_of = level_of(key, dims, split, -0.22, 0.18) if split else 1.0
    result = jax.random.normal(key, dims, jnp.float32) * spread * factor_of
    return jnp.minimum(jnp.maximum(result, -most), most).astype(kind)


def setup_inputs(seed: int = 0) -> dict:
    keys = jax.random.split(jax.random.key(seed), 13)
    return {
        "inputs": normal_values(keys[0], (TOKENS, D), 1.0, 6.0, ((0, 8),)),
        "cotangent": normal_values(keys[1], (TOKENS, D), 1.0, 6.0, ((0, 8),)),
        "doc_lengths": jax.vmap(lambda own: ragged(own, NDOC, SEQ_LEN, SEQ_LEN // 2, 2))(jax.random.split(keys[2], SEQS)).reshape((SEQS, NDOC)).astype(jnp.int32),
        "gain_attn": jnp.clip(1.0 + 0.1 * jax.random.normal(keys[3], (D,), jnp.float32), 0.5, 1.5),
        "w_query": normal_values(keys[4], (D, H * HD), D ** -0.5, 0.125, ((0, 8), (1, 4)), jnp.float32),
        "w_key": normal_values(keys[5], (D, KV * HD), D ** -0.5, 0.125, ((0, 8), (1, 4)), jnp.float32),
        "w_value": normal_values(keys[6], (D, KV * HD), D ** -0.5, 0.125, ((0, 8), (1, 4)), jnp.float32),
        "w_out": normal_values(keys[7], (H * HD, D), (D // 8) ** -0.5, 0.375, ((0, 4), (1, 8)), jnp.float32),
        "gain_mlp": jnp.clip(1.0 + 0.1 * jax.random.normal(keys[8], (D,), jnp.float32), 0.5, 1.5),
        "w_gate": normal_values(keys[9], (D, FF), D ** -0.5, 0.125, ((0, 8), (1, 4)), jnp.float32),
        "w_up": normal_values(keys[10], (D, FF), D ** -0.5, 0.125, ((0, 8), (1, 4)), jnp.float32),
        "w_down": normal_values(keys[11], (FF, D), FF ** -0.5, 0.0625, ((0, 4), (1, 8)), jnp.float32),
    }


@jax.custom_vjp
def low(v):
    return lax.optimization_barrier(v.astype(jnp.bfloat16)).astype(jnp.float32)

@jax.custom_vjp
def low_back(v):
    return v

def low_keep(v):
    return (low(v), None)

def low_pass(kept, grad):
    return (grad,)

def back_keep(v):
    return (v, None)

def back_low(kept, grad):
    return (low(grad),)
low.defvjp(low_keep, low_pass)
low_back.defvjp(back_keep, back_low)
EPSILON = 1e-05
NEGATIVE = -1e+30
HIGHEST = lax.Precision.HIGHEST

def frequencies():
    exponent = jnp.arange(0, HD, 2).astype(jnp.float32) / HD
    initial = 1.0 / 500000.0 ** exponent
    wavelength = 2.0 * math.pi / initial
    smoothing = (8192.0 / wavelength - 1.0) / 3.0
    blended = (1.0 - smoothing) * initial / 32.0 + smoothing * initial
    return jnp.where(wavelength < 2048.0, initial, jnp.where(wavelength > 8192.0, initial / 32.0, blended))

def rope_tables(position):
    angles = position.astype(jnp.float32)[:, None] * frequencies()[None, :]
    cosine = jnp.cos(angles)
    sine_part = jnp.sin(angles)
    return (jnp.concatenate([cosine, cosine], -1), jnp.concatenate([sine_part, sine_part], -1))

def rotate(values, cosine, sine_part):
    middle = values.shape[-1] // 2
    turned = jnp.concatenate([-values[..., middle:], values[..., :middle]], -1)
    return values * cosine[:, None, :] + turned * sine_part[:, None, :]

def documents(lengths_row, seq_total):
    doc_ends = jnp.cumsum(lengths_row).astype(jnp.int32)
    doc_starts = (doc_ends - lengths_row).astype(jnp.int32)
    token_index = jnp.arange(seq_total, dtype=jnp.int32)
    segment = lax.optimization_barrier(jnp.sum((token_index[:, None] >= doc_ends[None, :]).astype(jnp.int32), 1)).astype(jnp.int32)
    member = segment[:, None] == jnp.arange(lengths_row.shape[0], dtype=jnp.int32)[None, :]
    position = (token_index - lax.optimization_barrier(jnp.sum(jnp.where(member, doc_starts[None, :], 0), 1))).astype(jnp.int32)
    return (segment, position)

def matmul(left, right):
    return jnp.dot(left, right, precision=HIGHEST, preferred_element_type=jnp.float32)

def norm_apply(source, gain_vector):
    rscale = lax.rsqrt(lax.optimization_barrier(jnp.mean(source * source, -1, keepdims=True)) + EPSILON)
    return source * rscale * gain_vector

def attention(queries, keys_all, values_all, segment):
    seq_total = queries.shape[0]
    block_rows = min(512, seq_total)
    per_group = queries.shape[1] // keys_all.shape[1]
    scale_factor = HD ** (-0.5)
    columns = jnp.arange(seq_total, dtype=jnp.int32)

    def one_block(first_row):
        query_blk = lax.dynamic_slice_in_dim(queries, first_row, block_rows, 0)
        query_blk = query_blk.reshape(block_rows, keys_all.shape[1], per_group, HD)
        row_ids = first_row + jnp.arange(block_rows, dtype=jnp.int32)
        seg_rows = lax.dynamic_slice_in_dim(segment, first_row, block_rows, 0)
        scores = jnp.einsum('bkgd,lkd->kgbl', query_blk, keys_all, precision=HIGHEST) * scale_factor
        scores = low_back(scores)
        allowed = (seg_rows[:, None] == segment[None, :]) & (columns[None, :] <= row_ids[:, None])
        scores = jnp.where(allowed, scores, NEGATIVE)
        highest = lax.optimization_barrier(jnp.max(scores, -1, keepdims=True))
        raw_weights = jnp.exp(scores - highest)
        soft_weights = low(raw_weights / lax.optimization_barrier(jnp.sum(raw_weights, -1, keepdims=True)))
        mixed_heads = jnp.einsum('kgbl,lkd->bkgd', soft_weights, values_all, precision=HIGHEST)
        return mixed_heads.reshape(block_rows, -1)
    first_rows = jnp.arange(seq_total // block_rows, dtype=jnp.int32) * block_rows
    return lax.map(jax.checkpoint(one_block), first_rows).reshape(seq_total, -1)

def layer_forward(source, gain_attn, w_query, w_key, w_value, w_out, gain_mlp, w_gate, w_up, w_down, segment, position):
    seq_total = source.shape[0]
    cosine, sine_part = rope_tables(position)
    normed = low(norm_apply(source, low(gain_attn)))
    queries = low_back(matmul(normed, low(w_query))).reshape(seq_total, -1, HD)
    queries = low(rotate(queries, cosine, sine_part))
    keys_all = low_back(matmul(normed, low(w_key))).reshape(seq_total, -1, HD)
    keys_all = low(rotate(keys_all, cosine, sine_part))
    values_all = low(low_back(matmul(normed, low(w_value)))).reshape(seq_total, -1, HD)
    mixed_heads = low(low_back(attention(queries, keys_all, values_all, segment)))
    branch = low_back(matmul(mixed_heads, low(w_out)))
    hidden_state = source + branch
    normed_mlp = low(norm_apply(hidden_state, low(gain_mlp)))
    gate_value = low_back(matmul(normed_mlp, low(w_gate)))
    upward = low_back(matmul(normed_mlp, low(w_up)))
    activated = low(gate_value * jax.nn.sigmoid(gate_value) * upward)
    return hidden_state + low_back(matmul(activated, low(w_down)))

def reference(inputs, cotangent, doc_lengths, gain_attn, w_query, w_key, w_value, w_out, gain_mlp, w_gate, w_up, w_down):
    params = (gain_attn, w_query, w_key, w_value, w_out, gain_mlp, w_gate, w_up, w_down)
    source_all = inputs.astype(jnp.float32).reshape(SEQS, SEQ_LEN, D)
    cot_all = cotangent.astype(jnp.float32).reshape(SEQS, SEQ_LEN, D)

    def one_sequence(summed, sequence_items):
        seq_source, seq_cot, lengths_row = sequence_items
        segment, position = documents(lengths_row, SEQ_LEN)

        def forward_fn(seq_source_in, *weights):
            return layer_forward(seq_source_in, *weights, segment, position)
        output, pullback = jax.vjp(forward_fn, seq_source, *params)
        gradients = pullback(seq_cot)
        summed = tuple((earlier + fresh_grad for earlier, fresh_grad in zip(summed, gradients[1:])))
        return (summed, (output.astype(jnp.bfloat16), gradients[0]))
    zero_totals = tuple((jnp.zeros(param.shape, jnp.float32) for param in params))
    summed, (outputs_all, input_grads) = lax.scan(one_sequence, zero_totals, (source_all, cot_all, doc_lengths))
    return (outputs_all.reshape(TOKENS, D), input_grads.reshape(TOKENS, D), summed[0], summed[1], summed[2], summed[3], summed[4], summed[5], summed[6], summed[7], summed[8])
```

```python
import math

import jax
import jax.numpy as jnp
from jax import lax
from jax.sharding import PartitionSpec as P

HD = 64


EPSILON = 1e-05
NEGATIVE = -1e30


def frequencies():
    exponent = jnp.arange(0, HD, 2).astype(jnp.float32) / HD
    initial = 1.0 / 500000.0**exponent
    wavelength = 2.0 * math.pi / initial
    smoothing = (8192.0 / wavelength - 1.0) / 3.0
    blended = (1.0 - smoothing) * initial / 32.0 + smoothing * initial
    return jnp.where(
        wavelength < 2048.0, initial, jnp.where(wavelength > 8192.0, initial / 32.0, blended)
    )


def rope_tables(position):
    angles = position.astype(jnp.float32)[:, None] * frequencies()[None, :]
    cosine = jnp.cos(angles)
    sine_part = jnp.sin(angles)
    return (jnp.concatenate([cosine, cosine], -1), jnp.concatenate([sine_part, sine_part], -1))


def rotate(values, cosine, sine_part):
    middle = values.shape[-1] // 2
    turned = jnp.concatenate([-values[..., middle:], values[..., :middle]], -1)
    return values * cosine[:, None, :] + turned * sine_part[:, None, :]


def unrotate(values, cosine, sine_part):
    middle = values.shape[-1] // 2
    scaled = values * sine_part[:, None, :]
    turned = jnp.concatenate([scaled[..., middle:], -scaled[..., :middle]], -1)
    return values * cosine[:, None, :] + turned


def documents(lengths_row, seq_total):
    doc_ends = jnp.cumsum(lengths_row)
    doc_starts = doc_ends - lengths_row
    token_index = jnp.arange(seq_total, dtype=jnp.int32)
    segment = jnp.sum((token_index[:, None] >= doc_ends[None, :]).astype(jnp.int32), 1)
    member = segment[:, None] == jnp.arange(lengths_row.shape[0], dtype=jnp.int32)[None, :]
    position = token_index - jnp.sum(jnp.where(member, doc_starts[None, :], 0), 1)
    return (segment, position)


def norm_forward(source, gain_vector):
    rscale = lax.rsqrt(jnp.mean(source * source, -1, keepdims=True) + EPSILON)
    scaled = source * rscale
    return ((scaled * gain_vector).astype(jnp.bfloat16), scaled, rscale)


def norm_backward(grad_normed, scaled, rscale, gain_vector):
    gain_grad = jnp.sum(grad_normed * scaled, 0)
    grad_scaled = grad_normed * gain_vector
    grad_source = rscale * (
        grad_scaled - scaled * jnp.mean(grad_scaled * scaled, -1, keepdims=True)
    )
    return (grad_source, gain_grad)


def block_scores(query_blk, first_row, keys_all, segment):
    length = query_blk.shape[0]
    row_ids = first_row + jnp.arange(length, dtype=jnp.int32)
    columns = jnp.arange(keys_all.shape[0], dtype=jnp.int32)
    seg_rows = lax.dynamic_slice_in_dim(segment, first_row, length, 0)
    allowed = (seg_rows[:, None] == segment[None, :]) & (columns[None, :] <= row_ids[:, None])
    scores = jnp.einsum(
        "bkgd,lkd->kgbl", query_blk, keys_all, preferred_element_type=jnp.float32
    ) * HD ** (-0.5)
    return jnp.where(allowed, scores, NEGATIVE)


def shards(
    inputs,
    cotangent,
    doc_lengths,
    gain_attn,
    w_query,
    w_key,
    w_value,
    w_out,
    gain_mlp,
    w_gate,
    w_up,
    w_down,
):
    tokens_here = inputs.shape[0]
    offset = lax.axis_index("context") * tokens_here
    segment, position = documents(doc_lengths[0], tokens_here * lax.axis_size("context"))
    cosine, sine_part = rope_tables(lax.dynamic_slice_in_dim(position, offset, tokens_here, 0))
    heads_here = w_query.shape[1] // HD
    groups_here = w_key.shape[1] // HD
    per_group = heads_here // groups_here
    block_rows = min(512, tokens_here)
    blocks = tokens_here // block_rows
    scale_factor = HD ** (-0.5)
    attention_copy = (
        gain_attn.astype(jnp.bfloat16),
        w_query.astype(jnp.bfloat16),
        w_key.astype(jnp.bfloat16),
        w_value.astype(jnp.bfloat16),
        w_out.astype(jnp.bfloat16),
    )
    mlp_copy = (
        gain_mlp.astype(jnp.bfloat16),
        w_gate.astype(jnp.bfloat16),
        w_up.astype(jnp.bfloat16),
        w_down.astype(jnp.bfloat16),
    )
    gain_one, query_full, key_full, value_full, out_full = (
        lax.all_gather(attention_copy[0], ("dp", "context"), axis=0, tiled=True),
        lax.all_gather(attention_copy[1], ("dp", "context"), axis=0, tiled=True),
        lax.all_gather(attention_copy[2], ("dp", "context"), axis=0, tiled=True),
        lax.all_gather(attention_copy[3], ("dp", "context"), axis=0, tiled=True),
        lax.all_gather(attention_copy[4], ("dp", "context"), axis=1, tiled=True),
    )
    gain_one_f = gain_one.astype(jnp.float32)
    source = inputs.astype(jnp.float32)
    grad_output = cotangent.astype(jnp.float32)
    normed, scaled_one, rscale_one = norm_forward(source, gain_one_f)
    queries = jnp.dot(normed, query_full, preferred_element_type=jnp.float32).reshape(
        tokens_here, heads_here, HD
    )
    queries = rotate(queries, cosine, sine_part).astype(jnp.bfloat16)
    keys_here = jnp.dot(normed, key_full, preferred_element_type=jnp.float32).reshape(
        tokens_here, groups_here, HD
    )
    keys_here = rotate(keys_here, cosine, sine_part).astype(jnp.bfloat16)
    values_here = (
        jnp.dot(normed, value_full, preferred_element_type=jnp.float32)
        .astype(jnp.bfloat16)
        .reshape(tokens_here, groups_here, HD)
    )
    keys_all, values_all = (
        lax.all_gather(keys_here, "context", axis=0, tiled=True),
        lax.all_gather(values_here, "context", axis=0, tiled=True),
    )
    query_blocks = queries.reshape(blocks, block_rows, groups_here, per_group, HD)
    block_starts = offset + jnp.arange(blocks, dtype=jnp.int32) * block_rows

    def forward_block(block_items):
        query_blk, first_row = block_items
        scores = block_scores(query_blk, first_row, keys_all, segment)
        highest = jnp.max(scores, -1, keepdims=True)
        raw_weights = jnp.exp(scores - highest)
        totals = jnp.sum(raw_weights, -1, keepdims=True)
        soft_weights = (raw_weights / totals).astype(jnp.bfloat16)
        mixed_blk = jnp.einsum(
            "kgbl,lkd->bkgd", soft_weights, values_all, preferred_element_type=jnp.float32
        )
        return (mixed_blk.astype(jnp.bfloat16), highest[..., 0] + jnp.log(totals[..., 0]))

    mixed_blocks, log_totals = lax.map(forward_block, (query_blocks, block_starts))
    mixed_heads = mixed_blocks.reshape(tokens_here, heads_here * HD)
    attention_terms = jnp.dot(mixed_heads, out_full, preferred_element_type=jnp.float32)
    gain_two, gate_full, up_full, down_full = (
        lax.all_gather(mlp_copy[0], ("dp", "context"), axis=0, tiled=True),
        lax.all_gather(mlp_copy[1], ("dp", "context"), axis=0, tiled=True),
        lax.all_gather(mlp_copy[2], ("dp", "context"), axis=0, tiled=True),
        lax.all_gather(mlp_copy[3], ("dp", "context"), axis=1, tiled=True),
    )
    gain_two_f = gain_two.astype(jnp.float32)
    branch = lax.psum(attention_terms.astype(jnp.bfloat16), "tensor").astype(jnp.float32)
    hidden_state = source + branch
    normed_mlp, scaled_two, rscale_two = norm_forward(hidden_state, gain_two_f)
    gate_value = jnp.dot(normed_mlp, gate_full, preferred_element_type=jnp.float32)
    upward = jnp.dot(normed_mlp, up_full, preferred_element_type=jnp.float32)
    sigmoid_gate = jax.nn.sigmoid(gate_value)
    swish_gate = gate_value * sigmoid_gate
    activated = (swish_gate * upward).astype(jnp.bfloat16)
    mlp_terms = jnp.dot(activated, down_full, preferred_element_type=jnp.float32)
    mlp_branch = lax.psum(mlp_terms.astype(jnp.bfloat16), "tensor").astype(jnp.float32)
    activations = (hidden_state + mlp_branch).astype(jnp.bfloat16)
    grad_down = jnp.einsum("tf,td->fd", activated, cotangent, preferred_element_type=jnp.float32)
    grad_activated = jnp.einsum(
        "td,fd->tf", cotangent, down_full, preferred_element_type=jnp.float32
    )
    grad_gate_in = (
        grad_activated * upward * sigmoid_gate * (1.0 + gate_value * (1.0 - sigmoid_gate))
    ).astype(jnp.bfloat16)
    grad_upward = (grad_activated * swish_gate).astype(jnp.bfloat16)
    grad_gate = jnp.einsum(
        "td,tf->df", normed_mlp, grad_gate_in, preferred_element_type=jnp.float32
    )
    grad_up = jnp.einsum("td,tf->df", normed_mlp, grad_upward, preferred_element_type=jnp.float32)
    partial_two = jnp.einsum(
        "tf,df->td", grad_gate_in, gate_full, preferred_element_type=jnp.float32
    )
    partial_two = partial_two + jnp.einsum(
        "tf,df->td", grad_upward, up_full, preferred_element_type=jnp.float32
    )
    grad_normed_mlp = lax.psum(partial_two.astype(jnp.bfloat16), "tensor").astype(jnp.float32)
    grad_hidden, gain_grad_two = norm_backward(grad_normed_mlp, scaled_two, rscale_two, gain_two_f)
    grad_hidden = grad_hidden + grad_output
    grad_branch = grad_hidden.astype(jnp.bfloat16)
    grad_gate_own, grad_up_own, grad_down_own = (
        lax.psum_scatter(grad_gate.astype(jnp.bfloat16), ("dp", "context"), scatter_dimension=0, tiled=True).astype(jnp.float32),
        lax.psum_scatter(grad_up.astype(jnp.bfloat16), ("dp", "context"), scatter_dimension=0, tiled=True).astype(jnp.float32),
        lax.psum_scatter(grad_down.astype(jnp.bfloat16), ("dp", "context"), scatter_dimension=1, tiled=True).astype(jnp.float32),
    )
    grad_out = jnp.einsum("te,td->ed", mixed_heads, grad_branch, preferred_element_type=jnp.float32)
    grad_mixed = jnp.einsum(
        "td,ed->te", grad_branch, out_full, preferred_element_type=jnp.float32
    ).astype(jnp.bfloat16)
    grad_mixed_blocks = grad_mixed.reshape(blocks, block_rows, groups_here, per_group, HD)

    def backward_block(running, block_items):
        key_acc, value_acc = running
        query_blk, first_row, grad_blk, log_blk = block_items
        scores = block_scores(query_blk, first_row, keys_all, segment)
        soft_weights = jnp.exp(scores - log_blk[..., None])
        dprobs = jnp.einsum(
            "bkgd,lkd->kgbl", grad_blk, values_all, preferred_element_type=jnp.float32
        )
        row_delta = jnp.sum(soft_weights * dprobs, -1, keepdims=True)
        dscores = (soft_weights * (dprobs - row_delta)).astype(jnp.bfloat16)
        dquery = (
            jnp.einsum("kgbl,lkd->bkgd", dscores, keys_all, preferred_element_type=jnp.float32)
            * scale_factor
        )
        key_acc = (
            key_acc
            + jnp.einsum("kgbl,bkgd->lkd", dscores, query_blk, preferred_element_type=jnp.float32)
            * scale_factor
        )
        value_acc = value_acc + jnp.einsum(
            "kgbl,bkgd->lkd",
            soft_weights.astype(jnp.bfloat16),
            grad_blk,
            preferred_element_type=jnp.float32,
        )
        return ((key_acc, value_acc), dquery)

    zero_keys = jnp.zeros(keys_all.shape, jnp.float32)
    (key_acc, value_acc), dquery_blocks = lax.scan(
        backward_block,
        (zero_keys, zero_keys),
        (query_blocks, block_starts, grad_mixed_blocks, log_totals),
    )
    key_grad, value_grad = (
        lax.psum_scatter(key_acc, "context", scatter_dimension=0, tiled=True),
        lax.psum_scatter(value_acc, "context", scatter_dimension=0, tiled=True),
    )
    grad_key_in = (
        unrotate(key_grad, cosine, sine_part)
        .astype(jnp.bfloat16)
        .reshape(tokens_here, groups_here * HD)
    )
    grad_value_in = value_grad.astype(jnp.bfloat16).reshape(tokens_here, groups_here * HD)
    grad_query_in = (
        unrotate(dquery_blocks.reshape(tokens_here, heads_here, HD), cosine, sine_part)
        .astype(jnp.bfloat16)
        .reshape(tokens_here, heads_here * HD)
    )
    grad_query = jnp.einsum("td,te->de", normed, grad_query_in, preferred_element_type=jnp.float32)
    grad_key = jnp.einsum("td,te->de", normed, grad_key_in, preferred_element_type=jnp.float32)
    grad_value = jnp.einsum("td,te->de", normed, grad_value_in, preferred_element_type=jnp.float32)
    partial_one = jnp.einsum(
        "te,de->td", grad_query_in, query_full, preferred_element_type=jnp.float32
    )
    partial_one = partial_one + jnp.einsum(
        "te,de->td", grad_key_in, key_full, preferred_element_type=jnp.float32
    )
    partial_one = partial_one + jnp.einsum(
        "te,de->td", grad_value_in, value_full, preferred_element_type=jnp.float32
    )
    grad_normed = lax.psum(partial_one.astype(jnp.bfloat16), "tensor").astype(jnp.float32)
    grad_source, gain_grad_one = norm_backward(grad_normed, scaled_one, rscale_one, gain_one_f)
    input_grad = grad_source + grad_hidden
    gain_total_one, gain_total_two = (gain_grad_one, gain_grad_two)
    grad_gain_attn, grad_gain_mlp, grad_query_own, grad_key_own, grad_value_own, grad_out_own = (
        lax.psum_scatter(gain_total_one, ("dp", "context"), scatter_dimension=0, tiled=True),
        lax.psum_scatter(gain_total_two, ("dp", "context"), scatter_dimension=0, tiled=True),
        lax.psum_scatter(grad_query.astype(jnp.bfloat16), ("dp", "context"), scatter_dimension=0, tiled=True).astype(jnp.float32),
        lax.psum_scatter(grad_key.astype(jnp.bfloat16), ("dp", "context"), scatter_dimension=0, tiled=True).astype(jnp.float32),
        lax.psum_scatter(grad_value.astype(jnp.bfloat16), ("dp", "context"), scatter_dimension=0, tiled=True).astype(jnp.float32),
        lax.psum_scatter(grad_out.astype(jnp.bfloat16), ("dp", "context"), scatter_dimension=1, tiled=True).astype(jnp.float32),
    )
    return (
        activations,
        input_grad,
        grad_gain_attn,
        grad_query_own,
        grad_key_own,
        grad_value_own,
        grad_out_own,
        grad_gain_mlp,
        grad_gate_own,
        grad_up_own,
        grad_down_own,
    )


def solution(mesh):
    return jax.shard_map(
        shards,
        mesh=mesh,
        in_specs=(
            P(("dp", "context"), None),
            P(("dp", "context"), None),
            P("dp", None),
            P(("dp", "context")),
            P(("dp", "context"), "tensor"),
            P(("dp", "context"), "tensor"),
            P(("dp", "context"), "tensor"),
            P("tensor", ("dp", "context")),
            P(("dp", "context")),
            P(("dp", "context"), "tensor"),
            P(("dp", "context"), "tensor"),
            P("tensor", ("dp", "context")),
        ),
        out_specs=(
            P(("dp", "context"), None),
            P(("dp", "context"), None),
            P(("dp", "context")),
            P(("dp", "context"), "tensor"),
            P(("dp", "context"), "tensor"),
            P(("dp", "context"), "tensor"),
            P("tensor", ("dp", "context")),
            P(("dp", "context")),
            P(("dp", "context"), "tensor"),
            P(("dp", "context"), "tensor"),
            P("tensor", ("dp", "context")),
        ),
        check_vma=False,
    )
```

```python
import functools
import math

import jax
import jax.numpy as jnp
from jax import lax
from jax.experimental import pallas as pl
from jax.experimental.pallas import tpu as pltpu
from jax.sharding import PartitionSpec as P

HD = 64
WINDOW = 512
QROWS = 256
EPSILON = 1e-05
NEGATIVE = -1e30
MESH = pl.DeviceIdType.MESH
F32 = jnp.float32
BF16 = jnp.bfloat16
NN = (((1,), (0,)), ((), ()))
NT = (((1,), (1,)), ((), ()))
TN = (((0,), (0,)), ((), ()))
VMEM_LIMIT = 62 * 2**20


def dot(left, right, dims=NN):
    return lax.dot_general(left, right, dims, preferred_element_type=F32)


def frequencies():
    exponent = jnp.arange(0, HD, 2).astype(jnp.float32) / HD
    initial = 1.0 / 500000.0**exponent
    wavelength = 2.0 * math.pi / initial
    smoothing = (8192.0 / wavelength - 1.0) / 3.0
    blended = (1.0 - smoothing) * initial / 32.0 + smoothing * initial
    return jnp.where(
        wavelength < 2048.0, initial, jnp.where(wavelength > 8192.0, initial / 32.0, blended)
    )


def aligned(index, size):
    return pl.ds(pl.multiple_of(index * size, size), size)


class Place:
    def __init__(self, dp, tensor):
        self.dp, self.tensor = dp, tensor
        self.bits = dp.bit_length() - 1
        self.p = lax.axis_index("dp")
        self.c = lax.axis_index("context")
        self.t = lax.axis_index("tensor")
        self.core = (self.p, 1 - self.c, self.t)
        self.low = lax.rem(lax.div(self.t * 2, tensor), 2)
        self.early = 1 - self.low
        self.late = self.low
        step = 1 - 2 * self.low
        self.inward = (self.p, self.c, self.t + step)
        self.outward = (self.p, self.c, self.t - step)
        edge = self.low * (tensor - 1 - self.t) + (1 - self.low) * self.t
        self.depth = edge
        self.at_end = edge == 0

    def flipped(self, mask):
        position = self.p
        for b in range(self.bits):
            if mask >> b & 1:
                bit = lax.rem(lax.div(self.p, 2**b), 2)
                position = position + (1 - 2 * bit) * 2**b
        return position

    def across(self, b):
        return (self.flipped(1 << b), self.c, self.t)

    def greet(self):
        barrier = pltpu.get_barrier_semaphore()
        for device in [self.core] + [self.across(b) for b in range(self.bits)] + [self.inward]:
            pl.semaphore_signal(barrier, inc=1, device_id=device, device_id_type=MESH)

        @pl.when(jnp.logical_not(self.at_end))
        def _():
            pl.semaphore_signal(barrier, inc=1, device_id=self.outward, device_id_type=MESH)

    def meet(self):
        barrier = pltpu.get_barrier_semaphore()

        @pl.when(self.at_end)
        def _():
            pl.semaphore_wait(barrier, 2 + self.bits)

        @pl.when(jnp.logical_not(self.at_end))
        def _():
            pl.semaphore_wait(barrier, 3 + self.bits)


def remote(source, target, send, receive, device):
    return pltpu.make_async_remote_copy(
        src_ref=source,
        dst_ref=target,
        send_sem=send,
        recv_sem=receive,
        device_id=device,
        device_id_type=MESH,
    )


def orders_of(bits, halves):
    forward = tuple(range(bits))
    return (forward, forward[::-1]) if halves == 2 else (forward,)


def phase_masks(order, phase):
    masks = [0]
    for b in order[:phase]:
        masks = masks + [m | 1 << b for m in masks]
    return [m | 1 << order[phase] for m in masks]


class Gather:
    def __init__(self, place, shard, full, axis, sems, halves=2):
        self.place, self.shard, self.full, self.axis = place, shard, full, axis
        self.halves = halves
        self.send, self.receive, self.core_send, self.core_receive, self.local = sems
        self.orders = orders_of(place.bits, halves)
        self.rows = shard.shape[0] // halves
        self.sends = []

    @staticmethod
    def semaphores(dp, halves=2):
        bits = dp.bit_length() - 1
        return [
            pltpu.SemaphoreType.DMA((halves, dp, max(bits, 1))),
            pltpu.SemaphoreType.DMA((halves, dp)),
            pltpu.SemaphoreType.DMA((halves, dp)),
            pltpu.SemaphoreType.DMA((halves, dp)),
            pltpu.SemaphoreType.DMA((1,)),
        ]

    def part(self, half):
        return self.shard.at[pl.ds(half * self.rows, self.rows)]

    def slot(self, position, core, half):
        index = position * 2 + core
        if self.axis == 0:
            rows = self.shard.shape[0]
            first = pl.multiple_of(index * rows + half * self.rows, self.rows)
            return self.full.at[pl.ds(first, self.rows)]
        return self.full.at[
            pl.ds(half * self.rows, self.rows), aligned(index, self.shard.shape[1])
        ]

    def _forward(self, half, mask, source):
        place = self.place
        order = self.orders[half]
        last = max([order.index(b) for b in order if mask >> b & 1], default=-1)
        target = self.slot(place.flipped(mask), place.c, half)
        for j in range(last + 1, place.bits):
            copy = remote(
                source,
                target,
                self.send.at[half, mask, j],
                self.receive.at[half, mask | 1 << order[j]],
                place.across(order[j]),
            )
            copy.start()
            self.sends.append(copy)
        copy = remote(
            source,
            target,
            self.core_send.at[half, mask],
            self.core_receive.at[half, mask],
            place.core,
        )
        copy.start()
        self.sends.append(copy)

    def start(self):
        place = self.place
        for half in range(self.halves):
            self._forward(half, 0, self.part(half))
        index = place.p * 2 + place.c
        if self.axis == 0:
            own = self.full.at[aligned(index, self.shard.shape[0])]
        else:
            own = self.full.at[:, aligned(index, self.shard.shape[1])]
        self.own = pltpu.make_async_copy(self.shard, own, self.local.at[0])
        self.own.start()

    def pass_on(self, phase):
        place = self.place
        for half in range(self.halves):
            for mask in phase_masks(self.orders[half], phase):
                source = self.slot(place.flipped(mask), place.c, half)
                remote(
                    source,
                    source,
                    self.send.at[half, mask, 0],
                    self.receive.at[half, mask],
                    place.core,
                ).wait_recv()
                self._forward(half, mask, source)

    def finish(self):
        place = self.place
        self.own.wait()
        for half in range(self.halves):
            for mask in range(place.dp):
                target = self.slot(place.flipped(mask), 1 - place.c, half)
                remote(
                    target,
                    target,
                    self.core_send.at[half, mask],
                    self.core_receive.at[half, mask],
                    place.core,
                ).wait_recv()

    def drain(self):
        for copy in self.sends:
            copy.wait_send()
        self.sends = []


class LineSum:
    lags = (0, 3, 5, 7)

    def __init__(self, place, part, inbox, result, sems, pieces, root):
        self.place, self.part, self.inbox, self.result = place, part, inbox, result
        self.sum_send, self.sum_receive, self.back_send, self.back_receive = sems
        self.pieces = pieces
        self.rows = part.shape[1] // pieces
        self.rounds = pieces + self.lags[-1]
        self.root = root

    @staticmethod
    def semaphores(pieces):
        return [pltpu.SemaphoreType.DMA((2, pieces))] * 4

    def _copy(self, kind, flow, i, device):
        rows = aligned(i, self.rows)
        if kind == "sum":
            return remote(
                self.part.at[flow, rows],
                self.inbox.at[flow, rows],
                self.sum_send.at[flow, i],
                self.sum_receive.at[flow, i],
                device,
            )
        return remote(
            self.result.at[flow, rows],
            self.result.at[flow, rows],
            self.back_send.at[flow, i],
            self.back_receive.at[flow, i],
            device,
        )

    def _add(self, flow, i):
        rows = aligned(i, self.rows)
        total = self.part[flow, rows].astype(F32) + self.inbox[flow, rows].astype(F32)
        self.part[flow, rows] = total.astype(BF16)

    def early_start(self):
        @pl.when(self.place.at_end)
        def _():
            def one(i, carry):
                self._copy("sum", self.place.early, i, self.place.inward).start()
                return carry

            lax.fori_loop(0, self.pieces, one, 0)

    def early_sum(self, i):
        place = self.place

        @pl.when(jnp.logical_not(place.at_end))
        def _():
            copy = self._copy("sum", place.early, i, place.inward)
            copy.wait_recv()
            self._add(place.early, i)
            copy.start()

    def late_sum(self, i):
        place = self.place
        copy = self._copy("sum", place.late, i, place.outward)
        copy.wait_recv()

        @pl.when(jnp.logical_not(place.at_end))
        def _():
            self._add(place.late, i)
            copy.start()

        @pl.when(place.at_end)
        def _():
            rows = aligned(i, self.rows)
            total = self.part[place.late, rows].astype(F32)
            total = total + self.inbox[place.late, rows].astype(F32)
            self.root(i, rows, total)
            self._copy("back", place.late, i, place.inward).start()

    def late_back(self, i):
        place = self.place

        @pl.when(jnp.logical_not(place.at_end))
        def _():
            copy = self._copy("back", place.late, i, place.inward)
            copy.wait_recv()
            copy.start()

    def early_back(self, i):
        place = self.place
        copy = self._copy("back", place.early, i, place.outward)
        copy.wait_recv()

        @pl.when(jnp.logical_not(place.at_end))
        def _():
            copy.start()

    def round(self, n):
        for lag, kind in zip(self.lags, ("early_sum", "late_sum", "late_back", "early_back")):
            i = n - lag
            if isinstance(i, int):
                if 0 <= i < self.pieces:
                    getattr(self, kind)(i)
            else:

                @pl.when((i >= 0) & (i < self.pieces))
                def _(kind=kind, i=i):
                    getattr(self, kind)(i)

    def run(self, first, last):
        def one(n, carry):
            self.round(n)
            return carry

        lax.fori_loop(first, last, one, 0)

    def drain(self):
        place = self.place

        def one(i, carry):
            self._copy("sum", place.early, i, place.inward).wait_send()
            self._copy("back", place.late, i, place.inward).wait_send()

            @pl.when(jnp.logical_not(place.at_end))
            def _():
                self._copy("sum", place.late, i, place.outward).wait_send()
                self._copy("back", place.early, i, place.outward).wait_send()

            return carry

        lax.fori_loop(0, self.pieces, one, 0)


class Scatter:
    def __init__(self, place, part, inbox, out, axis, sems):
        self.place, self.part, self.inbox, self.out, self.axis = place, part, inbox, out, axis
        self.send, self.receive, self.local = sems
        self.orders = orders_of(place.bits, 2)
        self.rows = out.shape[1] // 2
        self.sends = []

    @staticmethod
    def semaphores(dp):
        return [
            pltpu.SemaphoreType.DMA((2, dp)),
            pltpu.SemaphoreType.DMA((2, dp)),
            pltpu.SemaphoreType.DMA((1,)),
        ]

    @staticmethod
    def inbox_shape(dp, rows, columns):
        slots = sum(2**phase - 1 for phase in range(1, dp.bit_length() - 1))
        return (2, max(slots, 1), rows // 2, columns)

    def slot(self, position, half):
        if self.axis == 0:
            rows = self.out.shape[1]
            first = pl.multiple_of(position * rows + half * self.rows, self.rows)
            return self.part.at[pl.ds(first, self.rows)]
        return self.part.at[
            pl.ds(half * self.rows, self.rows), aligned(position, self.out.shape[2])
        ]

    def landing(self, half, phase, mask):
        if mask == 0:
            return self.out.at[1 + phase, pl.ds(half * self.rows, self.rows)]
        return self.inbox.at[half, self.code(half, phase, mask)]

    def code(self, half, phase, mask):
        order = self.orders[half]
        number = 0
        for later in range(self.place.bits - 1, phase, -1):
            number += 2**later - 1
        inside = [m for m in range(1, self.place.dp) if all(b in order[:phase] for b in bits_of(m))]
        return number + inside.index(mask)

    def _copies(self, half, phase):
        order = self.orders[half]
        b = order[phase]
        for mask in phase_masks(order, phase):
            yield remote(
                self.slot(self.place.flipped(mask), half),
                self.landing(half, phase, mask & ~(1 << b)),
                self.send.at[half, mask],
                self.receive.at[half, mask],
                self.place.across(b),
            )

    def start(self):
        place = self.place
        index = place.p
        if self.axis == 0:
            own = self.part.at[aligned(index, self.out.shape[1])]
        else:
            own = self.part.at[:, aligned(index, self.out.shape[2])]
        self.own = pltpu.make_async_copy(own, self.out.at[0], self.local.at[0])
        self.own.start()
        if place.bits:
            self._send(place.bits - 1)

    def _send(self, phase):
        for half in range(2):
            for copy in self._copies(half, phase):
                copy.start()
                self.sends.append(copy)

    def pass_on(self, phase):
        for half in range(2):
            order = self.orders[half]
            for copy, mask in zip(self._copies(half, phase), phase_masks(order, phase)):
                rest = mask & ~(1 << order[phase])
                if rest:
                    copy.wait_recv()
                    target = self.slot(self.place.flipped(rest), half)
                    source = self.landing(half, phase, rest)
                    pieces = max(1, self.rows // 64)
                    size = self.rows // pieces

                    def add(i, carry, target=target, source=source, size=size):
                        rows = aligned(i, size)
                        total = target[rows].astype(F32) + source[rows].astype(F32)
                        target[rows] = total.astype(BF16)
                        return carry

                    lax.fori_loop(0, pieces, add, 0)
        self._send(phase - 1)

    def finish(self):
        self.own.wait()
        for phase in range(self.place.bits):
            for half in range(2):
                order = self.orders[half]
                for copy, mask in zip(self._copies(half, phase), phase_masks(order, phase)):
                    if not mask & ~(1 << order[phase]):
                        copy.wait_recv()
        for copy in self.sends:
            copy.wait_send()
        self.sends = []


def bits_of(mask):
    return [b for b in range(mask.bit_length()) if mask >> b & 1]


def turned(z):
    width = z.shape[-1]
    half = HD // 2
    if width == 2 * HD:
        lane = lax.broadcasted_iota(jnp.int32, z.shape, 1)
        return jnp.where(lax.rem(lane, HD) < half, pltpu.roll(z, width - half, 1), pltpu.roll(z, half, 1))
    pieces = []
    for h in range(width // HD):
        pieces += [z[:, h * HD + half : (h + 1) * HD], z[:, h * HD : h * HD + half]]
    return jnp.concatenate(pieces, -1)


def document_starts(lengths, rows):
    starts = jnp.zeros(rows.shape, jnp.int32)
    end = lengths[0, 0]
    for k in range(lengths.shape[1]):
        starts = jnp.where(rows >= end, end, starts)
        if k + 1 < lengths.shape[1]:
            end = end + lengths[0, k + 1]
    return starts


def tables(place, lengths, freq, cosine, sine, tokens):
    rows = lax.broadcasted_iota(jnp.int32, (tokens, 128), 0) + place.c * tokens
    angle = (rows - document_starts(lengths, rows)).astype(F32) * freq[0:1, :]
    lane = lax.broadcasted_iota(jnp.int32, (tokens, 128), 1)
    cosine[...] = jnp.cos(angle)
    turned_sine = jnp.sin(angle)
    sine[...] = jnp.where(lax.rem(lane, HD) < HD // 2, -turned_sine, turned_sine)


def fill_bias(place, lengths, bias, tokens):
    keys = bias.shape[1]
    for b in range(tokens // QROWS):
        shape = (keys, QROWS)
        query = lax.broadcasted_iota(jnp.int32, shape, 1) + (place.c * tokens + b * QROWS)
        key = lax.broadcasted_iota(jnp.int32, shape, 0) + place.c * b * QROWS
        row = lax.broadcasted_iota(jnp.int32, (8, QROWS), 1) + (place.c * tokens + b * QROWS)
        starts = document_starts(lengths, row)[0:1, :]
        bias[b] = jnp.where((key >= starts) & (key <= query), 0.0, NEGATIVE)


def softmax_of(key, query, bias):
    scores = dot(key, query, NT) + bias
    highest = jnp.max(scores, 0, keepdims=True)
    raw = jnp.exp(scores - highest)
    return raw * (1.0 / jnp.sum(raw, 0, keepdims=True))


def forward_kernel(cfg, *refs):
    (
        x_in, lengths, freq, gains_in, wq_in, wk_in, wv_in, wo_in, wg_in, wu_in, wd_in,
        qkv_out, wo_out, wg_full, wu_full, wd_full, gains_out,
        normed_out, q_out, k_out, v_out, mixed_out, hidden_out, normed_mlp_out,
        x, wq, wk, wv, wo, wg, wu, wd, gains32,
        sqkv, swo, swg, swu, swd, sgains,
        wqkv, wout, gains, normed, rscale, cosine, sine, bias,
        qh, kh, vh, kv, kv_in, mixed, part, inbox, result, hidden,
        load, store, kv_send, kv_receive, *sems,
    ) = refs
    place = Place(cfg.dp, cfg.tensor)
    tokens, width = x.shape
    heads, groups = cfg.heads, cfg.groups
    query_width, key_width = heads * HD, groups * HD
    loads = []
    for i, (source, target) in enumerate(
        [(gains_in, gains32), (wq_in, wq), (wk_in, wk), (wv_in, wv), (x_in, x), (wo_in, wo), (wg_in, wg), (wu_in, wu), (wd_in, wd)]
    ):
        copy = pltpu.make_async_copy(source, target, load.at[i])
        copy.start()
        loads.append(copy)
    place.greet()
    gathers = []
    for i, (shard, full, axis, halves) in enumerate(
        [
            (sgains, gains, 1, 1),
            (sqkv, wqkv, 0, 2),
            (swo, wout, 1, 2),
            (swg, wg_full, 0, 2),
            (swu, wu_full, 0, 2),
            (swd, wd_full, 1, 2),
        ]
    ):
        gathers.append(Gather(place, shard, full, axis, sems[5 * i : 5 * i + 5], halves))
    g_gains, g_qkv, g_wo, g_wg, g_wu, g_wd = gathers
    line_sems = sems[5 * len(gathers) :]
    for i in range(4):
        loads[i].wait()
    sgains[...] = gains32[...].astype(BF16)
    sqkv[:, :query_width] = wq[...].astype(BF16)
    sqkv[:, query_width : query_width + key_width] = wk[...].astype(BF16)
    sqkv[:, query_width + key_width :] = wv[...].astype(BF16)
    place.meet()
    g_gains.start()
    g_qkv.start()
    loads[5].wait()
    swo[...] = wo[...].astype(BF16)
    for i, (raw, staged) in enumerate([(wg, swg), (wu, swu), (wd, swd)]):
        loads[6 + i].wait()
        pieces = 8
        for n in range(pieces):
            rows = pl.ds(n * (raw.shape[0] // pieces), raw.shape[0] // pieces)
            staged[rows] = raw[rows].astype(BF16)
    for phase in range(place.bits):
        g_gains.pass_on(phase)
        g_qkv.pass_on(phase)
        if phase == 0:
            g_wo.start()
            g_wg.start()
            g_wu.start()
            g_wd.start()
            loads[4].wait()
            rows_at = 64

            def scale(i, carry):
                rows = aligned(i, rows_at)
                block = x[rows].astype(F32)
                mean = jnp.sum(block * block, -1, keepdims=True) * (1.0 / width)
                rscale[rows] = lax.rsqrt(mean + EPSILON)
                return carry

            lax.fori_loop(0, tokens // rows_at, scale, 0)
            tables(place, lengths, freq, cosine, sine, tokens)
            fill_bias(place, lengths, bias, tokens)
    g_gains.finish()

    def norm(i, carry):
        rows = aligned(i, 64)
        scaled = x[rows].astype(F32) * rscale[rows]
        normed[rows] = (scaled * gains[0:1, :].astype(F32)).astype(BF16)
        return carry

    lax.fori_loop(0, tokens // 64, norm, 0)
    stores = []

    def keep(source, target):
        copy = pltpu.make_async_copy(source, target, store.at[len(stores)])
        copy.start()
        stores.append(copy)

    keep(normed, normed_out)
    keep(gains, gains_out)
    g_qkv.finish()
    keep(wqkv, qkv_out)
    for b in range(tokens // QROWS):
        rows = pl.ds(b * QROWS, QROWS)
        product = dot(normed[rows], wqkv[...])
        table_c, table_s = cosine[rows], sine[rows]
        for block in range(query_width // 128):
            z = product[:, block * 128 : (block + 1) * 128]
            z = (z * table_c + turned(z) * table_s) * HD**-0.5
            for h in range(2):
                qh[2 * block + h, rows] = z[:, h * HD : (h + 1) * HD].astype(BF16)
        z = product[:, query_width : query_width + key_width]
        if key_width % 128 == 0:
            wide = key_width // 128
            table_c = jnp.concatenate([table_c] * wide, -1)
            table_s = jnp.concatenate([table_s] * wide, -1)
        else:
            table_c, table_s = table_c[:, :key_width], table_s[:, :key_width]
        z = z * table_c + turned(z) * table_s
        kv[rows, :key_width] = z.astype(BF16)
        kv[rows, key_width:] = product[:, query_width + key_width :].astype(BF16)
    pass_kv = remote(kv, kv_in, kv_send.at[0], kv_receive.at[0], place.core)

    @pl.when(place.c == 0)
    def _():
        pass_kv.start()
        for g in range(groups):
            kh[g, tokens:] = jnp.zeros((tokens, HD), BF16)
            vh[g, tokens:] = jnp.zeros((tokens, HD), BF16)

    own_rows = aligned(place.c, tokens)
    for g in range(groups):
        kh[g, own_rows] = kv[:, g * HD : (g + 1) * HD]
        vh[g, own_rows] = kv[:, key_width + g * HD : key_width + (g + 1) * HD]

    @pl.when(place.c == 1)
    def _():
        pass_kv.wait_recv()
        for g in range(groups):
            kh[g, :tokens] = kv_in[:, g * HD : (g + 1) * HD]
            vh[g, :tokens] = kv_in[:, key_width + g * HD : key_width + (g + 1) * HD]

    keep(qh, q_out)
    keep(kh, k_out)
    keep(vh, v_out)
    if place.bits:
        g_wo.pass_on(0)

    def attend(b):
        rows = aligned(b, QROWS)
        window = pl.ds(pl.multiple_of(place.c * b * QROWS, QROWS), bias.shape[1])

        def pair(j, carry):
            outs = []
            for h in range(2):
                head = 2 * j + h
                g = lax.div(head, heads // groups)
                weights = softmax_of(kh[g, window], qh[head, rows], bias[b]).astype(BF16)
                outs.append(dot(vh[g, window], weights, TN))
            mixed[rows, aligned(j, 128)] = jnp.concatenate(outs, 0).T.astype(BF16)
            return carry

        lax.fori_loop(0, heads // 2, pair, 0)

    def project(b):
        rows = aligned(b, QROWS)
        part[b] = dot(mixed[rows], wout[...]).astype(BF16)

    def root(i, rows, total):
        local = pl.ds(pl.multiple_of(place.late * QROWS + i * line.rows, line.rows), line.rows)
        total = total + x[local].astype(F32)
        hidden[rows] = total
        r = lax.rsqrt(jnp.sum(total * total, -1, keepdims=True) * (1.0 / width) + EPSILON)
        result[place.late, rows] = (total * r * gains[1:2, :].astype(F32)).astype(BF16)

    line = LineSum(place, part, inbox, result, line_sems, cfg.pieces, root)
    attend(place.early)
    for phase in range(1, place.bits):
        g_wo.pass_on(phase)
    g_wo.finish()
    keep(wout, wo_out)
    project(place.early)
    line.early_start()
    attend(place.late)
    project(place.late)
    keep(mixed, mixed_out)
    agenda = []
    for g in (g_wg, g_wu, g_wd):
        for phase in range(place.bits):
            agenda.append(functools.partial(g.pass_on, phase))
    marks = [line.rounds * (k + 1) // (len(agenda) + 1) for k in range(len(agenda))]
    at = 0
    for mark, item in zip(marks, agenda):
        line.run(at, mark)
        item()
        at = mark
    line.run(at, line.rounds)
    copy_back = pltpu.make_async_copy(result, normed_mlp_out, store.at[len(stores)])
    copy_back.start()
    stores.append(copy_back)
    keep(hidden, hidden_out)
    for g in (g_wg, g_wu, g_wd):
        g.finish()
    for g in gathers:
        g.drain()
    line.drain()

    @pl.when(place.c == 0)
    def _():
        pass_kv.wait_send()

    for copy in stores:
        copy.wait()


class Config:
    def __init__(self, dp, tensor, tokens, width, heads, groups, hidden_units):
        self.dp, self.tensor, self.tokens, self.width = dp, tensor, tokens, width
        self.heads, self.groups, self.hidden_units = heads, groups, hidden_units
        self.pieces = 8
        self.chunks = 4
        self.query_width, self.key_width = heads * HD, groups * HD
        self.qkv_width = self.query_width + 2 * self.key_width
        self.blocks = dp * 2
        self.block = width // self.blocks
        self.window = WINDOW + QROWS


def forward_call(cfg, x, lengths, freq, gains, wq, wk, wv, wo, wg, wu, wd):
    tokens, width, units = cfg.tokens, cfg.width, cfg.hidden_units
    any_spec = pl.BlockSpec(memory_space=pl.ANY)
    shape = jax.ShapeDtypeStruct
    outs = [
        shape((width, cfg.qkv_width), BF16),
        shape((cfg.query_width, width), BF16),
        shape((width, units), BF16),
        shape((width, units), BF16),
        shape((units, width), BF16),
        shape((16, width), BF16),
        shape((tokens, width), BF16),
        shape((cfg.heads, tokens, HD), BF16),
        shape((cfg.groups, 2 * tokens, HD), BF16),
        shape((cfg.groups, 2 * tokens, HD), BF16),
        shape((tokens, cfg.query_width), BF16),
        shape((QROWS, width), F32),
        shape((2, QROWS, width), BF16),
    ]
    shards = [wq, wk, wv, wo, wg, wu, wd]
    scratch = [pltpu.VMEM(x.shape, BF16)]
    scratch += [pltpu.VMEM(w.shape, F32) for w in shards]
    scratch += [pltpu.VMEM(gains.shape, F32)]
    scratch += [pltpu.VMEM((wq.shape[0], cfg.qkv_width), BF16)]
    scratch += [pltpu.VMEM(w.shape, BF16) for w in (wo, wg, wu, wd, gains)]
    scratch += [
        pltpu.VMEM((width, cfg.qkv_width), BF16),
        pltpu.VMEM((cfg.query_width, width), BF16),
        pltpu.VMEM((16, width), BF16),
        pltpu.VMEM((tokens, width), BF16),
        pltpu.VMEM((tokens, 1), F32),
        pltpu.VMEM((tokens, 128), F32),
        pltpu.VMEM((tokens, 128), F32),
        pltpu.VMEM((2, cfg.window, QROWS), F32),
        pltpu.VMEM((cfg.heads, tokens, HD), BF16),
        pltpu.VMEM((cfg.groups, 2 * tokens, HD), BF16),
        pltpu.VMEM((cfg.groups, 2 * tokens, HD), BF16),
        pltpu.VMEM((tokens, 2 * cfg.key_width), BF16),
        pltpu.VMEM((tokens, 2 * cfg.key_width), BF16),
        pltpu.VMEM((tokens, cfg.query_width), BF16),
        pltpu.VMEM((2, QROWS, width), BF16),
        pltpu.VMEM((2, QROWS, width), BF16),
        pltpu.VMEM((2, QROWS, width), BF16),
        pltpu.VMEM((QROWS, width), F32),
        pltpu.SemaphoreType.DMA((9,)),
        pltpu.SemaphoreType.DMA((12,)),
        pltpu.SemaphoreType.DMA((1,)),
        pltpu.SemaphoreType.DMA((1,)),
    ]
    for halves in (1, 2, 2, 2, 2, 2):
        scratch += Gather.semaphores(cfg.dp, halves)
    scratch += LineSum.semaphores(cfg.pieces)
    return pl.pallas_call(
        functools.partial(forward_kernel, cfg),
        out_shape=outs,
        in_specs=[
            any_spec,
            pl.BlockSpec(memory_space=pltpu.SMEM),
            pl.BlockSpec(memory_space=pltpu.VMEM),
        ]
        + [any_spec] * 8,
        out_specs=[any_spec] * len(outs),
        scratch_shapes=scratch,
        compiler_params=pltpu.CompilerParams(
            collective_id=1, has_side_effects=True, vmem_limit_bytes=VMEM_LIMIT
        ),
        name="attention_forward",
    )(x, lengths, freq, gains, wq, wk, wv, wo, wg, wu, wd)


def mlp_kernel(cfg, *refs):
    (
        n2_in, wg_in, wu_in, wd_in, dy_in, hidden_in, gains_in,
        terms_out, gate_out, up_out, down_out, db_out, dh_out, gain_out,
        n2, wg, wu, wd, dy, hidden, gains, n2_all, dy_all, act, dgate, dup,
        part, inbox, result, relay, gain_sum,
        load, store, own_sem, swap_send, swap_receive, chunk_send, chunk_receive, *sems,
    ) = refs
    place = Place(cfg.dp, cfg.tensor)
    tokens, width = n2.shape
    units = wg.shape[1]
    block, owners = cfg.block, cfg.dp
    chunk = units // cfg.chunks
    loads = []

    def fetch(source, target):
        copy = pltpu.make_async_copy(source, target, load.at[len(loads)])
        copy.start()
        loads.append(copy)
        return copy

    def weights(i):
        columns = aligned(i, chunk)
        return [
            pltpu.make_async_copy(wg_in.at[:, columns], wg.at[:, columns], load.at[5 + 3 * i]),
            pltpu.make_async_copy(wu_in.at[:, columns], wu.at[:, columns], load.at[6 + 3 * i]),
            pltpu.make_async_copy(wd_in.at[columns], wd.at[columns], load.at[7 + 3 * i]),
        ]

    fetch(n2_in.at[0], n2.at[pl.ds(0, QROWS)])
    fetch(n2_in.at[1], n2.at[pl.ds(QROWS, QROWS)])
    fetch(dy_in, dy)
    for i in range(cfg.chunks):
        for copy in weights(i):
            copy.start()
    fetch(gains_in, gains)
    fetch(hidden_in, hidden)
    place.greet()
    place.meet()
    swaps, owns = [], []
    for k, (source, target) in enumerate([(n2, n2_all), (dy, dy_all)]):
        loads[0 if k == 0 else 2].wait()
        if k == 0:
            loads[1].wait()
        for q in range(owners):
            columns = pl.ds(q * block, block)
            copy = remote(
                source.at[:, aligned(2 * q + 1 - place.c, block)],
                target.at[pl.ds(tokens, tokens), columns],
                swap_send.at[k, q],
                swap_receive.at[k, q],
                place.core,
            )
            copy.start()
            swaps.append(copy)
            copy = pltpu.make_async_copy(
                source.at[:, aligned(2 * q + place.c, block)],
                target.at[pl.ds(0, tokens), columns],
                own_sem.at[k, q],
            )
            copy.start()
            owns.append(copy)

    def exchange(i):
        columns = aligned(i, chunk)
        return [
            remote(
                array.at[pl.ds(0, tokens), columns],
                array.at[pl.ds(tokens, tokens), columns],
                chunk_send.at[k, i],
                chunk_receive.at[k, i],
                place.core,
            )
            for k, array in enumerate((act, dgate, dup))
        ]

    def hidden_units(i, carry):
        columns = aligned(i, chunk)
        for copy in weights(i):
            copy.wait()
        gate = dot(n2[...], wg[:, columns])
        upward = dot(n2[...], wu[:, columns])
        back = dot(dy[...], wd[columns], NT)
        sigmoid = 1.0 / (1.0 + jnp.exp(-gate))
        swish = gate * sigmoid
        act[:tokens, columns] = (swish * upward).astype(BF16)
        dgate[:tokens, columns] = (
            back * upward * sigmoid * (1.0 + gate * (1.0 - sigmoid))
        ).astype(BF16)
        dup[:tokens, columns] = (back * swish).astype(BF16)
        for copy in exchange(i):
            copy.start()
        return carry

    lax.fori_loop(0, cfg.chunks, hidden_units, 0)
    columns_at = width // 4

    def back_through(b):
        def one(i, carry):
            rows, columns = aligned(b, QROWS), aligned(i, columns_at)
            total = dot(dgate[rows], wg[columns], NT) + dot(dup[rows], wu[columns], NT)
            part[b, :, columns] = total.astype(BF16)
            return carry

        lax.fori_loop(0, 4, one, 0)

    def root(i, rows, total):
        local = pl.ds(pl.multiple_of(place.late * QROWS + i * line.rows, line.rows), line.rows)
        source = hidden[rows]
        r = lax.rsqrt(jnp.sum(source * source, -1, keepdims=True) * (1.0 / width) + EPSILON)
        scaled = source * r
        gain_sum[...] += jnp.sum((total * scaled).reshape(line.rows // 8, 8, width), 0)
        e = total * gains[1:2, :].astype(F32)
        mean = jnp.sum(e * scaled, -1, keepdims=True) * (1.0 / width)
        dh = dy[local].astype(F32) + r * (e - scaled * mean)
        hidden[rows] = dh
        result[place.late, rows] = dh.astype(BF16)

    line_count = 4
    line = LineSum(place, part, inbox, result, sems[:line_count], cfg.pieces, root)
    back_through(place.early)
    line.early_start()
    back_through(place.late)
    gain_sum[...] = jnp.zeros_like(gain_sum)
    for copy in loads[3:]:
        copy.wait()
    for copy in owns:
        copy.wait()
    for copy in swaps:
        copy.wait_recv()

    def arrived(i, carry):
        for copy in exchange(i):
            copy.wait_recv()
        return carry

    lax.fori_loop(0, cfg.chunks, arrived, 0)
    down = wd.at[:, pl.ds(0, owners * block)]
    gate_rows = wg.at[pl.ds(0, owners * block)]
    up_rows = wu.at[pl.ds(0, owners * block)]
    scatter = Scatter(place, down, relay, down_out, 1, sems[line_count:])
    stores = []

    def keep(source, target):
        copy = pltpu.make_async_copy(source, target, store.at[len(stores)])
        copy.start()
        stores.append(copy)

    def forward_terms(i):
        columns = aligned(i, columns_at)
        n2[:, columns] = dot(act[:tokens], wd[:, columns]).astype(BF16)

    def grad_down(i):
        rows = aligned(i, units // 4)
        down[rows] = dot(act[:, rows], dy_all[...], TN).astype(BF16)

    def grad_gate(i):
        columns = aligned(i, units // 4)
        gate_rows[:, columns] = dot(n2_all[...], dgate[:, columns], TN).astype(BF16)

    def grad_up(i):
        columns = aligned(i, units // 4)
        up_rows[:, columns] = dot(n2_all[...], dup[:, columns], TN).astype(BF16)

    for copy in swaps:
        copy.wait_send()

    def between(fill, first):
        def one(i, carry):
            line.round(first + i)
            fill(i)
            return carry

        lax.fori_loop(0, 4, one, 0)

    between(forward_terms, 0)
    keep(n2, terms_out)
    between(grad_down, 4)
    scatter.start()
    between(grad_gate, 8)
    keep(gate_rows, gate_out)
    between(grad_up, 12)
    keep(up_rows, up_out)
    line.run(16, line.rounds)
    keep(hidden, dh_out)
    keep(result, db_out)
    keep(gain_sum, gain_out)
    for phase in range(place.bits - 1, 0, -1):
        scatter.pass_on(phase)
    scatter.finish()
    line.drain()

    def gone(i, carry):
        for copy in exchange(i):
            copy.wait_send()
        return carry

    lax.fori_loop(0, cfg.chunks, gone, 0)
    for copy in stores:
        copy.wait()


def mlp_call(cfg, n2, wg, wu, wd, dy, hidden, gains):
    tokens, width, units = cfg.tokens, cfg.width, cfg.hidden_units
    any_spec = pl.BlockSpec(memory_space=pl.ANY)
    shape = jax.ShapeDtypeStruct
    bits = cfg.dp.bit_length() - 1
    mine = cfg.dp * cfg.block
    outs = [
        shape((tokens, width), BF16),
        shape((mine, units), BF16),
        shape((mine, units), BF16),
        shape((1 + bits, units, cfg.block), BF16),
        shape((2, QROWS, width), BF16),
        shape((QROWS, width), F32),
        shape((8, width), F32),
    ]
    scratch = [
        pltpu.VMEM((tokens, width), BF16),
        pltpu.VMEM((width, units), BF16),
        pltpu.VMEM((width, units), BF16),
        pltpu.VMEM((units, width), BF16),
        pltpu.VMEM((tokens, width), BF16),
        pltpu.VMEM((QROWS, width), F32),
        pltpu.VMEM((16, width), BF16),
        pltpu.VMEM((2 * tokens, mine), BF16),
        pltpu.VMEM((2 * tokens, mine), BF16),
        pltpu.VMEM((2 * tokens, units), BF16),
        pltpu.VMEM((2 * tokens, units), BF16),
        pltpu.VMEM((2 * tokens, units), BF16),
        pltpu.VMEM((2, QROWS, width), BF16),
        pltpu.VMEM((2, QROWS, width), BF16),
        pltpu.VMEM((2, QROWS, width), BF16),
        pltpu.VMEM(Scatter.inbox_shape(cfg.dp, units, cfg.block), BF16),
        pltpu.VMEM((8, width), F32),
        pltpu.SemaphoreType.DMA((5 + 3 * cfg.chunks,)),
        pltpu.SemaphoreType.DMA((6,)),
        pltpu.SemaphoreType.DMA((2, cfg.dp)),
        pltpu.SemaphoreType.DMA((2, cfg.dp)),
        pltpu.SemaphoreType.DMA((2, cfg.dp)),
        pltpu.SemaphoreType.DMA((3, cfg.chunks)),
        pltpu.SemaphoreType.DMA((3, cfg.chunks)),
    ]
    scratch += LineSum.semaphores(cfg.pieces)
    scratch += Scatter.semaphores(cfg.dp)
    return pl.pallas_call(
        functools.partial(mlp_kernel, cfg),
        out_shape=outs,
        in_specs=[any_spec] * 7,
        out_specs=[any_spec] * len(outs),
        scratch_shapes=scratch,
        compiler_params=pltpu.CompilerParams(
            collective_id=2, has_side_effects=True, vmem_limit_bytes=VMEM_LIMIT
        ),
        name="feed_forward",
    )(n2, wg, wu, wd, dy, hidden, gains)


def backward_kernel(cfg, *refs):
    (
        db_in, mixed_in, wo_in, qkv_in, q_in, k_in, v_in, normed_in, x_in, dh_in,
        terms_in, hidden_in, gate_in, up_in, gain_in, gains_in, lengths, freq,
        activations_out, grad_out, gate_out, up_out, qkv_out, out_out, gain_out,
        db, wo, wqkv, qh, kh, vh, normed_all, mixed_all, db_all, dqkv, x, dh,
        terms, inbox_two, final, hidden, part, inbox_one, result,
        gate_rows, up_rows, relay_gate, relay_up, relay_qkv, relay_out,
        qkv_rows, out_columns, dmixed, dk, dv, dkv, dkv_in, cosine, sine, bias,
        gains, gain_two, gain_one, gain_rows, gain_box, gain_line,
        load, store, own_sem, swap_send, swap_receive, dkv_send, dkv_receive,
        gain_send, gain_receive, last_send, last_receive, *sems,
    ) = refs
    place = Place(cfg.dp, cfg.tensor)
    tokens, width = x.shape
    heads, groups = cfg.heads, cfg.groups
    query_width, key_width = cfg.query_width, cfg.key_width
    block, owners = cfg.block, cfg.dp
    loads = []

    def fetch(source, target):
        copy = pltpu.make_async_copy(source, target, load.at[len(loads)])
        copy.start()
        loads.append(copy)
        return copy

    first = [
        fetch(db_in, db),
        fetch(wo_in, wo),
        fetch(q_in, qh),
        fetch(k_in, kh),
        fetch(v_in, vh),
        fetch(terms_in.at[pl.ds(0, QROWS)], terms.at[0]),
        fetch(terms_in.at[pl.ds(QROWS, QROWS)], terms.at[1]),
    ]
    wide = [fetch(gate_in, gate_rows), fetch(up_in, up_rows)]
    rest = [
        fetch(hidden_in, hidden),
        fetch(qkv_in, wqkv),
        fetch(mixed_in, mixed_all.at[pl.ds(0, tokens)]),
        fetch(x_in, x),
        fetch(dh_in, dh),
        fetch(gains_in, gains),
        fetch(gain_in, gain_two),
    ]
    barrier = pltpu.get_barrier_semaphore()
    greeted = [place.core]
    for mask in range(1, cfg.dp):
        greeted += [(place.flipped(mask), place.c, place.t), (place.flipped(mask), 1 - place.c, place.t)]
    for step in range(1, cfg.tensor):
        greeted.append((place.p, place.c, lax.rem(place.t + step, cfg.tensor)))
    for device in greeted:
        pl.semaphore_signal(barrier, inc=1, device_id=device, device_id_type=MESH)
    tables(place, lengths, freq, cosine, sine, tokens)
    fill_bias(place, lengths, bias, tokens)
    pl.semaphore_wait(barrier, len(greeted))

    for copy in first[:2]:
        copy.wait()
    swaps, owns = [], []

    def swap(source, target, k, q):
        copy = remote(source, target, swap_send.at[k, q], swap_receive.at[k, q], place.core)
        copy.start()
        swaps.append(copy)

    for q in range(owners):
        columns = pl.ds(q * block, block)
        other, own = aligned(2 * q + 1 - place.c, block), aligned(2 * q + place.c, block)
        swap(normed_in.at[:, other], normed_all.at[pl.ds(tokens, tokens), columns], 0, q)
        copy = pltpu.make_async_copy(
            normed_in.at[:, own], normed_all.at[pl.ds(0, tokens), columns], own_sem.at[0, q]
        )
        copy.start()
        owns.append(copy)
        for b in range(2):
            target = pl.ds(tokens + b * QROWS, QROWS)
            swap(db.at[b, :, other], db_all.at[target, columns], 1 + b, q)
            copy = pltpu.make_async_copy(
                db.at[b, :, own], db_all.at[pl.ds(b * QROWS, QROWS), columns], own_sem.at[1 + b, q]
            )
            copy.start()
            owns.append(copy)
    swap(mixed_in, mixed_all.at[pl.ds(tokens, tokens)], 3, 0)

    n_line, n_scatter = 4, 3
    scatters = []
    for i, (rows, relay, out, axis) in enumerate(
        [
            (out_columns, relay_out, out_out, 1),
            (gate_rows, relay_gate, gate_out, 0),
            (up_rows, relay_up, up_out, 0),
            (qkv_rows, relay_qkv, qkv_out, 0),
        ]
    ):
        at = 2 * n_line + n_scatter * i
        scatters.append(Scatter(place, rows, relay, out, axis, sems[at : at + n_scatter]))
    s_out, s_gate, s_up, s_qkv = scatters

    def local_rows(line, i):
        return pl.ds(pl.multiple_of(place.late * QROWS + i * line.rows, line.rows), line.rows)

    def root_two(i, rows, total):
        final[place.late, rows] = (hidden[rows] + total).astype(BF16)

    def root_one(i, rows, total):
        source = x[local_rows(line_one, i)].astype(F32)
        r = lax.rsqrt(jnp.sum(source * source, -1, keepdims=True) * (1.0 / width) + EPSILON)
        scaled = source * r
        gain_one[...] += jnp.sum((total * scaled).reshape(line_one.rows // 8, 8, width), 0)
        e = total * gains[0:1, :].astype(F32)
        mean = jnp.sum(e * scaled, -1, keepdims=True) * (1.0 / width)
        result[place.late, rows] = (dh[rows] + r * (e - scaled * mean)).astype(BF16)

    line_two = LineSum(place, terms, inbox_two, final, sems[:n_line], cfg.pieces, root_two)
    line_one = LineSum(
        place, part, inbox_one, result, sems[n_line : 2 * n_line], cfg.pieces, root_one
    )
    for copy in first[2:]:
        copy.wait()
    line_two.early_start()
    for copy in wide:
        copy.wait()
    s_gate.start()
    s_up.start()

    def back_out(b, carry):
        product = dot(db[b], wo[...], NT)
        rows = aligned(b, QROWS)
        for h in range(heads):
            dmixed[h, rows] = product[:, h * HD : (h + 1) * HD].astype(BF16)
        return carry

    lax.fori_loop(0, 2, back_out, 0)
    for copy in rest:
        copy.wait()
    dk[...] = jnp.zeros_like(dk)
    dv[...] = jnp.zeros_like(dv)

    def attend_back(b, rounds):
        rows = aligned(b, QROWS)
        window = pl.ds(pl.multiple_of(place.c * b * QROWS, QROWS), bias.shape[1])

        def pair(j, carry):
            outs = []
            for h in range(2):
                head = 2 * j + h
                g = lax.div(head, heads // groups)
                key, value = kh[g, window], vh[g, window]
                query, grad = qh[head, rows], dmixed[head, rows]
                weights = softmax_of(key, query, bias[b])
                dprobs = dot(value, grad, NT)
                delta = jnp.sum(weights * dprobs, 0, keepdims=True)
                dscores = (weights * (dprobs - delta)).astype(BF16)
                dv[g, window] += dot(weights.astype(BF16), grad)
                dk[g, window] += dot(dscores, query)
                outs.append(dot(key, dscores, TN))
            z = jnp.concatenate(outs, 0).T * HD**-0.5
            z = z * cosine[rows] - turned(z) * sine[rows]
            dqkv[rows, aligned(j, 128)] = z.astype(BF16)
            for k in range(2):
                line_two.round(rounds + 2 * j + k)
            return carry

        lax.fori_loop(0, heads // 2, pair, 0)

    attend_back(place.early, 0)
    attend_back(place.late, heads)
    line_two.run(min(2 * heads, line_two.rounds), line_two.rounds)
    stores = []

    def keep(source, target):
        copy = pltpu.make_async_copy(source, target, store.at[len(stores)])
        copy.start()
        stores.append(copy)

    keep(final, activations_out)
    pass_back = remote(dkv, dkv_in, dkv_send.at[0], dkv_receive.at[0], place.core)

    def packed(rows):
        return jnp.concatenate(
            [dk[g, rows] for g in range(groups)] + [dv[g, rows] for g in range(groups)], -1
        )

    @pl.when(place.c == 1)
    def _():
        dkv[...] = packed(pl.ds(0, tokens))
        pass_back.start()

    own_rows = aligned(place.c, tokens)
    z = packed(own_rows)

    @pl.when(place.c == 0)
    def _():
        pass_back.wait_recv()
        dkv[...] = z + dkv_in[...]

    @pl.when(place.c == 1)
    def _():
        pass_back.wait_send()
        dkv[...] = z

    dkeys = dkv[:, :key_width]
    if key_width % 128 == 0:
        wide_by = key_width // 128
        table_c = jnp.concatenate([cosine[...]] * wide_by, -1)
        table_s = jnp.concatenate([sine[...]] * wide_by, -1)
    else:
        table_c, table_s = cosine[:, :key_width], sine[:, :key_width]
    dkeys = dkeys * table_c - turned(dkeys) * table_s
    dqkv[:tokens, query_width : query_width + key_width] = dkeys.astype(BF16)
    dqkv[:tokens, query_width + key_width :] = dkv[:, key_width:].astype(BF16)
    swap(dqkv.at[pl.ds(0, tokens)], dqkv.at[pl.ds(tokens, tokens)], 3, 1)
    columns_at = width // 4

    def back_through(b):
        def one(i, carry):
            rows, columns = aligned(b, QROWS), aligned(i, columns_at)
            part[b, :, columns] = dot(dqkv[rows], wqkv[columns], NT).astype(BF16)
            return carry

        lax.fori_loop(0, 4, one, 0)

    gain_one[...] = jnp.zeros_like(gain_one)
    back_through(place.early)
    line_one.early_start()
    back_through(place.late)
    line_one.run(0, 1)
    for copy in owns:
        copy.wait()
    for copy in swaps:
        copy.wait_recv()
    qkv_rows[...] = dot(normed_all[...], dqkv[...], TN).astype(BF16)
    s_qkv.start()
    line_one.run(1, 3)
    out_columns[...] = dot(mixed_all[...], db_all[...], TN).astype(BF16)
    s_out.start()
    line_one.run(3, 4)
    agenda = []
    for phase in range(place.bits - 1, 0, -1):
        for s in (s_gate, s_up, s_qkv, s_out):
            agenda.append(functools.partial(s.pass_on, phase))
    last_sum = cfg.pieces + line_one.lags[1]
    marks = [4 + (last_sum - 4) * (k + 1) // (len(agenda) + 1) for k in range(len(agenda))]
    at = 4
    for mark, item in zip(marks, agenda):
        line_one.run(at, mark)
        item()
        at = mark
    line_one.run(at, last_sum)

    ends = (0, cfg.tensor - 1)
    mine = place.p * 2 + place.c

    def gain_copy(mask, core):
        index = place.flipped(mask) * 2 + core
        return remote(
            gain_rows.at[:, aligned(index, block)],
            gain_box.at[mine],
            gain_send.at[mask, lax.rem(core + place.c, 2)],
            gain_receive.at[mask, lax.rem(core + place.c, 2)],
            (place.flipped(mask), core, place.t),
        )

    others = [(mask, core) for mask in range(cfg.dp) for core in range(2)]

    @pl.when(place.at_end)
    def _():
        gain_rows[0:1, :] = jnp.sum(gain_one[...], 0, keepdims=True)
        gain_rows[1:2, :] = jnp.sum(gain_two[...], 0, keepdims=True)
        gain_rows[2:, :] = jnp.zeros((6, width), F32)
        for mask in range(cfg.dp):
            for apart in range(2):
                if mask or apart:
                    core = place.c if apart == 0 else 1 - place.c
                    gain_copy(mask, core).start()
        gain_box[mine] = gain_rows[:, aligned(mine, block)]

    line_one.run(last_sum, line_one.rounds - 2)

    def line_copy(step, end):
        return remote(
            gain_line.at[end],
            gain_line.at[end],
            last_send.at[step],
            last_receive.at[end],
            (place.p, place.c, lax.rem(place.t + step, cfg.tensor)),
        )

    for end, at_t in enumerate(ends):

        @pl.when(place.t == at_t)
        def _(end=end):
            for mask in range(cfg.dp):
                for apart in range(2):
                    if mask or apart:
                        core = place.c if apart == 0 else 1 - place.c
                        gain_copy(mask, core).wait_recv()
            gain_line[end] = jnp.sum(gain_box[...], 0)
            for step in range(1, cfg.tensor):
                line_copy(step, end).start()

    line_one.run(line_one.rounds - 2, line_one.rounds)
    keep(result, grad_out)
    for end, at_t in enumerate(ends):

        @pl.when(place.t != at_t)
        def _(end=end):
            line_copy(1, end).wait_recv()

    gain_one[:, :block] = gain_line[0] + gain_line[1]
    keep(gain_one.at[:, pl.ds(0, block)], gain_out)
    for s in scatters:
        s.finish()

    @pl.when(place.at_end)
    def _():
        for mask in range(cfg.dp):
            for apart in range(2):
                if mask or apart:
                    core = place.c if apart == 0 else 1 - place.c
                    gain_copy(mask, core).wait_send()
        for step in range(1, cfg.tensor):
            line_copy(step, 0).wait_send()

    for copy in swaps:
        copy.wait_send()
    line_two.drain()
    line_one.drain()
    for copy in stores:
        copy.wait()


def backward_call(cfg, *operands):
    tokens, width, units = cfg.tokens, cfg.width, cfg.hidden_units
    any_spec = pl.BlockSpec(memory_space=pl.ANY)
    shape = jax.ShapeDtypeStruct
    bits = cfg.dp.bit_length() - 1
    mine = cfg.dp * cfg.block
    heads, groups, qkv_width = cfg.heads, cfg.groups, cfg.qkv_width
    outs = [
        shape((2, QROWS, width), BF16),
        shape((2, QROWS, width), BF16),
        shape((1 + bits, cfg.block, units), BF16),
        shape((1 + bits, cfg.block, units), BF16),
        shape((1 + bits, cfg.block, qkv_width), BF16),
        shape((1 + bits, cfg.query_width, cfg.block), BF16),
        shape((8, cfg.block), F32),
    ]
    halves = (2, QROWS, width)
    scratch = [
        pltpu.VMEM(halves, BF16),
        pltpu.VMEM((cfg.query_width, width), BF16),
        pltpu.VMEM((width, qkv_width), BF16),
        pltpu.VMEM((heads, tokens, HD), BF16),
        pltpu.VMEM((groups, 2 * tokens, HD), BF16),
        pltpu.VMEM((groups, 2 * tokens, HD), BF16),
        pltpu.VMEM((2 * tokens, mine), BF16),
        pltpu.VMEM((2 * tokens, cfg.query_width), BF16),
        pltpu.VMEM((2 * tokens, mine), BF16),
        pltpu.VMEM((2 * tokens, qkv_width), BF16),
        pltpu.VMEM((tokens, width), BF16),
        pltpu.VMEM((QROWS, width), F32),
        pltpu.VMEM(halves, BF16),
        pltpu.VMEM(halves, BF16),
        pltpu.VMEM(halves, BF16),
        pltpu.VMEM((QROWS, width), F32),
        pltpu.VMEM(halves, BF16),
        pltpu.VMEM(halves, BF16),
        pltpu.VMEM(halves, BF16),
        pltpu.VMEM((mine, units), BF16),
        pltpu.VMEM((mine, units), BF16),
        pltpu.VMEM(Scatter.inbox_shape(cfg.dp, cfg.block, units), BF16),
        pltpu.VMEM(Scatter.inbox_shape(cfg.dp, cfg.block, units), BF16),
        pltpu.VMEM(Scatter.inbox_shape(cfg.dp, cfg.block, qkv_width), BF16),
        pltpu.VMEM(Scatter.inbox_shape(cfg.dp, cfg.query_width, cfg.block), BF16),
        pltpu.VMEM((mine, qkv_width), BF16),
        pltpu.VMEM((cfg.query_width, mine), BF16),
        pltpu.VMEM((heads, tokens, HD), BF16),
        pltpu.VMEM((groups, 2 * tokens, HD), F32),
        pltpu.VMEM((groups, 2 * tokens, HD), F32),
        pltpu.VMEM((tokens, 2 * cfg.key_width), F32),
        pltpu.VMEM((tokens, 2 * cfg.key_width), F32),
        pltpu.VMEM((tokens, 128), F32),
        pltpu.VMEM((tokens, 128), F32),
        pltpu.VMEM((2, cfg.window, QROWS), F32),
        pltpu.VMEM((16, width), BF16),
        pltpu.VMEM((8, width), F32),
        pltpu.VMEM((8, width), F32),
        pltpu.VMEM((8, width), F32),
        pltpu.VMEM((2 * cfg.dp, 8, cfg.block), F32),
        pltpu.VMEM((2, 8, cfg.block), F32),
        pltpu.SemaphoreType.DMA((16,)),
        pltpu.SemaphoreType.DMA((3,)),
        pltpu.SemaphoreType.DMA((3, cfg.dp)),
        pltpu.SemaphoreType.DMA((4, max(cfg.dp, 2))),
        pltpu.SemaphoreType.DMA((4, max(cfg.dp, 2))),
        pltpu.SemaphoreType.DMA((1,)),
        pltpu.SemaphoreType.DMA((1,)),
        pltpu.SemaphoreType.DMA((cfg.dp, 2)),
        pltpu.SemaphoreType.DMA((cfg.dp, 2)),
        pltpu.SemaphoreType.DMA((cfg.tensor,)),
        pltpu.SemaphoreType.DMA((2,)),
    ]
    scratch += LineSum.semaphores(cfg.pieces) * 2
    scratch += Scatter.semaphores(cfg.dp) * 4
    in_specs = [any_spec] * 16 + [
        pl.BlockSpec(memory_space=pltpu.SMEM),
        pl.BlockSpec(memory_space=pltpu.VMEM),
    ]
    return pl.pallas_call(
        functools.partial(backward_kernel, cfg),
        out_shape=outs,
        in_specs=in_specs,
        out_specs=[any_spec] * len(outs),
        scratch_shapes=scratch,
        compiler_params=pltpu.CompilerParams(
            collective_id=3, has_side_effects=True, vmem_limit_bytes=VMEM_LIMIT
        ),
        name="attention_backward",
    )(*operands)


def solution(mesh):
    dp, tensor = mesh.shape["dp"], mesh.shape["tensor"]

    def shards(
        inputs, cotangent, doc_lengths, gain_attn, w_query, w_key, w_value, w_out, gain_mlp,
        w_gate, w_up, w_down,
    ):
        tokens, width = inputs.shape
        cfg = Config(
            dp,
            tensor,
            tokens,
            width,
            w_query.shape[1] // HD,
            w_key.shape[1] // HD,
            w_gate.shape[1],
        )
        freq = jnp.tile(frequencies(), (8, 4))
        gains = jnp.zeros((16, gain_attn.shape[0]), F32).at[0].set(gain_attn).at[1].set(gain_mlp)
        (
            wqkv, wo, wg, wu, wd, gains_full, normed, q, k, v, mixed, hidden, normed_mlp,
        ) = forward_call(
            cfg, inputs, doc_lengths, freq, gains, w_query, w_key, w_value, w_out, w_gate, w_up, w_down
        )
        terms, gate_rows, up_rows, down_terms, db, dh, gain_two = mlp_call(
            cfg, normed_mlp, wg, wu, wd, cotangent, hidden, gains_full
        )
        activations, input_grad, gate_terms, up_terms, qkv_terms, out_terms, gain_sums = (
            backward_call(
                cfg, db, mixed, wo, wqkv, q, k, v, normed, inputs, dh, terms, hidden,
                gate_rows, up_rows, gain_two, gains_full, doc_lengths, freq,
            )
        )

        def total(pieces):
            return jnp.sum(pieces.astype(F32), 0)

        qkv_grad = total(qkv_terms)
        query_width, key_width = cfg.query_width, cfg.key_width
        return (
            activations.reshape(tokens, width),
            input_grad.reshape(tokens, width).astype(F32),
            gain_sums[0],
            qkv_grad[:, :query_width],
            qkv_grad[:, query_width : query_width + key_width],
            qkv_grad[:, query_width + key_width :],
            total(out_terms),
            gain_sums[1],
            total(gate_terms),
            total(up_terms),
            total(down_terms),
        )

    rows, columns, gain = P(("dp", "context"), "tensor"), P("tensor", ("dp", "context")), P(("dp", "context"))
    tokens = P(("dp", "context"), None)
    return jax.shard_map(
        shards,
        mesh=mesh,
        in_specs=(tokens, tokens, P("dp", None), gain, rows, rows, rows, columns, gain, rows, rows, columns),
        out_specs=(tokens, tokens, gain, rows, rows, rows, columns, gain, rows, rows, columns),
        check_vma=False,
    )
```

```python
import functools
import math

import jax
import jax.numpy as jnp
from jax import lax
from jax.experimental import pallas as pl
from jax.experimental.pallas import tpu as pltpu
from jax.sharding import PartitionSpec as P

HD = 64
WINDOW = 512
QROWS = 256
EPSILON = 1e-05
NEGATIVE = -1e30
MESH = pl.DeviceIdType.MESH
F32 = jnp.float32
BF16 = jnp.bfloat16
NN = (((1,), (0,)), ((), ()))
NT = (((1,), (1,)), ((), ()))
TN = (((0,), (0,)), ((), ()))
VMEM_LIMIT = 62 * 2**20


def dot(left, right, dims=NN):
    return lax.dot_general(left, right, dims, preferred_element_type=F32)


def frequencies():
    exponent = jnp.arange(0, HD, 2).astype(jnp.float32) / HD
    initial = 1.0 / 500000.0**exponent
    wavelength = 2.0 * math.pi / initial
    smoothing = (8192.0 / wavelength - 1.0) / 3.0
    blended = (1.0 - smoothing) * initial / 32.0 + smoothing * initial
    return jnp.where(
        wavelength < 2048.0, initial, jnp.where(wavelength > 8192.0, initial / 32.0, blended)
    )


def aligned(index, size):
    return pl.ds(pl.multiple_of(index * size, size), size)


class Place:
    def __init__(self, dp, tensor):
        self.dp, self.tensor = dp, tensor
        self.bits = dp.bit_length() - 1
        self.p = lax.axis_index("dp")
        self.c = lax.axis_index("context")
        self.t = lax.axis_index("tensor")
        self.core = (self.p, 1 - self.c, self.t)
        self.low = lax.rem(lax.div(self.t * 2, tensor), 2)
        self.early = 1 - self.low
        self.late = self.low
        step = 1 - 2 * self.low
        self.inward = (self.p, self.c, self.t + step)
        self.outward = (self.p, self.c, self.t - step)
        edge = self.low * (tensor - 1 - self.t) + (1 - self.low) * self.t
        self.depth = edge
        self.at_end = edge == 0

    def flipped(self, mask):
        position = self.p
        for b in range(self.bits):
            if mask >> b & 1:
                bit = lax.rem(lax.div(self.p, 2**b), 2)
                position = position + (1 - 2 * bit) * 2**b
        return position

    def across(self, b):
        return (self.flipped(1 << b), self.c, self.t)

    def greet(self):
        barrier = pltpu.get_barrier_semaphore()
        for device in [self.core] + [self.across(b) for b in range(self.bits)] + [self.inward]:
            pl.semaphore_signal(barrier, inc=1, device_id=device, device_id_type=MESH)

        @pl.when(jnp.logical_not(self.at_end))
        def _():
            pl.semaphore_signal(barrier, inc=1, device_id=self.outward, device_id_type=MESH)

    def meet(self):
        barrier = pltpu.get_barrier_semaphore()

        @pl.when(self.at_end)
        def _():
            pl.semaphore_wait(barrier, 2 + self.bits)

        @pl.when(jnp.logical_not(self.at_end))
        def _():
            pl.semaphore_wait(barrier, 3 + self.bits)


def remote(source, target, send, receive, device):
    return pltpu.make_async_remote_copy(
        src_ref=source,
        dst_ref=target,
        send_sem=send,
        recv_sem=receive,
        device_id=device,
        device_id_type=MESH,
    )


def orders_of(bits, halves):
    forward = tuple(range(bits))
    return (forward, forward[::-1]) if halves == 2 else (forward,)


def phase_masks(order, phase):
    masks = [0]
    for b in order[:phase]:
        masks = masks + [m | 1 << b for m in masks]
    return [m | 1 << order[phase] for m in masks]


class Gather:
    def __init__(self, place, shard, full, axis, sems, halves=2):
        self.place, self.shard, self.full, self.axis = place, shard, full, axis
        self.halves = halves
        self.send, self.receive, self.core_send, self.core_receive, self.local = sems
        self.orders = orders_of(place.bits, halves)
        self.rows = shard.shape[0] // halves
        self.sends = []

    @staticmethod
    def semaphores(dp, halves=2):
        bits = dp.bit_length() - 1
        return [
            pltpu.SemaphoreType.DMA((halves, dp, max(bits, 1))),
            pltpu.SemaphoreType.DMA((halves, dp)),
            pltpu.SemaphoreType.DMA((halves, dp)),
            pltpu.SemaphoreType.DMA((halves, dp)),
            pltpu.SemaphoreType.DMA((1,)),
        ]

    def part(self, half):
        return self.shard.at[pl.ds(half * self.rows, self.rows)]

    def slot(self, position, core, half):
        index = position * 2 + core
        if self.axis == 0:
            rows = self.shard.shape[0]
            first = pl.multiple_of(index * rows + half * self.rows, self.rows)
            return self.full.at[pl.ds(first, self.rows)]
        return self.full.at[
            pl.ds(half * self.rows, self.rows), aligned(index, self.shard.shape[1])
        ]

    def _forward(self, half, mask, source):
        place = self.place
        order = self.orders[half]
        last = max([order.index(b) for b in order if mask >> b & 1], default=-1)
        target = self.slot(place.flipped(mask), place.c, half)
        for j in range(last + 1, place.bits):
            copy = remote(
                source,
                target,
                self.send.at[half, mask, j],
                self.receive.at[half, mask | 1 << order[j]],
                place.across(order[j]),
            )
            copy.start()
            self.sends.append(copy)
        copy = remote(
            source,
            target,
            self.core_send.at[half, mask],
            self.core_receive.at[half, mask],
            place.core,
        )
        copy.start()
        self.sends.append(copy)

    def start(self):
        place = self.place
        for half in range(self.halves):
            self._forward(half, 0, self.part(half))
        index = place.p * 2 + place.c
        if self.axis == 0:
            own = self.full.at[aligned(index, self.shard.shape[0])]
        else:
            own = self.full.at[:, aligned(index, self.shard.shape[1])]
        self.own = pltpu.make_async_copy(self.shard, own, self.local.at[0])
        self.own.start()

    def pass_on(self, phase):
        place = self.place
        for half in range(self.halves):
            for mask in phase_masks(self.orders[half], phase):
                source = self.slot(place.flipped(mask), place.c, half)
                remote(
                    source,
                    source,
                    self.send.at[half, mask, 0],
                    self.receive.at[half, mask],
                    place.core,
                ).wait_recv()
                self._forward(half, mask, source)

    def finish(self):
        place = self.place
        self.own.wait()
        for half in range(self.halves):
            for mask in range(place.dp):
                target = self.slot(place.flipped(mask), 1 - place.c, half)
                remote(
                    target,
                    target,
                    self.core_send.at[half, mask],
                    self.core_receive.at[half, mask],
                    place.core,
                ).wait_recv()

    def drain(self):
        for copy in self.sends:
            copy.wait_send()
        self.sends = []


class LineSum:
    lags = (0, 3, 5, 7)

    def __init__(self, place, part, inbox, result, sems, pieces, root):
        self.place, self.part, self.inbox, self.result = place, part, inbox, result
        self.sum_send, self.sum_receive, self.back_send, self.back_receive = sems
        self.pieces = pieces
        self.rows = part.shape[1] // pieces
        self.rounds = pieces + self.lags[-1]
        self.root = root

    @staticmethod
    def semaphores(pieces):
        return [pltpu.SemaphoreType.DMA((2, pieces))] * 4

    def _copy(self, kind, flow, i, device):
        rows = aligned(i, self.rows)
        if kind == "sum":
            return remote(
                self.part.at[flow, rows],
                self.inbox.at[flow, rows],
                self.sum_send.at[flow, i],
                self.sum_receive.at[flow, i],
                device,
            )
        return remote(
            self.result.at[flow, rows],
            self.result.at[flow, rows],
            self.back_send.at[flow, i],
            self.back_receive.at[flow, i],
            device,
        )

    def _add(self, flow, i):
        rows = aligned(i, self.rows)
        total = self.part[flow, rows].astype(F32) + self.inbox[flow, rows].astype(F32)
        self.part[flow, rows] = total.astype(BF16)

    def early_start(self):
        @pl.when(self.place.at_end)
        def _():
            def one(i, carry):
                self._copy("sum", self.place.early, i, self.place.inward).start()
                return carry

            lax.fori_loop(0, self.pieces, one, 0)

    def early_sum(self, i):
        place = self.place

        @pl.when(jnp.logical_not(place.at_end))
        def _():
            copy = self._copy("sum", place.early, i, place.inward)
            copy.wait_recv()
            self._add(place.early, i)
            copy.start()

    def late_sum(self, i):
        place = self.place
        copy = self._copy("sum", place.late, i, place.outward)
        copy.wait_recv()

        @pl.when(jnp.logical_not(place.at_end))
        def _():
            self._add(place.late, i)
            copy.start()

        @pl.when(place.at_end)
        def _():
            rows = aligned(i, self.rows)
            total = self.part[place.late, rows].astype(F32)
            total = total + self.inbox[place.late, rows].astype(F32)
            self.root(i, rows, total)
            self._copy("back", place.late, i, place.inward).start()

    def late_back(self, i):
        place = self.place

        @pl.when(jnp.logical_not(place.at_end))
        def _():
            copy = self._copy("back", place.late, i, place.inward)
            copy.wait_recv()
            copy.start()

    def early_back(self, i):
        place = self.place
        copy = self._copy("back", place.early, i, place.outward)
        copy.wait_recv()

        @pl.when(jnp.logical_not(place.at_end))
        def _():
            copy.start()

    def round(self, n):
        for lag, kind in zip(self.lags, ("early_sum", "late_sum", "late_back", "early_back")):
            i = n - lag
            if isinstance(i, int):
                if 0 <= i < self.pieces:
                    getattr(self, kind)(i)
            else:

                @pl.when((i >= 0) & (i < self.pieces))
                def _(kind=kind, i=i):
                    getattr(self, kind)(i)

    def run(self, first, last):
        def one(n, carry):
            self.round(n)
            return carry

        lax.fori_loop(first, last, one, 0)

    def drain(self):
        place = self.place

        def one(i, carry):
            self._copy("sum", place.early, i, place.inward).wait_send()
            self._copy("back", place.late, i, place.inward).wait_send()

            @pl.when(jnp.logical_not(place.at_end))
            def _():
                self._copy("sum", place.late, i, place.outward).wait_send()
                self._copy("back", place.early, i, place.outward).wait_send()

            return carry

        lax.fori_loop(0, self.pieces, one, 0)


class Scatter:
    def __init__(self, place, part, inbox, out, axis, sems):
        self.place, self.part, self.inbox, self.out, self.axis = place, part, inbox, out, axis
        self.send, self.receive, self.local = sems
        self.orders = orders_of(place.bits, 2)
        self.rows = out.shape[1] // 2
        self.sends = []

    @staticmethod
    def semaphores(dp):
        return [
            pltpu.SemaphoreType.DMA((2, dp)),
            pltpu.SemaphoreType.DMA((2, dp)),
            pltpu.SemaphoreType.DMA((1,)),
        ]

    @staticmethod
    def inbox_shape(dp, rows, columns):
        slots = sum(2**phase - 1 for phase in range(1, dp.bit_length() - 1))
        return (2, max(slots, 1), rows // 2, columns)

    def slot(self, position, half):
        if self.axis == 0:
            rows = self.out.shape[1]
            first = pl.multiple_of(position * rows + half * self.rows, self.rows)
            return self.part.at[pl.ds(first, self.rows)]
        return self.part.at[
            pl.ds(half * self.rows, self.rows), aligned(position, self.out.shape[2])
        ]

    def landing(self, half, phase, mask):
        if mask == 0:
            return self.out.at[1 + phase, pl.ds(half * self.rows, self.rows)]
        return self.inbox.at[half, self.code(half, phase, mask)]

    def code(self, half, phase, mask):
        order = self.orders[half]
        number = 0
        for later in range(self.place.bits - 1, phase, -1):
            number += 2**later - 1
        inside = [m for m in range(1, self.place.dp) if all(b in order[:phase] for b in bits_of(m))]
        return number + inside.index(mask)

    def _copies(self, half, phase):
        order = self.orders[half]
        b = order[phase]
        for mask in phase_masks(order, phase):
            yield remote(
                self.slot(self.place.flipped(mask), half),
                self.landing(half, phase, mask & ~(1 << b)),
                self.send.at[half, mask],
                self.receive.at[half, mask],
                self.place.across(b),
            )

    def start(self):
        place = self.place
        index = place.p
        if self.axis == 0:
            own = self.part.at[aligned(index, self.out.shape[1])]
        else:
            own = self.part.at[:, aligned(index, self.out.shape[2])]
        self.own = pltpu.make_async_copy(own, self.out.at[0], self.local.at[0])
        self.own.start()
        if place.bits:
            self._send(place.bits - 1)

    def _send(self, phase):
        for half in range(2):
            for copy in self._copies(half, phase):
                copy.start()
                self.sends.append(copy)

    def pass_on(self, phase):
        for half in range(2):
            order = self.orders[half]
            for copy, mask in zip(self._copies(half, phase), phase_masks(order, phase)):
                rest = mask & ~(1 << order[phase])
                if rest:
                    copy.wait_recv()
                    target = self.slot(self.place.flipped(rest), half)
                    source = self.landing(half, phase, rest)
                    pieces = max(1, self.rows // 64)
                    size = self.rows // pieces

                    def add(i, carry, target=target, source=source, size=size):
                        rows = aligned(i, size)
                        total = target[rows].astype(F32) + source[rows].astype(F32)
                        target[rows] = total.astype(BF16)
                        return carry

                    lax.fori_loop(0, pieces, add, 0)
        self._send(phase - 1)

    def finish(self):
        self.own.wait()
        for phase in range(self.place.bits):
            for half in range(2):
                order = self.orders[half]
                for copy, mask in zip(self._copies(half, phase), phase_masks(order, phase)):
                    if not mask & ~(1 << order[phase]):
                        copy.wait_recv()
        for copy in self.sends:
            copy.wait_send()
        self.sends = []


def bits_of(mask):
    return [b for b in range(mask.bit_length()) if mask >> b & 1]


def turned(z):
    width = z.shape[-1]
    half = HD // 2
    if width == 2 * HD:
        lane = lax.broadcasted_iota(jnp.int32, z.shape, 1)
        return jnp.where(lax.rem(lane, HD) < half, pltpu.roll(z, width - half, 1), pltpu.roll(z, half, 1))
    pieces = []
    for h in range(width // HD):
        pieces += [z[:, h * HD + half : (h + 1) * HD], z[:, h * HD : h * HD + half]]
    return jnp.concatenate(pieces, -1)


def document_starts(lengths, rows):
    starts = jnp.zeros(rows.shape, jnp.int32)
    end = lengths[0, 0]
    for k in range(lengths.shape[1]):
        starts = jnp.where(rows >= end, end, starts)
        if k + 1 < lengths.shape[1]:
            end = end + lengths[0, k + 1]
    return starts


def tables(place, lengths, freq, cosine, sine, tokens):
    rows = lax.broadcasted_iota(jnp.int32, (tokens, 128), 0) + place.c * tokens
    angle = (rows - document_starts(lengths, rows)).astype(F32) * freq[0:1, :]
    lane = lax.broadcasted_iota(jnp.int32, (tokens, 128), 1)
    cosine[...] = jnp.cos(angle)
    turned_sine = jnp.sin(angle)
    sine[...] = jnp.where(lax.rem(lane, HD) < HD // 2, -turned_sine, turned_sine)


def fill_bias(place, lengths, bias, tokens):
    keys = bias.shape[1]
    for b in range(tokens // QROWS):
        shape = (keys, QROWS)
        query = lax.broadcasted_iota(jnp.int32, shape, 1) + (place.c * tokens + b * QROWS)
        key = lax.broadcasted_iota(jnp.int32, shape, 0) + place.c * b * QROWS
        row = lax.broadcasted_iota(jnp.int32, (8, QROWS), 1) + (place.c * tokens + b * QROWS)
        starts = document_starts(lengths, row)[0:1, :]
        bias[b] = jnp.where((key >= starts) & (key <= query), 0.0, NEGATIVE)


def softmax_of(key, query, bias):
    scores = dot(key, query, NT) + bias
    highest = jnp.max(scores, 0, keepdims=True)
    raw = jnp.exp(scores - highest)
    return raw * (1.0 / jnp.sum(raw, 0, keepdims=True))


def forward_kernel(cfg, *refs):
    (
        x_in, dy_in, lengths, freq, gains_in, wq_in, wk_in, wv_in, wo_in, wg_in, wu_in, wd_in,
        gu_full, wd_full,
        qkv_out, wo_out, gains_out, normed_out, q_out, k_out, v_out, mixed_out, hidden_out,
        n2_all, dy_all, act_all, dgu_all, dn2_out, terms_out,
        x, wq, wk, wv, wo, wraw, wd, gains32,
        sqkv, swo, sgu, swd, sgains,
        wqkv, wout, gains, normed, rscale, cosine, sine, bias,
        qh, kh, vh, kv, kv_in, mixed, part, inbox, result, hidden,
        gu_buffer, wd_buffer, act, dgu, dn2_sum, terms_sum,
        load, store, kv_send, kv_receive, fill, spill, swap_send, swap_receive,
        chunk_send, chunk_receive, *sems,
    ) = refs
    place = Place(cfg.dp, cfg.tensor)
    tokens, width = x.shape
    heads, groups = cfg.heads, cfg.groups
    query_width, key_width = cfg.query_width, cfg.key_width
    units, chunks = cfg.hidden_units, cfg.chunks
    chunk = units // chunks
    block, owners = cfg.block, cfg.dp
    loads = []

    def fetch(source, target):
        copy = pltpu.make_async_copy(source, target, load.at[len(loads)])
        copy.start()
        loads.append(copy)
        return copy

    small = [
        fetch(source, target)
        for source, target in ((gains_in, gains32), (wq_in, wq), (wk_in, wk), (wv_in, wv))
    ]
    load_x, load_wo = fetch(x_in, x), fetch(wo_in, wo)
    load_wg, load_wd = fetch(wg_in, wraw), fetch(wd_in, wd)
    place.greet()
    n_sems = 5
    gathers = []

    def gather(shard, full, axis, halves=2):
        at = n_sems * len(gathers)
        gathers.append(Gather(place, shard, full, axis, sems[at : at + n_sems], halves))
        return gathers[-1]

    g_gains = gather(sgains, gains, 1, 1)
    g_qkv = gather(sqkv, wqkv, 0)
    g_wo = gather(swo, wout, 1)
    g_gu, g_wd = [], []
    for i in range(chunks):
        columns = pl.ds(i * 2 * chunk, 2 * chunk)
        g_gu.append(gather(sgu.at[:, columns], gu_full.at[:, columns], 0))
        rows = pl.ds(i * chunk, chunk)
        g_wd.append(gather(swd.at[rows], wd_full.at[rows], 1))
    line_sems = sems[n_sems * len(gathers) :]
    for copy in small:
        copy.wait()
    sgains[...] = gains32[...].astype(BF16)
    sqkv[:, :query_width] = wq[...].astype(BF16)
    sqkv[:, query_width : query_width + key_width] = wk[...].astype(BF16)
    sqkv[:, query_width + key_width :] = wv[...].astype(BF16)
    place.meet()
    g_gains.start()
    g_qkv.start()
    load_wo.wait()
    swo[...] = wo[...].astype(BF16)

    def stage(second):
        for i in range(chunks):
            first = (2 * i + second) * chunk
            sgu[:, first : first + chunk] = wraw[:, i * chunk : (i + 1) * chunk].astype(BF16)

    load_wg.wait()
    stage(0)
    load_wu = fetch(wu_in, wraw)
    for phase in range(place.bits):
        g_gains.pass_on(phase)
        g_qkv.pass_on(phase)
        if phase == 0:
            g_wo.start()
            load_x.wait()
            rows_at = 64

            def scale(i, carry):
                rows = aligned(i, rows_at)
                wide = x[rows].astype(F32)
                mean = jnp.sum(wide * wide, -1, keepdims=True) * (1.0 / width)
                rscale[rows] = lax.rsqrt(mean + EPSILON)
                return carry

            lax.fori_loop(0, tokens // rows_at, scale, 0)
            tables(place, lengths, freq, cosine, sine, tokens)
            fill_bias(place, lengths, bias, tokens)
            load_wu.wait()
            stage(1)
            load_wd.wait()
            for i in range(chunks):
                rows = pl.ds(i * chunk, chunk)
                swd[rows] = wd[rows].astype(BF16)
    g_gains.finish()

    def norm(i, carry):
        rows = aligned(i, 64)
        scaled = x[rows].astype(F32) * rscale[rows]
        normed[rows] = (scaled * gains[0:1, :].astype(F32)).astype(BF16)
        return carry

    lax.fori_loop(0, tokens // 64, norm, 0)
    stores = []

    def keep(source, target):
        copy = pltpu.make_async_copy(source, target, store.at[len(stores)])
        copy.start()
        stores.append(copy)
        return copy

    normed_kept = keep(normed, normed_out)
    keep(gains, gains_out)
    g_qkv.finish()
    keep(wqkv, qkv_out)

    def begin(i):
        g_gu[i].start()
        g_wd[i].start()

    def advance(i, phase):
        g_gu[i].pass_on(phase)
        g_wd[i].pass_on(phase)

    for b in range(tokens // QROWS):
        rows = pl.ds(b * QROWS, QROWS)
        product = dot(normed[rows], wqkv[...])
        if b == 0:
            if place.bits:
                g_wo.pass_on(0)
            begin(0)
            begin(1)
        table_c, table_s = cosine[rows], sine[rows]
        for column in range(query_width // 128):
            z = product[:, column * 128 : (column + 1) * 128]
            z = (z * table_c + turned(z) * table_s) * HD**-0.5
            for h in range(2):
                qh[2 * column + h, rows] = z[:, h * HD : (h + 1) * HD].astype(BF16)
        z = product[:, query_width : query_width + key_width]
        if key_width % 128 == 0:
            wide = key_width // 128
            table_c = jnp.concatenate([table_c] * wide, -1)
            table_s = jnp.concatenate([table_s] * wide, -1)
        else:
            table_c, table_s = table_c[:, :key_width], table_s[:, :key_width]
        z = z * table_c + turned(z) * table_s
        kv[rows, :key_width] = z.astype(BF16)
        kv[rows, key_width:] = product[:, query_width + key_width :].astype(BF16)
    pass_kv = remote(kv, kv_in, kv_send.at[0], kv_receive.at[0], place.core)

    @pl.when(place.c == 0)
    def _():
        pass_kv.start()
        for g in range(groups):
            kh[g, tokens:] = jnp.zeros((tokens, HD), BF16)
            vh[g, tokens:] = jnp.zeros((tokens, HD), BF16)

    own_rows = aligned(place.c, tokens)
    for g in range(groups):
        kh[g, own_rows] = kv[:, g * HD : (g + 1) * HD]
        vh[g, own_rows] = kv[:, key_width + g * HD : key_width + (g + 1) * HD]

    @pl.when(place.c == 1)
    def _():
        pass_kv.wait_recv()
        for g in range(groups):
            kh[g, :tokens] = kv_in[:, g * HD : (g + 1) * HD]
            vh[g, :tokens] = kv_in[:, key_width + g * HD : key_width + (g + 1) * HD]

    keep(qh, q_out)
    keep(kh, k_out)
    keep(vh, v_out)
    normed_kept.wait()
    dy = normed
    load_dy = fetch(dy_in, dy)

    def attend(b):
        rows = aligned(b, QROWS)
        window = pl.ds(pl.multiple_of(place.c * b * QROWS, QROWS), bias.shape[1])

        def pair(j, carry):
            outs = []
            for h in range(2):
                head = 2 * j + h
                g = lax.div(head, heads // groups)
                weights = softmax_of(kh[g, window], qh[head, rows], bias[b]).astype(BF16)
                outs.append(dot(vh[g, window], weights, TN))
            mixed[rows, aligned(j, 128)] = jnp.concatenate(outs, 0).T.astype(BF16)
            return carry

        lax.fori_loop(0, heads // 2, pair, 0)

    def project(b):
        rows = aligned(b, QROWS)
        part[b] = dot(mixed[rows], wout[...]).astype(BF16)

    def root(i, rows, total):
        local = pl.ds(pl.multiple_of(place.late * QROWS + i * line.rows, line.rows), line.rows)
        total = total + x[local].astype(F32)
        hidden[rows] = total
        r = lax.rsqrt(jnp.sum(total * total, -1, keepdims=True) * (1.0 / width) + EPSILON)
        result[place.late, rows] = (total * r * gains[1:2, :].astype(F32)).astype(BF16)

    line = LineSum(place, part, inbox, result, line_sems, cfg.pieces, root)
    attend(place.early)
    for phase in range(1, place.bits):
        g_wo.pass_on(phase)
    g_wo.finish()
    keep(wout, wo_out)
    project(place.early)
    line.early_start()
    attend(place.late)
    project(place.late)
    keep(mixed, mixed_out)

    swaps, owns = [], []

    def swap(source, target, k, q, target_rows, sub):
        columns = pl.ds(q * block, block)
        copy = remote(
            source.at[:, aligned(2 * q + 1 - place.c, block)],
            target.at[pl.ds(tokens + sub, target_rows), columns],
            swap_send.at[k, q],
            swap_receive.at[k, q],
            place.core,
        )
        copy.start()
        swaps.append(copy)
        copy = pltpu.make_async_copy(
            source.at[:, aligned(2 * q + place.c, block)],
            target.at[pl.ds(sub, target_rows), columns],
            fill.at[k, q],
        )
        copy.start()
        owns.append(copy)

    load_dy.wait()
    for q in range(owners):
        swap(dy, dy_all, 0, q, tokens, 0)

    agenda = [(2, advance, 0, 0), (2, begin, 2), (9, advance, 1, 0), (9, begin, 3)]
    if not place.bits:
        agenda = [item for item in agenda if item[1] is begin]
    at = 0
    for mark, action, *rest in agenda:
        line.run(at, mark)
        action(*rest)
        at = mark
    line.run(at, line.rounds)
    for i in range(2):
        for phase in range(1, place.bits):
            advance(i, phase)
    if place.bits:
        advance(2, 0)
    for b in range(2):
        for q in range(owners):
            swap(result.at[b], n2_all, 1 + b, q, QROWS, b * QROWS)
    keep(hidden, hidden_out)

    def chunk_load(i):
        slot = i % 2
        return [
            pltpu.make_async_copy(
                gu_full.at[:, pl.ds(i * 2 * chunk, 2 * chunk)], gu_buffer.at[slot], spill.at[slot, 0]
            ),
            pltpu.make_async_copy(
                wd_full.at[pl.ds(i * chunk, chunk)], wd_buffer.at[slot], spill.at[slot, 1]
            ),
        ]

    def take(i):
        g_gu[i].finish()
        g_wd[i].finish()
        for copy in chunk_load(i):
            copy.start()

    def give(i):
        slot = i % 2
        act_columns, dgu_columns = pl.ds(i * chunk, chunk), pl.ds(i * 2 * chunk, 2 * chunk)
        copies = []
        for k, (source, target, columns) in enumerate(
            ((act, act_all, act_columns), (dgu, dgu_all, dgu_columns))
        ):
            copies.append(
                pltpu.make_async_copy(
                    source.at[slot], target.at[pl.ds(0, tokens), columns], spill.at[slot, 2 + k]
                )
            )
            copies.append(
                remote(
                    source.at[slot],
                    target.at[pl.ds(tokens, tokens), columns],
                    chunk_send.at[i, k],
                    chunk_receive.at[i, k],
                    place.core,
                )
            )
        return copies

    tile = width // 4
    n2 = result[...].reshape(tokens, width)
    take(0)
    for i in range(chunks):
        slot = i % 2
        for copy in chunk_load(i):
            copy.wait()
        if i + 1 < chunks:
            if i == 0:
                take(1)
        if i >= 2:
            own_act, sent_act, own_dgu, sent_dgu = give(i - 2)
            own_act.wait()
            own_dgu.wait()
            sent_act.wait_send()
            sent_dgu.wait_send()
        n2 = result[...].reshape(tokens, width)
        both = dot(n2, gu_buffer[slot])
        back = dot(dy[...], wd_buffer[slot], NT)
        gate, upward = both[:, :chunk], both[:, chunk:]
        sigmoid = 1.0 / (1.0 + jnp.exp(-gate))
        swish = gate * sigmoid
        act[slot] = (swish * upward).astype(BF16)
        dgu[slot, :, :chunk] = (
            back * upward * sigmoid * (1.0 + gate * (1.0 - sigmoid))
        ).astype(BF16)
        dgu[slot, :, chunk:] = (back * swish).astype(BF16)
        for copy in give(i):
            copy.start()

        def add(n, carry, i=i, slot=slot):
            columns = aligned(n, tile)
            more = dot(dgu[slot], gu_buffer[slot, columns], NT)
            terms = dot(act[slot], wd_buffer[slot, :, columns])
            if i:
                more = more + dn2_sum[:, columns]
                terms = terms + terms_sum[:, columns]
            if i + 1 < chunks:
                dn2_sum[:, columns] = more
                terms_sum[:, columns] = terms
            else:
                for b in range(2):
                    part[b, :, columns] = more[b * QROWS : (b + 1) * QROWS].astype(BF16)
                    inbox[b, :, columns] = terms[b * QROWS : (b + 1) * QROWS].astype(BF16)
            return carry

        if i + 1 == chunks:
            line.drain()
        lax.fori_loop(0, 4, add, 0)
        if 2 <= i + 1 < chunks:
            if i + 2 < chunks and place.bits:
                advance(i + 2, 0)
            for phase in range(1, place.bits):
                advance(i + 1, phase)
            take(i + 1)
    keep(part, dn2_out)
    keep(inbox, terms_out)
    for i in range(max(chunks - 2, 0), chunks):
        own_act, sent_act, own_dgu, sent_dgu = give(i)
        own_act.wait()
        own_dgu.wait()
        sent_act.wait_send()
        sent_dgu.wait_send()
    for i in range(chunks):
        own_act, sent_act, own_dgu, sent_dgu = give(i)
        sent_act.wait_recv()
        sent_dgu.wait_recv()
    for g in gathers:
        g.drain()
    for copy in owns:
        copy.wait()
    for copy in swaps:
        copy.wait_recv()
        copy.wait_send()

    @pl.when(place.c == 0)
    def _():
        pass_kv.wait_send()

    for copy in stores[1:]:
        copy.wait()


class Config:
    def __init__(self, dp, tensor, tokens, width, heads, groups, hidden_units):
        self.dp, self.tensor, self.tokens, self.width = dp, tensor, tokens, width
        self.heads, self.groups, self.hidden_units = heads, groups, hidden_units
        self.pieces = 8
        self.chunks = 4
        self.marks = (4, 4, 11)
        self.query_width, self.key_width = heads * HD, groups * HD
        self.qkv_width = self.query_width + 2 * self.key_width
        self.blocks = dp * 2
        self.block = width // self.blocks
        self.window = WINDOW + QROWS


def forward_call(cfg, x, dy, lengths, freq, gains, wq, wk, wv, wo, wg, wu, wd):
    tokens, width, units = cfg.tokens, cfg.width, cfg.hidden_units
    any_spec = pl.BlockSpec(memory_space=pl.ANY)
    shape = jax.ShapeDtypeStruct
    mine = cfg.dp * cfg.block
    chunk = units // cfg.chunks
    outs = [
        shape((width, 2 * units), BF16),
        shape((units, width), BF16),
        shape((width, cfg.qkv_width), BF16),
        shape((cfg.query_width, width), BF16),
        shape((16, width), BF16),
        shape((tokens, width), BF16),
        shape((cfg.heads, tokens, HD), BF16),
        shape((cfg.groups, 2 * tokens, HD), BF16),
        shape((cfg.groups, 2 * tokens, HD), BF16),
        shape((tokens, cfg.query_width), BF16),
        shape((QROWS, width), F32),
        shape((2 * tokens, mine), BF16),
        shape((2 * tokens, mine), BF16),
        shape((2 * tokens, units), BF16),
        shape((2 * tokens, 2 * units), BF16),
        shape((2, QROWS, width), BF16),
        shape((2, QROWS, width), BF16),
    ]
    scratch = [pltpu.VMEM(x.shape, BF16)]
    scratch += [pltpu.VMEM(w.shape, F32) for w in (wq, wk, wv, wo, wg, wd, gains)]
    scratch += [pltpu.VMEM((wq.shape[0], cfg.qkv_width), BF16)]
    scratch += [pltpu.VMEM(wo.shape, BF16)]
    scratch += [pltpu.VMEM((wg.shape[0], 2 * units), BF16)]
    scratch += [pltpu.VMEM(wd.shape, BF16)]
    scratch += [pltpu.VMEM(gains.shape, BF16)]
    scratch += [
        pltpu.VMEM((width, cfg.qkv_width), BF16),
        pltpu.VMEM((cfg.query_width, width), BF16),
        pltpu.VMEM((16, width), BF16),
        pltpu.VMEM((tokens, width), BF16),
        pltpu.VMEM((tokens, 1), F32),
        pltpu.VMEM((tokens, 128), F32),
        pltpu.VMEM((tokens, 128), F32),
        pltpu.VMEM((2, cfg.window, QROWS), F32),
        pltpu.VMEM((cfg.heads, tokens, HD), BF16),
        pltpu.VMEM((cfg.groups, 2 * tokens, HD), BF16),
        pltpu.VMEM((cfg.groups, 2 * tokens, HD), BF16),
        pltpu.VMEM((tokens, 2 * cfg.key_width), BF16),
        pltpu.VMEM((tokens, 2 * cfg.key_width), BF16),
        pltpu.VMEM((tokens, cfg.query_width), BF16),
        pltpu.VMEM((2, QROWS, width), BF16),
        pltpu.VMEM((2, QROWS, width), BF16),
        pltpu.VMEM((2, QROWS, width), BF16),
        pltpu.VMEM((QROWS, width), F32),
        pltpu.VMEM((2, width, 2 * chunk), BF16),
        pltpu.VMEM((2, chunk, width), BF16),
        pltpu.VMEM((2, tokens, chunk), BF16),
        pltpu.VMEM((2, tokens, 2 * chunk), BF16),
        pltpu.VMEM((tokens, width), F32),
        pltpu.VMEM((tokens, width), F32),
        pltpu.SemaphoreType.DMA((10,)),
        pltpu.SemaphoreType.DMA((14,)),
        pltpu.SemaphoreType.DMA((1,)),
        pltpu.SemaphoreType.DMA((1,)),
        pltpu.SemaphoreType.DMA((3, cfg.dp)),
        pltpu.SemaphoreType.DMA((2, 4)),
        pltpu.SemaphoreType.DMA((3, cfg.dp)),
        pltpu.SemaphoreType.DMA((3, cfg.dp)),
        pltpu.SemaphoreType.DMA((cfg.chunks, 2)),
        pltpu.SemaphoreType.DMA((cfg.chunks, 2)),
    ]
    for halves in [1] + [2] * (2 + 2 * cfg.chunks):
        scratch += Gather.semaphores(cfg.dp, halves)
    scratch += LineSum.semaphores(cfg.pieces)
    return pl.pallas_call(
        functools.partial(forward_kernel, cfg),
        out_shape=outs,
        in_specs=[
            any_spec,
            any_spec,
            pl.BlockSpec(memory_space=pltpu.SMEM),
            pl.BlockSpec(memory_space=pltpu.VMEM),
        ]
        + [any_spec] * 8,
        out_specs=[any_spec] * len(outs),
        scratch_shapes=scratch,
        compiler_params=pltpu.CompilerParams(
            collective_id=1, has_side_effects=True, vmem_limit_bytes=VMEM_LIMIT
        ),
        name="attention_forward",
    )(x, dy, lengths, freq, gains, wq, wk, wv, wo, wg, wu, wd)


def mlp_kernel(cfg, *refs):
    (
        dn2_in, n2_in, dy_all_in, act_in, dgu_in, dy_in, hidden_in, gains_in,
        gu_out, down_out, db_out, dh_out, gain_out,
        dy, hidden, gains, n2_all, dy_all, act, dgu, gu_rows, down,
        part, inbox, result, relay, gain_sum,
        load, store, *sems,
    ) = refs
    place = Place(cfg.dp, cfg.tensor)
    tokens, width = dy.shape
    units = act.shape[1]
    chunk = units // cfg.chunks
    loads = []

    def fetch(source, target):
        copy = pltpu.make_async_copy(source, target, load.at[len(loads)])
        copy.start()
        loads.append(copy)
        return copy

    load_part = fetch(dn2_in, part)
    first = [fetch(dy_in, dy), fetch(hidden_in, hidden), fetch(gains_in, gains)]
    second = [fetch(act_in, act), fetch(dy_all_in, dy_all)]
    third = [fetch(n2_in, n2_all), fetch(dgu_in, dgu)]
    place.greet()
    gain_sum[...] = jnp.zeros_like(gain_sum)
    place.meet()

    def root(i, rows, total):
        local = pl.ds(pl.multiple_of(place.late * QROWS + i * line.rows, line.rows), line.rows)
        source = hidden[rows]
        r = lax.rsqrt(jnp.sum(source * source, -1, keepdims=True) * (1.0 / width) + EPSILON)
        scaled = source * r
        gain_sum[...] += jnp.sum((total * scaled).reshape(line.rows // 8, 8, width), 0)
        e = total * gains[1:2, :].astype(F32)
        mean = jnp.sum(e * scaled, -1, keepdims=True) * (1.0 / width)
        dh = dy[local].astype(F32) + r * (e - scaled * mean)
        hidden[rows] = dh
        result[place.late, rows] = dh.astype(BF16)

    line_count = 4
    line = LineSum(place, part, inbox, result, sems[:line_count], cfg.pieces, root)
    scatter = Scatter(place, down, relay, down_out, 1, sems[line_count:])
    stores = []

    def keep(source, target):
        copy = pltpu.make_async_copy(source, target, store.at[len(stores)])
        copy.start()
        stores.append(copy)

    load_part.wait()
    line.early_start()

    def grad_down(i):
        rows = aligned(i, units // 4)
        down[rows] = dot(act[:, rows], dy_all[...], TN).astype(BF16)

    def grad_gate_up(i):
        target = aligned(lax.rem(i, 2) * cfg.chunks + lax.div(i, 2), chunk)
        gu_rows[:, target] = dot(n2_all[...], dgu[:, aligned(i, chunk)], TN).astype(BF16)

    def between(fill, rounds, fills):
        def one(i, carry):
            line.round(rounds + i)
            fill(fills + i)
            return carry

        lax.fori_loop(0, 4, one, 0)

    for copy in first + second:
        copy.wait()
    between(grad_down, 0, 0)
    scatter.start()
    for copy in third:
        copy.wait()
    between(grad_gate_up, 4, 0)
    between(grad_gate_up, 8, 4)
    keep(gu_rows, gu_out)
    for phase in range(place.bits - 1, 0, -1):
        scatter.pass_on(phase)
    line.run(12, line.rounds)
    keep(hidden, dh_out)
    keep(result, db_out)
    keep(gain_sum, gain_out)
    scatter.finish()
    line.drain()
    for copy in stores:
        copy.wait()


def mlp_call(cfg, *operands):
    tokens, width, units = cfg.tokens, cfg.width, cfg.hidden_units
    any_spec = pl.BlockSpec(memory_space=pl.ANY)
    shape = jax.ShapeDtypeStruct
    bits = cfg.dp.bit_length() - 1
    mine = cfg.dp * cfg.block
    outs = [
        shape((mine, 2 * units), BF16),
        shape((1 + bits, units, cfg.block), BF16),
        shape((2, QROWS, width), BF16),
        shape((QROWS, width), F32),
        shape((8, width), F32),
    ]
    scratch = [
        pltpu.VMEM((tokens, width), BF16),
        pltpu.VMEM((QROWS, width), F32),
        pltpu.VMEM((16, width), BF16),
        pltpu.VMEM((2 * tokens, mine), BF16),
        pltpu.VMEM((2 * tokens, mine), BF16),
        pltpu.VMEM((2 * tokens, units), BF16),
        pltpu.VMEM((2 * tokens, 2 * units), BF16),
        pltpu.VMEM((mine, 2 * units), BF16),
        pltpu.VMEM((units, mine), BF16),
        pltpu.VMEM((2, QROWS, width), BF16),
        pltpu.VMEM((2, QROWS, width), BF16),
        pltpu.VMEM((2, QROWS, width), BF16),
        pltpu.VMEM(Scatter.inbox_shape(cfg.dp, units, cfg.block), BF16),
        pltpu.VMEM((8, width), F32),
        pltpu.SemaphoreType.DMA((8,)),
        pltpu.SemaphoreType.DMA((4,)),
    ]
    scratch += LineSum.semaphores(cfg.pieces)
    scratch += Scatter.semaphores(cfg.dp)
    return pl.pallas_call(
        functools.partial(mlp_kernel, cfg),
        out_shape=outs,
        in_specs=[any_spec] * 8,
        out_specs=[any_spec] * len(outs),
        scratch_shapes=scratch,
        compiler_params=pltpu.CompilerParams(
            collective_id=2, has_side_effects=True, vmem_limit_bytes=VMEM_LIMIT
        ),
        name="feed_forward",
    )(*operands)


def backward_kernel(cfg, *refs):
    (
        db_in, mixed_in, wo_in, qkv_in, q_in, k_in, v_in, normed_in, x_in, dh_in,
        terms_in, hidden_in, gu_in, gain_in, gains_in, lengths, freq,
        activations_out, grad_out, gu_out, qkv_out, out_out, gain_out,
        db, wo, wqkv, qh, kh, vh, normed_all, mixed_all, db_all, dqkv, x, dh,
        terms, inbox_two, final, hidden, part, inbox_one, result,
        gu_rows, relay_gu, relay_qkv, relay_out,
        qkv_rows, out_columns, dmixed, dk, dv, dkv, dkv_in, cosine, sine, bias,
        gains, gain_two, gain_one, gain_rows, gain_box, gain_line,
        load, store, own_sem, swap_send, swap_receive, dkv_send, dkv_receive,
        gain_send, gain_receive, last_send, last_receive, *sems,
    ) = refs
    place = Place(cfg.dp, cfg.tensor)
    tokens, width = x.shape
    heads, groups = cfg.heads, cfg.groups
    query_width, key_width = cfg.query_width, cfg.key_width
    block, owners = cfg.block, cfg.dp
    loads = []

    def fetch(source, target):
        copy = pltpu.make_async_copy(source, target, load.at[len(loads)])
        copy.start()
        loads.append(copy)
        return copy

    first = [
        fetch(db_in, db),
        fetch(wo_in, wo),
        fetch(q_in, qh),
        fetch(k_in, kh),
        fetch(v_in, vh),
        fetch(terms_in, terms),
    ]
    wide = [fetch(gu_in, gu_rows)]
    rest = [
        fetch(hidden_in, hidden),
        fetch(qkv_in, wqkv),
        fetch(mixed_in, mixed_all.at[pl.ds(0, tokens)]),
        fetch(x_in, x),
        fetch(dh_in, dh),
        fetch(gains_in, gains),
        fetch(gain_in, gain_two),
    ]
    barrier = pltpu.get_barrier_semaphore()
    greeted = [place.core]
    for mask in range(1, cfg.dp):
        greeted += [(place.flipped(mask), place.c, place.t), (place.flipped(mask), 1 - place.c, place.t)]
    for step in range(1, cfg.tensor):
        greeted.append((place.p, place.c, lax.rem(place.t + step, cfg.tensor)))
    for device in greeted:
        pl.semaphore_signal(barrier, inc=1, device_id=device, device_id_type=MESH)
    tables(place, lengths, freq, cosine, sine, tokens)
    fill_bias(place, lengths, bias, tokens)
    pl.semaphore_wait(barrier, len(greeted))

    for copy in first[:2]:
        copy.wait()
    swaps, owns = [], []

    def swap(source, target, k, q):
        copy = remote(source, target, swap_send.at[k, q], swap_receive.at[k, q], place.core)
        copy.start()
        swaps.append(copy)

    for q in range(owners):
        columns = pl.ds(q * block, block)
        other, own = aligned(2 * q + 1 - place.c, block), aligned(2 * q + place.c, block)
        swap(normed_in.at[:, other], normed_all.at[pl.ds(tokens, tokens), columns], 0, q)
        copy = pltpu.make_async_copy(
            normed_in.at[:, own], normed_all.at[pl.ds(0, tokens), columns], own_sem.at[0, q]
        )
        copy.start()
        owns.append(copy)
        for b in range(2):
            target = pl.ds(tokens + b * QROWS, QROWS)
            swap(db.at[b, :, other], db_all.at[target, columns], 1 + b, q)
            copy = pltpu.make_async_copy(
                db.at[b, :, own], db_all.at[pl.ds(b * QROWS, QROWS), columns], own_sem.at[1 + b, q]
            )
            copy.start()
            owns.append(copy)
    swap(mixed_in, mixed_all.at[pl.ds(tokens, tokens)], 3, 0)

    n_line, n_scatter = 4, 3
    scatters = []
    for i, (rows, relay, out, axis) in enumerate(
        [
            (out_columns, relay_out, out_out, 1),
            (gu_rows, relay_gu, gu_out, 0),
            (qkv_rows, relay_qkv, qkv_out, 0),
        ]
    ):
        at = 2 * n_line + n_scatter * i
        scatters.append(Scatter(place, rows, relay, out, axis, sems[at : at + n_scatter]))
    s_out, s_gu, s_qkv = scatters

    def local_rows(line, i):
        return pl.ds(pl.multiple_of(place.late * QROWS + i * line.rows, line.rows), line.rows)

    def root_two(i, rows, total):
        final[place.late, rows] = (hidden[rows] + total).astype(BF16)

    def root_one(i, rows, total):
        source = x[local_rows(line_one, i)].astype(F32)
        r = lax.rsqrt(jnp.sum(source * source, -1, keepdims=True) * (1.0 / width) + EPSILON)
        scaled = source * r
        gain_one[...] += jnp.sum((total * scaled).reshape(line_one.rows // 8, 8, width), 0)
        e = total * gains[0:1, :].astype(F32)
        mean = jnp.sum(e * scaled, -1, keepdims=True) * (1.0 / width)
        result[place.late, rows] = (dh[rows] + r * (e - scaled * mean)).astype(BF16)

    line_two = LineSum(place, terms, inbox_two, final, sems[:n_line], cfg.pieces, root_two)
    line_one = LineSum(
        place, part, inbox_one, result, sems[n_line : 2 * n_line], cfg.pieces, root_one
    )
    for copy in first[2:]:
        copy.wait()
    line_two.early_start()
    for copy in wide:
        copy.wait()
    s_gu.start()

    def back_out(b, carry):
        product = dot(db[b], wo[...], NT)
        rows = aligned(b, QROWS)
        for h in range(heads):
            dmixed[h, rows] = product[:, h * HD : (h + 1) * HD].astype(BF16)
        return carry

    lax.fori_loop(0, 2, back_out, 0)
    for copy in rest:
        copy.wait()
    dk[...] = jnp.zeros_like(dk)
    dv[...] = jnp.zeros_like(dv)

    def attend_back(b, rounds):
        rows = aligned(b, QROWS)
        window = pl.ds(pl.multiple_of(place.c * b * QROWS, QROWS), bias.shape[1])

        def pair(j, carry):
            outs = []
            for h in range(2):
                head = 2 * j + h
                g = lax.div(head, heads // groups)
                key, value = kh[g, window], vh[g, window]
                query, grad = qh[head, rows], dmixed[head, rows]
                weights = softmax_of(key, query, bias[b])
                dprobs = dot(value, grad, NT)
                delta = jnp.sum(weights * dprobs, 0, keepdims=True)
                dscores = (weights * (dprobs - delta)).astype(BF16)
                dv[g, window] += dot(weights.astype(BF16), grad)
                dk[g, window] += dot(dscores, query)
                outs.append(dot(key, dscores, TN))
            z = jnp.concatenate(outs, 0).T * HD**-0.5
            z = z * cosine[rows] - turned(z) * sine[rows]
            dqkv[rows, aligned(j, 128)] = z.astype(BF16)
            line_two.round(rounds + j)
            return carry

        lax.fori_loop(0, heads // 2, pair, 0)

    attend_back(place.early, 0)
    attend_back(place.late, heads // 2)
    stores = []

    def keep(source, target):
        copy = pltpu.make_async_copy(source, target, store.at[len(stores)])
        copy.start()
        stores.append(copy)

    pass_back = remote(dkv, dkv_in, dkv_send.at[0], dkv_receive.at[0], place.core)

    def packed(rows):
        return jnp.concatenate(
            [dk[g, rows] for g in range(groups)] + [dv[g, rows] for g in range(groups)], -1
        )

    @pl.when(place.c == 1)
    def _():
        dkv[...] = packed(pl.ds(0, tokens))
        pass_back.start()

    own_rows = aligned(place.c, tokens)
    z = packed(own_rows)

    @pl.when(place.c == 0)
    def _():
        pass_back.wait_recv()
        dkv[...] = z + dkv_in[...]

    @pl.when(place.c == 1)
    def _():
        pass_back.wait_send()
        dkv[...] = z

    dkeys = dkv[:, :key_width]
    if key_width % 128 == 0:
        wide_by = key_width // 128
        table_c = jnp.concatenate([cosine[...]] * wide_by, -1)
        table_s = jnp.concatenate([sine[...]] * wide_by, -1)
    else:
        table_c, table_s = cosine[:, :key_width], sine[:, :key_width]
    dkeys = dkeys * table_c - turned(dkeys) * table_s
    dqkv[:tokens, query_width : query_width + key_width] = dkeys.astype(BF16)
    dqkv[:tokens, query_width + key_width :] = dkv[:, key_width:].astype(BF16)
    swap(dqkv.at[pl.ds(0, tokens)], dqkv.at[pl.ds(tokens, tokens)], 3, 1)
    columns_at = width // 4

    def back_through(b):
        def one(i, carry):
            rows, columns = aligned(b, QROWS), aligned(i, columns_at)
            part[b, :, columns] = dot(dqkv[rows], wqkv[columns], NT).astype(BF16)
            return carry

        lax.fori_loop(0, 4, one, 0)

    def run_lines(start, stop):
        def one(n, carry):
            line_two.round(heads + n)
            line_one.round(n)
            return carry

        lax.fori_loop(start, stop, one, 0)

    gain_one[...] = jnp.zeros_like(gain_one)
    back_through(place.early)
    line_one.early_start()
    back_through(place.late)
    run_lines(0, 1)
    for copy in owns:
        copy.wait()
    for copy in swaps:
        copy.wait_recv()
    qkv_rows[...] = dot(normed_all[...], dqkv[...], TN).astype(BF16)
    s_qkv.start()
    run_lines(1, 3)
    out_columns[...] = dot(mixed_all[...], db_all[...], TN).astype(BF16)
    s_out.start()
    run_lines(3, 4)
    agenda = []
    for phase in range(place.bits - 1, 0, -1):
        for s in (s_gu, s_qkv, s_out):
            agenda.append(functools.partial(s.pass_on, phase))
    last_sum = cfg.pieces + line_one.lags[1]
    marks = [4 + (last_sum - 4) * (k + 1) // (len(agenda) + 1) for k in range(len(agenda))]
    at = 4
    for mark, item in zip(marks, agenda):
        run_lines(at, mark)
        item()
        at = mark
    run_lines(at, last_sum)

    ends = (0, cfg.tensor - 1)
    mine = place.p * 2 + place.c

    def gain_copy(mask, core):
        index = place.flipped(mask) * 2 + core
        return remote(
            gain_rows.at[:, aligned(index, block)],
            gain_box.at[mine],
            gain_send.at[mask, lax.rem(core + place.c, 2)],
            gain_receive.at[mask, lax.rem(core + place.c, 2)],
            (place.flipped(mask), core, place.t),
        )

    others = [(mask, core) for mask in range(cfg.dp) for core in range(2)]

    @pl.when(place.at_end)
    def _():
        gain_rows[0:1, :] = jnp.sum(gain_one[...], 0, keepdims=True)
        gain_rows[1:2, :] = jnp.sum(gain_two[...], 0, keepdims=True)
        gain_rows[2:, :] = jnp.zeros((6, width), F32)
        for mask in range(cfg.dp):
            for apart in range(2):
                if mask or apart:
                    core = place.c if apart == 0 else 1 - place.c
                    gain_copy(mask, core).start()
        gain_box[mine] = gain_rows[:, aligned(mine, block)]

    run_lines(last_sum, line_one.rounds - 2)

    def line_copy(step, end):
        return remote(
            gain_line.at[end],
            gain_line.at[end],
            last_send.at[step],
            last_receive.at[end],
            (place.p, place.c, lax.rem(place.t + step, cfg.tensor)),
        )

    for end, at_t in enumerate(ends):

        @pl.when(place.t == at_t)
        def _(end=end):
            for mask in range(cfg.dp):
                for apart in range(2):
                    if mask or apart:
                        core = place.c if apart == 0 else 1 - place.c
                        gain_copy(mask, core).wait_recv()
            gain_line[end] = jnp.sum(gain_box[...], 0)
            for step in range(1, cfg.tensor):
                line_copy(step, end).start()

    run_lines(line_one.rounds - 2, line_one.rounds)
    keep(result, grad_out)
    line_two.run(heads + line_one.rounds, line_two.rounds)
    keep(final, activations_out)
    for end, at_t in enumerate(ends):

        @pl.when(place.t != at_t)
        def _(end=end):
            line_copy(1, end).wait_recv()

    gain_one[:, :block] = gain_line[0] + gain_line[1]
    keep(gain_one.at[:, pl.ds(0, block)], gain_out)
    for s in scatters:
        s.finish()

    @pl.when(place.at_end)
    def _():
        for mask in range(cfg.dp):
            for apart in range(2):
                if mask or apart:
                    core = place.c if apart == 0 else 1 - place.c
                    gain_copy(mask, core).wait_send()
        for step in range(1, cfg.tensor):
            line_copy(step, 0).wait_send()

    for copy in swaps:
        copy.wait_send()
    line_two.drain()
    line_one.drain()
    for copy in stores:
        copy.wait()


def backward_call(cfg, *operands):
    tokens, width, units = cfg.tokens, cfg.width, cfg.hidden_units
    any_spec = pl.BlockSpec(memory_space=pl.ANY)
    shape = jax.ShapeDtypeStruct
    bits = cfg.dp.bit_length() - 1
    mine = cfg.dp * cfg.block
    heads, groups, qkv_width = cfg.heads, cfg.groups, cfg.qkv_width
    outs = [
        shape((2, QROWS, width), BF16),
        shape((2, QROWS, width), BF16),
        shape((1 + bits, cfg.block, 2 * units), BF16),
        shape((1 + bits, cfg.block, qkv_width), BF16),
        shape((1 + bits, cfg.query_width, cfg.block), BF16),
        shape((8, cfg.block), F32),
    ]
    halves = (2, QROWS, width)
    scratch = [
        pltpu.VMEM(halves, BF16),
        pltpu.VMEM((cfg.query_width, width), BF16),
        pltpu.VMEM((width, qkv_width), BF16),
        pltpu.VMEM((heads, tokens, HD), BF16),
        pltpu.VMEM((groups, 2 * tokens, HD), BF16),
        pltpu.VMEM((groups, 2 * tokens, HD), BF16),
        pltpu.VMEM((2 * tokens, mine), BF16),
        pltpu.VMEM((2 * tokens, cfg.query_width), BF16),
        pltpu.VMEM((2 * tokens, mine), BF16),
        pltpu.VMEM((2 * tokens, qkv_width), BF16),
        pltpu.VMEM((tokens, width), BF16),
        pltpu.VMEM((QROWS, width), F32),
        pltpu.VMEM(halves, BF16),
        pltpu.VMEM(halves, BF16),
        pltpu.VMEM(halves, BF16),
        pltpu.VMEM((QROWS, width), F32),
        pltpu.VMEM(halves, BF16),
        pltpu.VMEM(halves, BF16),
        pltpu.VMEM(halves, BF16),
        pltpu.VMEM((mine, 2 * units), BF16),
        pltpu.VMEM(Scatter.inbox_shape(cfg.dp, cfg.block, 2 * units), BF16),
        pltpu.VMEM(Scatter.inbox_shape(cfg.dp, cfg.block, qkv_width), BF16),
        pltpu.VMEM(Scatter.inbox_shape(cfg.dp, cfg.query_width, cfg.block), BF16),
        pltpu.VMEM((mine, qkv_width), BF16),
        pltpu.VMEM((cfg.query_width, mine), BF16),
        pltpu.VMEM((heads, tokens, HD), BF16),
        pltpu.VMEM((groups, 2 * tokens, HD), F32),
        pltpu.VMEM((groups, 2 * tokens, HD), F32),
        pltpu.VMEM((tokens, 2 * cfg.key_width), F32),
        pltpu.VMEM((tokens, 2 * cfg.key_width), F32),
        pltpu.VMEM((tokens, 128), F32),
        pltpu.VMEM((tokens, 128), F32),
        pltpu.VMEM((2, cfg.window, QROWS), F32),
        pltpu.VMEM((16, width), BF16),
        pltpu.VMEM((8, width), F32),
        pltpu.VMEM((8, width), F32),
        pltpu.VMEM((8, width), F32),
        pltpu.VMEM((2 * cfg.dp, 8, cfg.block), F32),
        pltpu.VMEM((2, 8, cfg.block), F32),
        pltpu.SemaphoreType.DMA((16,)),
        pltpu.SemaphoreType.DMA((3,)),
        pltpu.SemaphoreType.DMA((3, cfg.dp)),
        pltpu.SemaphoreType.DMA((4, max(cfg.dp, 2))),
        pltpu.SemaphoreType.DMA((4, max(cfg.dp, 2))),
        pltpu.SemaphoreType.DMA((1,)),
        pltpu.SemaphoreType.DMA((1,)),
        pltpu.SemaphoreType.DMA((cfg.dp, 2)),
        pltpu.SemaphoreType.DMA((cfg.dp, 2)),
        pltpu.SemaphoreType.DMA((cfg.tensor,)),
        pltpu.SemaphoreType.DMA((2,)),
    ]
    scratch += LineSum.semaphores(cfg.pieces) * 2
    scratch += Scatter.semaphores(cfg.dp) * 3
    in_specs = [any_spec] * 15 + [
        pl.BlockSpec(memory_space=pltpu.SMEM),
        pl.BlockSpec(memory_space=pltpu.VMEM),
    ]
    return pl.pallas_call(
        functools.partial(backward_kernel, cfg),
        out_shape=outs,
        in_specs=in_specs,
        out_specs=[any_spec] * len(outs),
        scratch_shapes=scratch,
        compiler_params=pltpu.CompilerParams(
            collective_id=3, has_side_effects=True, vmem_limit_bytes=VMEM_LIMIT
        ),
        name="attention_backward",
    )(*operands)


def solution(mesh):
    dp, tensor = mesh.shape["dp"], mesh.shape["tensor"]

    def shards(
        inputs, cotangent, doc_lengths, gain_attn, w_query, w_key, w_value, w_out, gain_mlp,
        w_gate, w_up, w_down,
    ):
        tokens, width = inputs.shape
        cfg = Config(
            dp,
            tensor,
            tokens,
            width,
            w_query.shape[1] // HD,
            w_key.shape[1] // HD,
            w_gate.shape[1],
        )
        freq = jnp.tile(frequencies(), (8, 4))
        gains = jnp.zeros((16, gain_attn.shape[0]), F32).at[0].set(gain_attn).at[1].set(gain_mlp)
        (
            _, _, wqkv, wo, gains_full, normed, q, k, v, mixed, hidden,
            n2_all, dy_all, act_all, dgu_all, dn2, terms,
        ) = forward_call(
            cfg, inputs, cotangent, doc_lengths, freq, gains,
            w_query, w_key, w_value, w_out, w_gate, w_up, w_down,
        )
        gu_rows, down_terms, db, dh, gain_two = mlp_call(
            cfg, dn2, n2_all, dy_all, act_all, dgu_all, cotangent, hidden, gains_full
        )
        activations, input_grad, gu_terms, qkv_terms, out_terms, gain_sums = backward_call(
            cfg, db, mixed, wo, wqkv, q, k, v, normed, inputs, dh, terms, hidden,
            gu_rows, gain_two, gains_full, doc_lengths, freq,
        )

        def total(pieces):
            return jnp.sum(pieces.astype(F32), 0)

        qkv_grad = total(qkv_terms)
        units = cfg.hidden_units
        query_width, key_width = cfg.query_width, cfg.key_width
        return (
            activations.reshape(tokens, width),
            input_grad.reshape(tokens, width).astype(F32),
            gain_sums[0],
            qkv_grad[:, :query_width],
            qkv_grad[:, query_width : query_width + key_width],
            qkv_grad[:, query_width + key_width :],
            total(out_terms),
            gain_sums[1],
            total(gu_terms[:, :, :units]),
            total(gu_terms[:, :, units:]),
            total(down_terms),
        )

    rows, columns, gain = P(("dp", "context"), "tensor"), P("tensor", ("dp", "context")), P(("dp", "context"))
    tokens = P(("dp", "context"), None)
    return jax.shard_map(
        shards,
        mesh=mesh,
        in_specs=(tokens, tokens, P("dp", None), gain, rows, rows, rows, columns, gain, rows, rows, columns),
        out_specs=(tokens, tokens, gain, rows, rows, rows, columns, gain, rows, rows, columns),
        check_vma=False,
    )
```

```python
import functools
import math

import jax
import jax.numpy as jnp
from jax import lax
from jax.experimental import pallas as pl
from jax.experimental.pallas import tpu as pltpu
from jax.sharding import PartitionSpec as P

HD = 64
WINDOW = 512
QROWS = 256
EPSILON = 1e-05
NEGATIVE = -1e30
MESH = pl.DeviceIdType.MESH
F32 = jnp.float32
BF16 = jnp.bfloat16
NN = (((1,), (0,)), ((), ()))
NT = (((1,), (1,)), ((), ()))
TN = (((0,), (0,)), ((), ()))
VMEM_LIMIT = 127 * 2**19


def dot(left, right, dims=NN):
    return lax.dot_general(left, right, dims, preferred_element_type=F32)


def frequencies():
    exponent = jnp.arange(0, HD, 2).astype(jnp.float32) / HD
    initial = 1.0 / 500000.0**exponent
    wavelength = 2.0 * math.pi / initial
    smoothing = (8192.0 / wavelength - 1.0) / 3.0
    blended = (1.0 - smoothing) * initial / 32.0 + smoothing * initial
    return jnp.where(
        wavelength < 2048.0, initial, jnp.where(wavelength > 8192.0, initial / 32.0, blended)
    )


def aligned(index, size):
    return pl.ds(pl.multiple_of(index * size, size), size)


class Place:
    def __init__(self, dp, tensor):
        self.dp, self.tensor = dp, tensor
        self.bits = dp.bit_length() - 1
        self.p = lax.axis_index("dp")
        self.c = lax.axis_index("context")
        self.t = lax.axis_index("tensor")
        self.core = (self.p, 1 - self.c, self.t)
        self.low = lax.rem(lax.div(self.t * 2, tensor), 2)
        self.early = 1 - self.low
        self.late = self.low
        step = 1 - 2 * self.low
        self.inward = (self.p, self.c, self.t + step)
        self.outward = (self.p, self.c, self.t - step)
        edge = self.low * (tensor - 1 - self.t) + (1 - self.low) * self.t
        self.depth = edge
        self.at_end = edge == 0

    def flipped(self, mask):
        position = self.p
        for b in range(self.bits):
            if mask >> b & 1:
                bit = lax.rem(lax.div(self.p, 2**b), 2)
                position = position + (1 - 2 * bit) * 2**b
        return position

    def across(self, b):
        return (self.flipped(1 << b), self.c, self.t)

    def greet(self):
        barrier = pltpu.get_barrier_semaphore()
        for device in [self.core] + [self.across(b) for b in range(self.bits)] + [self.inward]:
            pl.semaphore_signal(barrier, inc=1, device_id=device, device_id_type=MESH)

        @pl.when(jnp.logical_not(self.at_end))
        def _():
            pl.semaphore_signal(barrier, inc=1, device_id=self.outward, device_id_type=MESH)

    def meet(self):
        barrier = pltpu.get_barrier_semaphore()

        @pl.when(self.at_end)
        def _():
            pl.semaphore_wait(barrier, 2 + self.bits)

        @pl.when(jnp.logical_not(self.at_end))
        def _():
            pl.semaphore_wait(barrier, 3 + self.bits)


def remote(source, target, send, receive, device):
    return pltpu.make_async_remote_copy(
        src_ref=source,
        dst_ref=target,
        send_sem=send,
        recv_sem=receive,
        device_id=device,
        device_id_type=MESH,
    )


def orders_of(bits, halves):
    forward = tuple(range(bits))
    return (forward, forward[::-1]) if halves == 2 else (forward,)


def phase_masks(order, phase):
    masks = [0]
    for b in order[:phase]:
        masks = masks + [m | 1 << b for m in masks]
    return [m | 1 << order[phase] for m in masks]


class Gather:
    def __init__(self, place, shard, full, axis, sems, halves=2):
        self.place, self.shard, self.full, self.axis = place, shard, full, axis
        self.halves = halves
        self.send, self.receive, self.core_send, self.core_receive, self.local = sems
        self.orders = orders_of(place.bits, halves)
        self.rows = shard.shape[0] // halves
        self.sends = []

    @staticmethod
    def semaphores(dp, halves=2):
        bits = dp.bit_length() - 1
        return [
            pltpu.SemaphoreType.DMA((halves, dp, max(bits, 1))),
            pltpu.SemaphoreType.DMA((halves, dp)),
            pltpu.SemaphoreType.DMA((halves, dp)),
            pltpu.SemaphoreType.DMA((halves, dp)),
            pltpu.SemaphoreType.DMA((1,)),
        ]

    def part(self, half):
        return self.shard.at[pl.ds(half * self.rows, self.rows)]

    def slot(self, position, core, half):
        index = position * 2 + core
        if self.axis == 0:
            rows = self.shard.shape[0]
            first = pl.multiple_of(index * rows + half * self.rows, self.rows)
            return self.full.at[pl.ds(first, self.rows)]
        return self.full.at[
            pl.ds(half * self.rows, self.rows), aligned(index, self.shard.shape[1])
        ]

    def _forward(self, half, mask, source):
        place = self.place
        order = self.orders[half]
        last = max([order.index(b) for b in order if mask >> b & 1], default=-1)
        target = self.slot(place.flipped(mask), place.c, half)
        for j in range(last + 1, place.bits):
            copy = remote(
                source,
                target,
                self.send.at[half, mask, j],
                self.receive.at[half, mask | 1 << order[j]],
                place.across(order[j]),
            )
            copy.start()
            self.sends.append(copy)
        copy = remote(
            source,
            target,
            self.core_send.at[half, mask],
            self.core_receive.at[half, mask],
            place.core,
        )
        copy.start()
        self.sends.append(copy)

    def start(self):
        place = self.place
        for half in range(self.halves):
            self._forward(half, 0, self.part(half))
        index = place.p * 2 + place.c
        if self.axis == 0:
            own = self.full.at[aligned(index, self.shard.shape[0])]
        else:
            own = self.full.at[:, aligned(index, self.shard.shape[1])]
        self.own = pltpu.make_async_copy(self.shard, own, self.local.at[0])
        self.own.start()

    def pass_on(self, phase):
        place = self.place
        for half in range(self.halves):
            for mask in phase_masks(self.orders[half], phase):
                source = self.slot(place.flipped(mask), place.c, half)
                remote(
                    source,
                    source,
                    self.send.at[half, mask, 0],
                    self.receive.at[half, mask],
                    place.core,
                ).wait_recv()
                self._forward(half, mask, source)

    def finish(self):
        place = self.place
        self.own.wait()
        for half in range(self.halves):
            for mask in range(place.dp):
                target = self.slot(place.flipped(mask), 1 - place.c, half)
                remote(
                    target,
                    target,
                    self.core_send.at[half, mask],
                    self.core_receive.at[half, mask],
                    place.core,
                ).wait_recv()

    def drain(self):
        for copy in self.sends:
            copy.wait_send()
        self.sends = []


class LineSum:
    lags = (0, 3, 5, 7)

    def __init__(self, place, part, inbox, result, sems, pieces, root):
        self.place, self.part, self.inbox, self.result = place, part, inbox, result
        self.sum_send, self.sum_receive, self.back_send, self.back_receive = sems
        self.pieces = pieces
        self.rows = part.shape[1] // pieces
        self.rounds = pieces + self.lags[-1]
        self.root = root

    @staticmethod
    def semaphores(pieces):
        return [pltpu.SemaphoreType.DMA((2, pieces))] * 4

    def _copy(self, kind, flow, i, device):
        rows = aligned(i, self.rows)
        if kind == "sum":
            return remote(
                self.part.at[flow, rows],
                self.inbox.at[flow, rows],
                self.sum_send.at[flow, i],
                self.sum_receive.at[flow, i],
                device,
            )
        return remote(
            self.result.at[flow, rows],
            self.result.at[flow, rows],
            self.back_send.at[flow, i],
            self.back_receive.at[flow, i],
            device,
        )

    def _add(self, flow, i):
        rows = aligned(i, self.rows)
        total = self.part[flow, rows].astype(F32) + self.inbox[flow, rows].astype(F32)
        self.part[flow, rows] = total.astype(BF16)

    def early_start(self):
        @pl.when(self.place.at_end)
        def _():
            def one(i, carry):
                self._copy("sum", self.place.early, i, self.place.inward).start()
                return carry

            lax.fori_loop(0, self.pieces, one, 0)

    def early_sum(self, i):
        place = self.place

        @pl.when(jnp.logical_not(place.at_end))
        def _():
            copy = self._copy("sum", place.early, i, place.inward)
            copy.wait_recv()
            self._add(place.early, i)
            copy.start()

    def late_sum(self, i):
        place = self.place
        copy = self._copy("sum", place.late, i, place.outward)
        copy.wait_recv()

        @pl.when(jnp.logical_not(place.at_end))
        def _():
            self._add(place.late, i)
            copy.start()

        @pl.when(place.at_end)
        def _():
            rows = aligned(i, self.rows)
            total = self.part[place.late, rows].astype(F32)
            total = total + self.inbox[place.late, rows].astype(F32)
            self.root(i, rows, total)
            self._copy("back", place.late, i, place.inward).start()

    def late_back(self, i):
        place = self.place

        @pl.when(jnp.logical_not(place.at_end))
        def _():
            copy = self._copy("back", place.late, i, place.inward)
            copy.wait_recv()
            copy.start()

    def early_back(self, i):
        place = self.place
        copy = self._copy("back", place.early, i, place.outward)
        copy.wait_recv()

        @pl.when(jnp.logical_not(place.at_end))
        def _():
            copy.start()

    def round(self, n):
        for lag, kind in zip(self.lags, ("early_sum", "late_sum", "late_back", "early_back")):
            i = n - lag
            if isinstance(i, int):
                if 0 <= i < self.pieces:
                    getattr(self, kind)(i)
            else:

                @pl.when((i >= 0) & (i < self.pieces))
                def _(kind=kind, i=i):
                    getattr(self, kind)(i)

    def run(self, first, last):
        def one(n, carry):
            self.round(n)
            return carry

        lax.fori_loop(first, last, one, 0)

    def drain(self):
        place = self.place

        def one(i, carry):
            self._copy("sum", place.early, i, place.inward).wait_send()
            self._copy("back", place.late, i, place.inward).wait_send()

            @pl.when(jnp.logical_not(place.at_end))
            def _():
                self._copy("sum", place.late, i, place.outward).wait_send()
                self._copy("back", place.early, i, place.outward).wait_send()

            return carry

        lax.fori_loop(0, self.pieces, one, 0)


class Scatter:
    def __init__(self, place, part, inbox, out, axis, sems):
        self.place, self.part, self.inbox, self.out, self.axis = place, part, inbox, out, axis
        self.send, self.receive, self.local = sems
        self.orders = orders_of(place.bits, 2)
        self.rows = out.shape[1] // 2
        self.sends = []

    @staticmethod
    def semaphores(dp):
        return [
            pltpu.SemaphoreType.DMA((2, dp)),
            pltpu.SemaphoreType.DMA((2, dp)),
            pltpu.SemaphoreType.DMA((1,)),
        ]

    @staticmethod
    def inbox_shape(dp, rows, columns):
        slots = sum(2**phase - 1 for phase in range(1, dp.bit_length() - 1))
        return (2, max(slots, 1), rows // 2, columns)

    def slot(self, position, half):
        if self.axis == 0:
            rows = self.out.shape[1]
            first = pl.multiple_of(position * rows + half * self.rows, self.rows)
            return self.part.at[pl.ds(first, self.rows)]
        return self.part.at[
            pl.ds(half * self.rows, self.rows), aligned(position, self.out.shape[2])
        ]

    def landing(self, half, phase, mask):
        if mask == 0:
            return self.out.at[1 + phase, pl.ds(half * self.rows, self.rows)]
        return self.inbox.at[half, self.code(half, phase, mask)]

    def code(self, half, phase, mask):
        order = self.orders[half]
        number = 0
        for later in range(self.place.bits - 1, phase, -1):
            number += 2**later - 1
        inside = [m for m in range(1, self.place.dp) if all(b in order[:phase] for b in bits_of(m))]
        return number + inside.index(mask)

    def _copies(self, half, phase):
        order = self.orders[half]
        b = order[phase]
        for mask in phase_masks(order, phase):
            yield remote(
                self.slot(self.place.flipped(mask), half),
                self.landing(half, phase, mask & ~(1 << b)),
                self.send.at[half, mask],
                self.receive.at[half, mask],
                self.place.across(b),
            )

    def start(self):
        place = self.place
        index = place.p
        if self.axis == 0:
            own = self.part.at[aligned(index, self.out.shape[1])]
        else:
            own = self.part.at[:, aligned(index, self.out.shape[2])]
        self.own = pltpu.make_async_copy(own, self.out.at[0], self.local.at[0])
        self.own.start()
        if place.bits:
            self._send(place.bits - 1)

    def _send(self, phase):
        for half in range(2):
            for copy in self._copies(half, phase):
                copy.start()
                self.sends.append(copy)

    def pass_on(self, phase):
        for half in range(2):
            order = self.orders[half]
            for copy, mask in zip(self._copies(half, phase), phase_masks(order, phase)):
                rest = mask & ~(1 << order[phase])
                if rest:
                    copy.wait_recv()
                    target = self.slot(self.place.flipped(rest), half)
                    source = self.landing(half, phase, rest)
                    pieces = max(1, self.rows // 64)
                    size = self.rows // pieces

                    def add(i, carry, target=target, source=source, size=size):
                        rows = aligned(i, size)
                        total = target[rows].astype(F32) + source[rows].astype(F32)
                        target[rows] = total.astype(BF16)
                        return carry

                    lax.fori_loop(0, pieces, add, 0)
        self._send(phase - 1)

    def finish(self):
        self.own.wait()
        for phase in range(self.place.bits):
            for half in range(2):
                order = self.orders[half]
                for copy, mask in zip(self._copies(half, phase), phase_masks(order, phase)):
                    if not mask & ~(1 << order[phase]):
                        copy.wait_recv()
        for copy in self.sends:
            copy.wait_send()
        self.sends = []


def bits_of(mask):
    return [b for b in range(mask.bit_length()) if mask >> b & 1]


def turned(z):
    width = z.shape[-1]
    half = HD // 2
    if width == 2 * HD:
        lane = lax.broadcasted_iota(jnp.int32, z.shape, 1)
        return jnp.where(lax.rem(lane, HD) < half, pltpu.roll(z, width - half, 1), pltpu.roll(z, half, 1))
    pieces = []
    for h in range(width // HD):
        pieces += [z[:, h * HD + half : (h + 1) * HD], z[:, h * HD : h * HD + half]]
    return jnp.concatenate(pieces, -1)


def document_starts(lengths, rows):
    starts = jnp.zeros(rows.shape, jnp.int32)
    end = lengths[0, 0]
    for k in range(lengths.shape[1]):
        starts = jnp.where(rows >= end, end, starts)
        if k + 1 < lengths.shape[1]:
            end = end + lengths[0, k + 1]
    return starts


def tables(place, lengths, freq, cosine, sine, tokens):
    rows = lax.broadcasted_iota(jnp.int32, (tokens, 128), 0) + place.c * tokens
    angle = (rows - document_starts(lengths, rows)).astype(F32) * freq[0:1, :]
    lane = lax.broadcasted_iota(jnp.int32, (tokens, 128), 1)
    cosine[...] = jnp.cos(angle)
    turned_sine = jnp.sin(angle)
    sine[...] = jnp.where(lax.rem(lane, HD) < HD // 2, -turned_sine, turned_sine)


def fill_bias(place, lengths, bias, tokens):
    keys = bias.shape[1]
    for b in range(tokens // QROWS):
        shape = (keys, QROWS)
        query = lax.broadcasted_iota(jnp.int32, shape, 1) + (place.c * tokens + b * QROWS)
        key = lax.broadcasted_iota(jnp.int32, shape, 0) + place.c * b * QROWS
        row = lax.broadcasted_iota(jnp.int32, (8, QROWS), 1) + (place.c * tokens + b * QROWS)
        starts = document_starts(lengths, row)[0:1, :]
        bias[b] = jnp.where((key >= starts) & (key <= query), 0.0, NEGATIVE)


def softmax_of(key, query, bias):
    scores = dot(key, query, NT) + bias
    highest = jnp.max(scores, 0, keepdims=True)
    raw = jnp.exp(scores - highest)
    return raw * (1.0 / jnp.sum(raw, 0, keepdims=True))


def forward_kernel(cfg, *refs):
    (
        x_in, dy_in, lengths, freq, gains_in, wq_in, wk_in, wv_in, wo_in, wg_in, wu_in, wd_in,
        gu_full, wd_full,
        qkv_out, wo_out, gains_out, normed_out, q_out, k_out, v_out, mixed_out, hidden_out,
        n2_all, dy_all, act_all, dgu_all, dn2_out, terms_out,
        x, wq, wk, wv, wo, wraw, wd, gains32,
        sqkv, swo, sgu, swd, sgains,
        wqkv, wout, gains, normed, rscale, cosine, sine, bias,
        qh, kh, vh, kv, kv_in, mixed, part, inbox, result, hidden,
        gu_buffer, wd_buffer, act, dgu, dn2_sum, terms_sum,
        load, store, kv_send, kv_receive, fill, spill, swap_send, swap_receive,
        chunk_send, chunk_receive, *sems,
    ) = refs
    place = Place(cfg.dp, cfg.tensor)
    tokens, width = x.shape
    heads, groups = cfg.heads, cfg.groups
    query_width, key_width = cfg.query_width, cfg.key_width
    units, chunks = cfg.hidden_units, cfg.chunks
    chunk = units // chunks
    block, owners = cfg.block, cfg.dp
    loads = []

    def fetch(source, target):
        copy = pltpu.make_async_copy(source, target, load.at[len(loads)])
        copy.start()
        loads.append(copy)
        return copy

    small = [
        fetch(source, target)
        for source, target in ((gains_in, gains32), (wq_in, wq), (wk_in, wk), (wv_in, wv))
    ]
    load_x, load_wo = fetch(x_in, x), fetch(wo_in, wo)
    load_wg, load_wd = fetch(wg_in, wraw), fetch(wd_in, wd)
    place.greet()
    n_sems = 5
    gathers = []

    def gather(shard, full, axis, halves=2):
        at = n_sems * len(gathers)
        gathers.append(Gather(place, shard, full, axis, sems[at : at + n_sems], halves))
        return gathers[-1]

    g_gains = gather(sgains, gains, 1, 1)
    g_qkv = gather(sqkv, wqkv, 0)
    g_wo = gather(swo, wout, 1)
    g_gu, g_wd = [], []
    for i in range(chunks):
        columns = pl.ds(i * 2 * chunk, 2 * chunk)
        g_gu.append(gather(sgu.at[:, columns], gu_full.at[:, columns], 0))
        rows = pl.ds(i * chunk, chunk)
        g_wd.append(gather(swd.at[rows], wd_full.at[rows], 1))
    line_sems = sems[n_sems * len(gathers) :]
    for copy in small:
        copy.wait()
    sgains[...] = gains32[...].astype(BF16)
    sqkv[:, :query_width] = wq[...].astype(BF16)
    sqkv[:, query_width : query_width + key_width] = wk[...].astype(BF16)
    sqkv[:, query_width + key_width :] = wv[...].astype(BF16)
    place.meet()
    g_gains.start()
    g_qkv.start()
    load_wo.wait()
    swo[...] = wo[...].astype(BF16)

    def stage(second):
        for i in range(chunks):
            first = (2 * i + second) * chunk
            sgu[:, first : first + chunk] = wraw[:, i * chunk : (i + 1) * chunk].astype(BF16)

    load_wg.wait()
    stage(0)
    load_wu = fetch(wu_in, wraw)
    for phase in range(place.bits):
        g_gains.pass_on(phase)
        g_qkv.pass_on(phase)
        if phase == 0:
            g_wo.start()
            load_x.wait()
            rows_at = 64

            def scale(i, carry):
                rows = aligned(i, rows_at)
                wide = x[rows].astype(F32)
                mean = jnp.sum(wide * wide, -1, keepdims=True) * (1.0 / width)
                rscale[rows] = lax.rsqrt(mean + EPSILON)
                return carry

            lax.fori_loop(0, tokens // rows_at, scale, 0)
            tables(place, lengths, freq, cosine, sine, tokens)
            fill_bias(place, lengths, bias, tokens)
            load_wu.wait()
            stage(1)
            load_wd.wait()
            for i in range(chunks):
                rows = pl.ds(i * chunk, chunk)
                swd[rows] = wd[rows].astype(BF16)
    g_gains.finish()

    def norm(i, carry):
        rows = aligned(i, 64)
        scaled = x[rows].astype(F32) * rscale[rows]
        normed[rows] = (scaled * gains[0:1, :].astype(F32)).astype(BF16)
        return carry

    lax.fori_loop(0, tokens // 64, norm, 0)
    stores = []

    def keep(source, target):
        copy = pltpu.make_async_copy(source, target, store.at[len(stores)])
        copy.start()
        stores.append(copy)
        return copy

    normed_kept = keep(normed, normed_out)
    keep(gains, gains_out)
    g_qkv.finish()
    keep(wqkv, qkv_out)

    def begin(i):
        g_gu[i].start()
        g_wd[i].start()

    def advance(i, phase):
        g_gu[i].pass_on(phase)
        g_wd[i].pass_on(phase)

    for b in range(tokens // QROWS):
        rows = pl.ds(b * QROWS, QROWS)
        product = dot(normed[rows], wqkv[...])
        if b == 0:
            if place.bits:
                g_wo.pass_on(0)
            begin(0)
            begin(1)
        table_c, table_s = cosine[rows], sine[rows]
        for column in range(query_width // 128):
            z = product[:, column * 128 : (column + 1) * 128]
            z = (z * table_c + turned(z) * table_s) * HD**-0.5
            for h in range(2):
                qh[2 * column + h, rows] = z[:, h * HD : (h + 1) * HD].astype(BF16)
        z = product[:, query_width : query_width + key_width]
        if key_width % 128 == 0:
            wide = key_width // 128
            table_c = jnp.concatenate([table_c] * wide, -1)
            table_s = jnp.concatenate([table_s] * wide, -1)
        else:
            table_c, table_s = table_c[:, :key_width], table_s[:, :key_width]
        z = z * table_c + turned(z) * table_s
        kv[rows, :key_width] = z.astype(BF16)
        kv[rows, key_width:] = product[:, query_width + key_width :].astype(BF16)
    pass_kv = remote(kv, kv_in, kv_send.at[0], kv_receive.at[0], place.core)

    @pl.when(place.c == 0)
    def _():
        pass_kv.start()
        for g in range(groups):
            kh[g, tokens:] = jnp.zeros((tokens, HD), BF16)
            vh[g, tokens:] = jnp.zeros((tokens, HD), BF16)

    own_rows = aligned(place.c, tokens)
    for g in range(groups):
        kh[g, own_rows] = kv[:, g * HD : (g + 1) * HD]
        vh[g, own_rows] = kv[:, key_width + g * HD : key_width + (g + 1) * HD]

    @pl.when(place.c == 1)
    def _():
        pass_kv.wait_recv()
        for g in range(groups):
            kh[g, :tokens] = kv_in[:, g * HD : (g + 1) * HD]
            vh[g, :tokens] = kv_in[:, key_width + g * HD : key_width + (g + 1) * HD]

    keep(qh, q_out)
    keep(kh, k_out)
    keep(vh, v_out)
    normed_kept.wait()
    dy = normed
    load_dy = fetch(dy_in, dy)

    def attend(b):
        rows = aligned(b, QROWS)
        window = pl.ds(pl.multiple_of(place.c * b * QROWS, QROWS), bias.shape[1])

        def pair(j, carry):
            outs = []
            for h in range(2):
                head = 2 * j + h
                g = lax.div(head, heads // groups)
                weights = softmax_of(kh[g, window], qh[head, rows], bias[b]).astype(BF16)
                outs.append(dot(vh[g, window], weights, TN))
            mixed[rows, aligned(j, 128)] = jnp.concatenate(outs, 0).T.astype(BF16)
            return carry

        lax.fori_loop(0, heads // 2, pair, 0)

    def project(b):
        rows = aligned(b, QROWS)
        part[b] = dot(mixed[rows], wout[...]).astype(BF16)

    def root(i, rows, total):
        local = pl.ds(pl.multiple_of(place.late * QROWS + i * line.rows, line.rows), line.rows)
        total = total + x[local].astype(F32)
        hidden[rows] = total
        r = lax.rsqrt(jnp.sum(total * total, -1, keepdims=True) * (1.0 / width) + EPSILON)
        result[place.late, rows] = (total * r * gains[1:2, :].astype(F32)).astype(BF16)

    line = LineSum(place, part, inbox, result, line_sems, cfg.pieces, root)
    attend(place.early)
    for phase in range(1, place.bits):
        g_wo.pass_on(phase)
    g_wo.finish()
    keep(wout, wo_out)
    project(place.early)
    line.early_start()
    attend(place.late)
    project(place.late)
    keep(mixed, mixed_out)

    swaps, owns = [], []

    def swap(source, target, k, q, target_rows, sub):
        columns = pl.ds(q * block, block)
        copy = remote(
            source.at[:, aligned(2 * q + 1 - place.c, block)],
            target.at[pl.ds(tokens + sub, target_rows), columns],
            swap_send.at[k, q],
            swap_receive.at[k, q],
            place.core,
        )
        copy.start()
        swaps.append(copy)
        copy = pltpu.make_async_copy(
            source.at[:, aligned(2 * q + place.c, block)],
            target.at[pl.ds(sub, target_rows), columns],
            fill.at[k, q],
        )
        copy.start()
        owns.append(copy)

    load_dy.wait()
    for q in range(owners):
        swap(dy, dy_all, 0, q, tokens, 0)

    agenda = [(2, advance, 0, 0), (2, begin, 2), (9, advance, 1, 0), (9, begin, 3)]
    if not place.bits:
        agenda = [item for item in agenda if item[1] is begin]
    at = 0
    for mark, action, *rest in agenda:
        line.run(at, mark)
        action(*rest)
        at = mark
    line.run(at, line.rounds)
    for i in range(2):
        for phase in range(1, place.bits):
            advance(i, phase)
    if place.bits:
        advance(2, 0)
    for b in range(2):
        for q in range(owners):
            swap(result.at[b], n2_all, 1 + b, q, QROWS, b * QROWS)
    keep(hidden, hidden_out)

    def chunk_load(i):
        slot = i % 2
        return [
            pltpu.make_async_copy(
                gu_full.at[:, pl.ds(i * 2 * chunk, 2 * chunk)], gu_buffer.at[slot], spill.at[slot, 0]
            ),
            pltpu.make_async_copy(
                wd_full.at[pl.ds(i * chunk, chunk)], wd_buffer.at[slot], spill.at[slot, 1]
            ),
        ]

    def take(i):
        g_gu[i].finish()
        g_wd[i].finish()
        for copy in chunk_load(i):
            copy.start()

    def give(i):
        slot = i % 2
        act_columns, dgu_columns = pl.ds(i * chunk, chunk), pl.ds(i * 2 * chunk, 2 * chunk)
        copies = []
        for k, (source, target, columns) in enumerate(
            ((act, act_all, act_columns), (dgu, dgu_all, dgu_columns))
        ):
            copies.append(
                pltpu.make_async_copy(
                    source.at[slot], target.at[pl.ds(0, tokens), columns], spill.at[slot, 2 + k]
                )
            )
            copies.append(
                remote(
                    source.at[slot],
                    target.at[pl.ds(tokens, tokens), columns],
                    chunk_send.at[i, k],
                    chunk_receive.at[i, k],
                    place.core,
                )
            )
        return copies

    tile = width // 4
    n2 = result[...].reshape(tokens, width)
    take(0)
    for i in range(chunks):
        slot = i % 2
        for copy in chunk_load(i):
            copy.wait()
        if i + 1 < chunks:
            if i == 0:
                take(1)
        if i >= 2:
            own_act, sent_act, own_dgu, sent_dgu = give(i - 2)
            own_act.wait()
            own_dgu.wait()
            sent_act.wait_send()
            sent_dgu.wait_send()
        n2 = result[...].reshape(tokens, width)
        both = dot(n2, gu_buffer[slot])
        back = dot(dy[...], wd_buffer[slot], NT)
        gate, upward = both[:, :chunk], both[:, chunk:]
        sigmoid = 1.0 / (1.0 + jnp.exp(-gate))
        swish = gate * sigmoid
        act[slot] = (swish * upward).astype(BF16)
        dgu[slot, :, :chunk] = (
            back * upward * sigmoid * (1.0 + gate * (1.0 - sigmoid))
        ).astype(BF16)
        dgu[slot, :, chunk:] = (back * swish).astype(BF16)
        for copy in give(i):
            copy.start()

        def add(n, carry, i=i, slot=slot):
            columns = aligned(n, tile)
            more = dot(dgu[slot], gu_buffer[slot, columns], NT)
            terms = dot(act[slot], wd_buffer[slot, :, columns])
            if i:
                more = more + dn2_sum[:, columns]
                terms = terms + terms_sum[:, columns]
            if i + 1 < chunks:
                dn2_sum[:, columns] = more
                terms_sum[:, columns] = terms
            else:
                for b in range(2):
                    part[b, :, columns] = more[b * QROWS : (b + 1) * QROWS].astype(BF16)
                    inbox[b, :, columns] = terms[b * QROWS : (b + 1) * QROWS].astype(BF16)
            return carry

        if i + 1 == chunks:
            line.drain()
        lax.fori_loop(0, 4, add, 0)
        if 2 <= i + 1 < chunks:
            if i + 2 < chunks and place.bits:
                advance(i + 2, 0)
            for phase in range(1, place.bits):
                advance(i + 1, phase)
            take(i + 1)
    keep(part, dn2_out)
    keep(inbox, terms_out)
    for i in range(max(chunks - 2, 0), chunks):
        own_act, sent_act, own_dgu, sent_dgu = give(i)
        own_act.wait()
        own_dgu.wait()
        sent_act.wait_send()
        sent_dgu.wait_send()
    for i in range(chunks):
        own_act, sent_act, own_dgu, sent_dgu = give(i)
        sent_act.wait_recv()
        sent_dgu.wait_recv()
    for g in gathers:
        g.drain()
    for copy in owns:
        copy.wait()
    for copy in swaps:
        copy.wait_recv()
        copy.wait_send()

    @pl.when(place.c == 0)
    def _():
        pass_kv.wait_send()

    for copy in stores[1:]:
        copy.wait()


class Config:
    def __init__(self, dp, tensor, tokens, width, heads, groups, hidden_units):
        self.dp, self.tensor, self.tokens, self.width = dp, tensor, tokens, width
        self.heads, self.groups, self.hidden_units = heads, groups, hidden_units
        self.pieces = 8
        self.chunks = 4
        self.behind = 12
        self.marks = (4, 4, 11)
        self.query_width, self.key_width = heads * HD, groups * HD
        self.qkv_width = self.query_width + 2 * self.key_width
        self.blocks = dp * 2
        self.block = width // self.blocks
        self.window = WINDOW + QROWS


def forward_call(cfg, x, dy, lengths, freq, gains, wq, wk, wv, wo, wg, wu, wd):
    tokens, width, units = cfg.tokens, cfg.width, cfg.hidden_units
    any_spec = pl.BlockSpec(memory_space=pl.ANY)
    shape = jax.ShapeDtypeStruct
    mine = cfg.dp * cfg.block
    chunk = units // cfg.chunks
    outs = [
        shape((width, 2 * units), BF16),
        shape((units, width), BF16),
        shape((width, cfg.qkv_width), BF16),
        shape((cfg.query_width, width), BF16),
        shape((16, width), BF16),
        shape((tokens, width), BF16),
        shape((cfg.heads, tokens, HD), BF16),
        shape((cfg.groups, 2 * tokens, HD), BF16),
        shape((cfg.groups, 2 * tokens, HD), BF16),
        shape((tokens, cfg.query_width), BF16),
        shape((QROWS, width), F32),
        shape((2 * tokens, mine), BF16),
        shape((2 * tokens, mine), BF16),
        shape((2 * tokens, units), BF16),
        shape((2 * tokens, 2 * units), BF16),
        shape((2, QROWS, width), BF16),
        shape((2, QROWS, width), BF16),
    ]
    scratch = [pltpu.VMEM(x.shape, BF16)]
    scratch += [pltpu.VMEM(w.shape, F32) for w in (wq, wk, wv, wo, wg, wd, gains)]
    scratch += [pltpu.VMEM((wq.shape[0], cfg.qkv_width), BF16)]
    scratch += [pltpu.VMEM(wo.shape, BF16)]
    scratch += [pltpu.VMEM((wg.shape[0], 2 * units), BF16)]
    scratch += [pltpu.VMEM(wd.shape, BF16)]
    scratch += [pltpu.VMEM(gains.shape, BF16)]
    scratch += [
        pltpu.VMEM((width, cfg.qkv_width), BF16),
        pltpu.VMEM((cfg.query_width, width), BF16),
        pltpu.VMEM((16, width), BF16),
        pltpu.VMEM((tokens, width), BF16),
        pltpu.VMEM((tokens, 1), F32),
        pltpu.VMEM((tokens, 128), F32),
        pltpu.VMEM((tokens, 128), F32),
        pltpu.VMEM((2, cfg.window, QROWS), F32),
        pltpu.VMEM((cfg.heads, tokens, HD), BF16),
        pltpu.VMEM((cfg.groups, 2 * tokens, HD), BF16),
        pltpu.VMEM((cfg.groups, 2 * tokens, HD), BF16),
        pltpu.VMEM((tokens, 2 * cfg.key_width), BF16),
        pltpu.VMEM((tokens, 2 * cfg.key_width), BF16),
        pltpu.VMEM((tokens, cfg.query_width), BF16),
        pltpu.VMEM((2, QROWS, width), BF16),
        pltpu.VMEM((2, QROWS, width), BF16),
        pltpu.VMEM((2, QROWS, width), BF16),
        pltpu.VMEM((QROWS, width), F32),
        pltpu.VMEM((2, width, 2 * chunk), BF16),
        pltpu.VMEM((2, chunk, width), BF16),
        pltpu.VMEM((2, tokens, chunk), BF16),
        pltpu.VMEM((2, tokens, 2 * chunk), BF16),
        pltpu.VMEM((tokens, width), F32),
        pltpu.VMEM((tokens, width), F32),
        pltpu.SemaphoreType.DMA((10,)),
        pltpu.SemaphoreType.DMA((14,)),
        pltpu.SemaphoreType.DMA((1,)),
        pltpu.SemaphoreType.DMA((1,)),
        pltpu.SemaphoreType.DMA((3, cfg.dp)),
        pltpu.SemaphoreType.DMA((2, 4)),
        pltpu.SemaphoreType.DMA((3, cfg.dp)),
        pltpu.SemaphoreType.DMA((3, cfg.dp)),
        pltpu.SemaphoreType.DMA((cfg.chunks, 2)),
        pltpu.SemaphoreType.DMA((cfg.chunks, 2)),
    ]
    for halves in [1] + [2] * (2 + 2 * cfg.chunks):
        scratch += Gather.semaphores(cfg.dp, halves)
    scratch += LineSum.semaphores(cfg.pieces)
    return pl.pallas_call(
        functools.partial(forward_kernel, cfg),
        out_shape=outs,
        in_specs=[
            any_spec,
            any_spec,
            pl.BlockSpec(memory_space=pltpu.SMEM),
            pl.BlockSpec(memory_space=pltpu.VMEM),
        ]
        + [any_spec] * 8,
        out_specs=[any_spec] * len(outs),
        scratch_shapes=scratch,
        compiler_params=pltpu.CompilerParams(
            collective_id=1, has_side_effects=True, vmem_limit_bytes=VMEM_LIMIT
        ),
        name="attention_forward",
    )(x, dy, lengths, freq, gains, wq, wk, wv, wo, wg, wu, wd)


def backward_kernel(cfg, *refs):
    (
        dn2_in, n2_in, dy_all_in, act_in, dgu_in, dy_in, hidden_in, terms_in,
        mixed_in, wo_in, qkv_in, q_in, k_in, v_in, normed_in, x_in, gains_in, lengths, freq,
        activations_out, grad_out, down_out, gu_out, qkv_out, out_out, gain_out,
        dy, hidden, dh, gains, n2_all, dy_all, act, dgu, gu_rows, down,
        part, inbox, result, terms, inbox_two, final,
        relay_down, relay_gu, relay_qkv, relay_out, qh, kh, vh,
        dmixed, dk, dv, dkv, dkv_in, cosine, sine, bias,
        gain_two, gain_one, gain_rows, gain_box, gain_line,
        load, store, own_sem, swap_send, swap_receive, dkv_send, dkv_receive,
        gain_send, gain_receive, last_send, last_receive, ready, *sems,
    ) = refs
    place = Place(cfg.dp, cfg.tensor)
    tokens, width = dy.shape
    heads, groups = cfg.heads, cfg.groups
    query_width, key_width, qkv_width = cfg.query_width, cfg.key_width, cfg.qkv_width
    units = act.shape[1]
    chunk = units // cfg.chunks
    block, owners = cfg.block, cfg.dp
    mine = owners * block
    spare = list(sems[3 * 4 + 4 * 3 :])
    at = 0

    def carve(array, rows, columns, first_row=0, first_column=0):
        if array.shape[0] >= first_row + rows and array.shape[1] >= first_column + columns:
            return array.at[pl.ds(first_row, rows), pl.ds(first_column, columns)]
        return spare.pop(0)

    views = []
    for columns in (mine, mine, qkv_width, qkv_width, query_width):
        views.append(carve(dgu, 2 * tokens, columns, 0, at))
        at += columns
    normed_all, db_all, dqkv, qkv_rows, mixed_all = views
    x = carve(act, tokens, width)
    wo = carve(act, query_width, width, tokens)
    wqkv = carve(down, width, qkv_width)
    out_columns = carve(n2_all, query_width, mine)
    loads = []

    def fetch(source, target):
        copy = pltpu.make_async_copy(source, target, load.at[len(loads)])
        copy.start()
        loads.append(copy)
        return copy

    load_part = fetch(dn2_in, part)
    first = [
        fetch(dy_in, dy),
        fetch(hidden_in, hidden),
        fetch(gains_in, gains),
        fetch(act_in, act),
        fetch(dy_all_in, dy_all),
    ]
    second = [fetch(n2_in, n2_all), fetch(dgu_in, dgu)]
    third = [fetch(terms_in, terms), fetch(q_in, qh), fetch(k_in, kh), fetch(v_in, vh)]
    barrier = pltpu.get_barrier_semaphore()
    greeted = [place.core]
    for mask in range(1, cfg.dp):
        greeted += [(place.flipped(mask), place.c, place.t), (place.flipped(mask), 1 - place.c, place.t)]
    for step in range(1, cfg.tensor):
        greeted.append((place.p, place.c, lax.rem(place.t + step, cfg.tensor)))
    for device in greeted:
        pl.semaphore_signal(barrier, inc=1, device_id=device, device_id_type=MESH)
    gain_two[...] = jnp.zeros_like(gain_two)
    gain_one[...] = jnp.zeros_like(gain_one)
    pl.semaphore_wait(barrier, len(greeted))
    n_line, n_scatter = 4, 3
    scatters = []
    for i, (rows, relay, out, axis) in enumerate(
        [
            (down, relay_down, down_out, 1),
            (gu_rows, relay_gu, gu_out, 0),
            (out_columns, relay_out, out_out, 1),
            (qkv_rows, relay_qkv, qkv_out, 0),
        ]
    ):
        at = 3 * n_line + n_scatter * i
        scatters.append(Scatter(place, rows, relay, out, axis, sems[at : at + n_scatter]))
    s_down, s_gu, s_out, s_qkv = scatters

    def local_rows(i):
        rows = QROWS // cfg.pieces
        return pl.ds(pl.multiple_of(place.late * QROWS + i * rows, rows), rows)

    def norm_back(source, total, gain, gain_sum):
        r = lax.rsqrt(jnp.sum(source * source, -1, keepdims=True) * (1.0 / width) + EPSILON)
        scaled = source * r
        gain_sum[...] += jnp.sum((total * scaled).reshape(-1, 8, width), 0)
        e = total * gain
        mean = jnp.sum(e * scaled, -1, keepdims=True) * (1.0 / width)
        return r * (e - scaled * mean)

    def root_three(i, rows, total):
        back = norm_back(hidden[rows], total, gains[1:2, :].astype(F32), gain_two)
        grad = dy[local_rows(i)].astype(F32) + back
        dh[rows] = grad
        result[place.late, rows] = grad.astype(BF16)

    def root_two(i, rows, total):
        final[place.late, rows] = (hidden[rows] + total).astype(BF16)

    def root_one(i, rows, total):
        source = x[local_rows(i)].astype(F32)
        back = norm_back(source, total, gains[0:1, :].astype(F32), gain_one)
        result[place.late, rows] = (dh[rows] + back).astype(BF16)

    line_three = LineSum(place, part, inbox, result, sems[:n_line], cfg.pieces, root_three)
    line_two = LineSum(
        place, terms, inbox_two, final, sems[n_line : 2 * n_line], cfg.pieces, root_two
    )
    line_one = LineSum(
        place, part, inbox, result, sems[2 * n_line : 3 * n_line], cfg.pieces, root_one
    )
    load_part.wait()
    line_three.early_start()

    def grad_down(i):
        rows = aligned(i, units // 4)
        down[rows] = dot(act[:, rows], dy_all[...], TN).astype(BF16)

    def grad_gate_up(i):
        target = aligned(lax.rem(i, 2) * cfg.chunks + lax.div(i, 2), chunk)
        gu_rows[:, target] = dot(n2_all[...], dgu[:, aligned(i, chunk)], TN).astype(BF16)

    def lines(n):
        line_three.round(n)
        line_two.round(n - cfg.behind)

    def between(fill, rounds, fills):
        def one(i, carry):
            lines(rounds + i)
            fill(fills + i)
            return carry

        lax.fori_loop(0, 4, one, 0)

    for copy in first:
        copy.wait()
    between(grad_down, 0, 0)
    s_down.start()
    tables(place, lengths, freq, cosine, sine, tokens)
    fill_bias(place, lengths, bias, tokens)
    for copy in second + third:
        copy.wait()
    between(grad_gate_up, 4, 0)
    between(grad_gate_up, 8, 4)
    line_two.early_start()
    pl.semaphore_signal(ready, inc=1, device_id=place.core, device_id_type=MESH)
    rest = [
        fetch(wo_in, wo),
        fetch(x_in, x),
        fetch(mixed_in, mixed_all.at[pl.ds(0, tokens)]),
    ]
    for phase in range(place.bits - 1, 0, -1):
        s_down.pass_on(phase)
    s_gu.start()
    lines(12)
    pl.semaphore_wait(ready, 1)
    swaps, owns, db_swaps, db_owns = [], [], [], []

    def swap(source, target, k, q, kept):
        copy = remote(source, target, swap_send.at[k, q], swap_receive.at[k, q], place.core)
        copy.start()
        kept.append(copy)

    def own(source, target, k, q, kept):
        copy = pltpu.make_async_copy(source, target, own_sem.at[k, q])
        copy.start()
        kept.append(copy)

    def shares(q):
        return pl.ds(q * block, block), aligned(2 * q + 1 - place.c, block), aligned(2 * q + place.c, block)

    for q in range(owners):
        columns, theirs, ours = shares(q)
        swap(normed_in.at[:, theirs], normed_all.at[pl.ds(tokens, tokens), columns], 0, q, swaps)
        own(normed_in.at[:, ours], normed_all.at[pl.ds(0, tokens), columns], 0, q, owns)
    swap(mixed_in, mixed_all.at[pl.ds(tokens, tokens)], 3, 0, swaps)
    lines(13)
    lines(14)
    db = result
    for b in range(2):
        for q in range(owners):
            columns, theirs, ours = shares(q)
            target = pl.ds(tokens + b * QROWS, QROWS)
            swap(db.at[b, :, theirs], db_all.at[target, columns], 1 + b, q, db_swaps)
            target = pl.ds(b * QROWS, QROWS)
            own(db.at[b, :, ours], db_all.at[target, columns], 1 + b, q, db_owns)
    for copy in rest:
        copy.wait()

    def back_out(b, carry):
        product = dot(db[b], wo[...], NT)
        rows = aligned(b, QROWS)
        for h in range(heads):
            dmixed[h, rows] = product[:, h * HD : (h + 1) * HD].astype(BF16)
        return carry

    lax.fori_loop(0, 2, back_out, 0)
    dk[...] = jnp.zeros_like(dk)
    dv[...] = jnp.zeros_like(dv)

    def attend_back(b, rounds):
        rows = aligned(b, QROWS)
        window = pl.ds(pl.multiple_of(place.c * b * QROWS, QROWS), bias.shape[1])

        def pair(j, carry):
            outs = []
            for h in range(2):
                head = 2 * j + h
                g = lax.div(head, heads // groups)
                key, value = kh[g, window], vh[g, window]
                query, grad = qh[head, rows], dmixed[head, rows]
                weights = softmax_of(key, query, bias[b])
                dprobs = dot(value, grad, NT)
                delta = jnp.sum(weights * dprobs, 0, keepdims=True)
                dscores = (weights * (dprobs - delta)).astype(BF16)
                dv[g, window] += dot(weights.astype(BF16), grad)
                dk[g, window] += dot(dscores, query)
                outs.append(dot(key, dscores, TN))
            z = jnp.concatenate(outs, 0).T * HD**-0.5
            z = z * cosine[rows] - turned(z) * sine[rows]
            dqkv[rows, aligned(j, 128)] = z.astype(BF16)
            line_two.round(rounds + j)
            return carry

        lax.fori_loop(0, heads // 2, pair, 0)

    done = line_three.rounds - cfg.behind
    attend_back(place.early, done)
    for copy in db_owns + owns:
        copy.wait()
    for copy in db_swaps + swaps:
        copy.wait_recv()
        copy.wait_send()
    s_down.finish()
    load_qkv = fetch(qkv_in, wqkv)
    out_columns[...] = dot(mixed_all[...], db_all[...], TN).astype(BF16)
    s_out.start()
    attend_back(place.late, done + heads // 2)
    done = done + heads
    stores = []

    def keep(source, target):
        copy = pltpu.make_async_copy(source, target, store.at[len(stores)])
        copy.start()
        stores.append(copy)

    pass_back = remote(dkv, dkv_in, dkv_send.at[0], dkv_receive.at[0], place.core)

    def packed(rows):
        return jnp.concatenate(
            [dk[g, rows] for g in range(groups)] + [dv[g, rows] for g in range(groups)], -1
        )

    @pl.when(place.c == 1)
    def _():
        dkv[...] = packed(pl.ds(0, tokens))
        pass_back.start()

    own_rows = aligned(place.c, tokens)
    z = packed(own_rows)

    @pl.when(place.c == 0)
    def _():
        pass_back.wait_recv()
        dkv[...] = z + dkv_in[...]

    @pl.when(place.c == 1)
    def _():
        pass_back.wait_send()
        dkv[...] = z

    dkeys = dkv[:, :key_width]
    if key_width % 128 == 0:
        wide_by = key_width // 128
        table_c = jnp.concatenate([cosine[...]] * wide_by, -1)
        table_s = jnp.concatenate([sine[...]] * wide_by, -1)
    else:
        table_c, table_s = cosine[:, :key_width], sine[:, :key_width]
    dkeys = dkeys * table_c - turned(dkeys) * table_s
    dqkv[:tokens, query_width : query_width + key_width] = dkeys.astype(BF16)
    dqkv[:tokens, query_width + key_width :] = dkv[:, key_width:].astype(BF16)
    late_swaps = []
    swap(dqkv.at[pl.ds(0, tokens)], dqkv.at[pl.ds(tokens, tokens)], 3, 1, late_swaps)
    load_qkv.wait()
    columns_at = width // 4

    def back_through(b):
        def one(i, carry):
            rows, columns = aligned(b, QROWS), aligned(i, columns_at)
            part[b, :, columns] = dot(dqkv[rows], wqkv[columns], NT).astype(BF16)
            return carry

        lax.fori_loop(0, 4, one, 0)

    def run_lines(start, stop):
        def one(n, carry):
            line_one.round(n)
            line_two.round(done + n)
            return carry

        lax.fori_loop(start, stop, one, 0)

    line_three.drain()
    back_through(place.early)
    line_one.early_start()
    back_through(place.late)
    run_lines(0, 1)
    for copy in late_swaps:
        copy.wait_recv()
    qkv_rows[...] = dot(normed_all[...], dqkv[...], TN).astype(BF16)
    s_qkv.start()
    run_lines(1, 4)
    agenda = []
    for phase in range(place.bits - 1, 0, -1):
        for s in (s_gu, s_out, s_qkv):
            agenda.append(functools.partial(s.pass_on, phase))
    last_sum = cfg.pieces + line_one.lags[1]
    marks = [4 + (last_sum - 4) * (k + 1) // (len(agenda) + 1) for k in range(len(agenda))]
    at = 4
    for mark, item in zip(marks, agenda):
        run_lines(at, mark)
        item()
        at = mark
    run_lines(at, last_sum)

    ends = (0, cfg.tensor - 1)
    mine = place.p * 2 + place.c

    def gain_copy(mask, core):
        index = place.flipped(mask) * 2 + core
        return remote(
            gain_rows.at[:, aligned(index, block)],
            gain_box.at[mine],
            gain_send.at[mask, lax.rem(core + place.c, 2)],
            gain_receive.at[mask, lax.rem(core + place.c, 2)],
            (place.flipped(mask), core, place.t),
        )

    others = [(mask, core) for mask in range(cfg.dp) for core in range(2)]

    @pl.when(place.at_end)
    def _():
        gain_rows[0:1, :] = jnp.sum(gain_one[...], 0, keepdims=True)
        gain_rows[1:2, :] = jnp.sum(gain_two[...], 0, keepdims=True)
        gain_rows[2:, :] = jnp.zeros((6, width), F32)
        for mask in range(cfg.dp):
            for apart in range(2):
                if mask or apart:
                    core = place.c if apart == 0 else 1 - place.c
                    gain_copy(mask, core).start()
        gain_box[mine] = gain_rows[:, aligned(mine, block)]

    run_lines(last_sum, line_one.rounds - 2)

    def line_copy(step, end):
        return remote(
            gain_line.at[end],
            gain_line.at[end],
            last_send.at[step],
            last_receive.at[end],
            (place.p, place.c, lax.rem(place.t + step, cfg.tensor)),
        )

    for end, at_t in enumerate(ends):

        @pl.when(place.t == at_t)
        def _(end=end):
            for mask in range(cfg.dp):
                for apart in range(2):
                    if mask or apart:
                        core = place.c if apart == 0 else 1 - place.c
                        gain_copy(mask, core).wait_recv()
            gain_line[end] = jnp.sum(gain_box[...], 0)
            for step in range(1, cfg.tensor):
                line_copy(step, end).start()

    run_lines(line_one.rounds - 2, line_one.rounds)
    keep(result, grad_out)
    line_two.run(done + line_one.rounds, line_two.rounds)
    keep(final, activations_out)
    for end, at_t in enumerate(ends):

        @pl.when(place.t != at_t)
        def _(end=end):
            line_copy(1, end).wait_recv()

    gain_one[:, :block] = gain_line[0] + gain_line[1]
    keep(gain_one.at[:, pl.ds(0, block)], gain_out)
    for s in scatters[1:]:
        s.finish()

    @pl.when(place.at_end)
    def _():
        for mask in range(cfg.dp):
            for apart in range(2):
                if mask or apart:
                    core = place.c if apart == 0 else 1 - place.c
                    gain_copy(mask, core).wait_send()
        for step in range(1, cfg.tensor):
            line_copy(step, 0).wait_send()

    for copy in late_swaps:
        copy.wait_send()
    line_two.drain()
    line_one.drain()
    for copy in stores:
        copy.wait()


def backward_call(cfg, *operands):
    tokens, width, units = cfg.tokens, cfg.width, cfg.hidden_units
    any_spec = pl.BlockSpec(memory_space=pl.ANY)
    shape = jax.ShapeDtypeStruct
    bits = cfg.dp.bit_length() - 1
    mine = cfg.dp * cfg.block
    heads, groups, qkv_width = cfg.heads, cfg.groups, cfg.qkv_width
    outs = [
        shape((2, QROWS, width), BF16),
        shape((2, QROWS, width), BF16),
        shape((1 + bits, units, cfg.block), BF16),
        shape((1 + bits, cfg.block, 2 * units), BF16),
        shape((1 + bits, cfg.block, qkv_width), BF16),
        shape((1 + bits, cfg.query_width, cfg.block), BF16),
        shape((8, cfg.block), F32),
    ]
    halves = (2, QROWS, width)
    scratch = [
        pltpu.VMEM((tokens, width), BF16),
        pltpu.VMEM((QROWS, width), F32),
        pltpu.VMEM((QROWS, width), F32),
        pltpu.VMEM((16, width), BF16),
        pltpu.VMEM((2 * tokens, mine), BF16),
        pltpu.VMEM((2 * tokens, mine), BF16),
        pltpu.VMEM((2 * tokens, units), BF16),
        pltpu.VMEM((2 * tokens, 2 * units), BF16),
        pltpu.VMEM((mine, 2 * units), BF16),
        pltpu.VMEM((units, mine), BF16),
    ]
    scratch += [pltpu.VMEM(halves, BF16)] * 6
    scratch += [
        pltpu.VMEM(Scatter.inbox_shape(cfg.dp, units, cfg.block), BF16),
        pltpu.VMEM(Scatter.inbox_shape(cfg.dp, cfg.block, 2 * units), BF16),
        pltpu.VMEM(Scatter.inbox_shape(cfg.dp, cfg.block, qkv_width), BF16),
        pltpu.VMEM(Scatter.inbox_shape(cfg.dp, cfg.query_width, cfg.block), BF16),
        pltpu.VMEM((heads, tokens, HD), BF16),
        pltpu.VMEM((groups, 2 * tokens, HD), BF16),
        pltpu.VMEM((groups, 2 * tokens, HD), BF16),
        pltpu.VMEM((heads, tokens, HD), BF16),
        pltpu.VMEM((groups, 2 * tokens, HD), F32),
        pltpu.VMEM((groups, 2 * tokens, HD), F32),
        pltpu.VMEM((tokens, 2 * cfg.key_width), F32),
        pltpu.VMEM((tokens, 2 * cfg.key_width), F32),
        pltpu.VMEM((tokens, 128), F32),
        pltpu.VMEM((tokens, 128), F32),
        pltpu.VMEM((2, cfg.window, QROWS), F32),
        pltpu.VMEM((8, width), F32),
        pltpu.VMEM((8, width), F32),
        pltpu.VMEM((8, width), F32),
        pltpu.VMEM((2 * cfg.dp, 8, cfg.block), F32),
        pltpu.VMEM((2, 8, cfg.block), F32),
        pltpu.SemaphoreType.DMA((16,)),
        pltpu.SemaphoreType.DMA((3,)),
        pltpu.SemaphoreType.DMA((3, cfg.dp)),
        pltpu.SemaphoreType.DMA((4, max(cfg.dp, 2))),
        pltpu.SemaphoreType.DMA((4, max(cfg.dp, 2))),
        pltpu.SemaphoreType.DMA((1,)),
        pltpu.SemaphoreType.DMA((1,)),
        pltpu.SemaphoreType.DMA((cfg.dp, 2)),
        pltpu.SemaphoreType.DMA((cfg.dp, 2)),
        pltpu.SemaphoreType.DMA((cfg.tensor,)),
        pltpu.SemaphoreType.DMA((2,)),
        pltpu.SemaphoreType.REGULAR,
    ]
    scratch += LineSum.semaphores(cfg.pieces) * 3
    scratch += Scatter.semaphores(cfg.dp) * 4
    at = 0
    for columns in (mine, mine, qkv_width, qkv_width, cfg.query_width):
        if 2 * units < at + columns:
            scratch.append(pltpu.VMEM((2 * tokens, columns), BF16))
        at += columns
    if units < width:
        scratch.append(pltpu.VMEM((tokens, width), BF16))
    if units < width or 2 * tokens < tokens + cfg.query_width:
        scratch.append(pltpu.VMEM((cfg.query_width, width), BF16))
    if units < width or mine < qkv_width:
        scratch.append(pltpu.VMEM((width, qkv_width), BF16))
    if 2 * tokens < cfg.query_width:
        scratch.append(pltpu.VMEM((cfg.query_width, mine), BF16))
    in_specs = [any_spec] * 17 + [
        pl.BlockSpec(memory_space=pltpu.SMEM),
        pl.BlockSpec(memory_space=pltpu.VMEM),
    ]
    return pl.pallas_call(
        functools.partial(backward_kernel, cfg),
        out_shape=outs,
        in_specs=in_specs,
        out_specs=[any_spec] * len(outs),
        scratch_shapes=scratch,
        compiler_params=pltpu.CompilerParams(
            collective_id=3, has_side_effects=True, vmem_limit_bytes=VMEM_LIMIT
        ),
        name="backward",
    )(*operands)


def solution(mesh):
    dp, tensor = mesh.shape["dp"], mesh.shape["tensor"]

    def shards(
        inputs, cotangent, doc_lengths, gain_attn, w_query, w_key, w_value, w_out, gain_mlp,
        w_gate, w_up, w_down,
    ):
        tokens, width = inputs.shape
        cfg = Config(
            dp,
            tensor,
            tokens,
            width,
            w_query.shape[1] // HD,
            w_key.shape[1] // HD,
            w_gate.shape[1],
        )
        freq = jnp.tile(frequencies(), (8, 4))
        gains = jnp.zeros((16, gain_attn.shape[0]), F32).at[0].set(gain_attn).at[1].set(gain_mlp)
        (
            _, _, wqkv, wo, gains_full, normed, q, k, v, mixed, hidden,
            n2_all, dy_all, act_all, dgu_all, dn2, terms,
        ) = forward_call(
            cfg, inputs, cotangent, doc_lengths, freq, gains,
            w_query, w_key, w_value, w_out, w_gate, w_up, w_down,
        )
        (
            activations, input_grad, down_terms, gu_terms, qkv_terms, out_terms, gain_sums,
        ) = backward_call(
            cfg, dn2, n2_all, dy_all, act_all, dgu_all, cotangent, hidden, terms,
            mixed, wo, wqkv, q, k, v, normed, inputs, gains_full, doc_lengths, freq,
        )

        def total(pieces):
            return jnp.sum(pieces.astype(F32), 0)

        qkv_grad = total(qkv_terms)
        units = cfg.hidden_units
        query_width, key_width = cfg.query_width, cfg.key_width
        return (
            activations.reshape(tokens, width),
            input_grad.reshape(tokens, width).astype(F32),
            gain_sums[0],
            qkv_grad[:, :query_width],
            qkv_grad[:, query_width : query_width + key_width],
            qkv_grad[:, query_width + key_width :],
            total(out_terms),
            gain_sums[1],
            total(gu_terms[:, :, :units]),
            total(gu_terms[:, :, units:]),
            total(down_terms),
        )

    rows, columns, gain = P(("dp", "context"), "tensor"), P("tensor", ("dp", "context")), P(("dp", "context"))
    tokens = P(("dp", "context"), None)
    return jax.shard_map(
        shards,
        mesh=mesh,
        in_specs=(tokens, tokens, P("dp", None), gain, rows, rows, rows, columns, gain, rows, rows, columns),
        out_specs=(tokens, tokens, gain, rows, rows, rows, columns, gain, rows, rows, columns),
        check_vma=False,
    )
```

```python
import functools
import math

import jax
import jax.numpy as jnp
import numpy as np
from jax import lax
from jax.experimental import pallas as pl
from jax.experimental.pallas import tpu as pltpu
from jax.sharding import PartitionSpec as P

HD = 64
WINDOW = 512
QROWS = 256
EPSILON = 1e-05
NEGATIVE = -1e30
MESH = pl.DeviceIdType.MESH
F32 = jnp.float32
BF16 = jnp.bfloat16
NN = (((1,), (0,)), ((), ()))
NT = (((1,), (1,)), ((), ()))
TN = (((0,), (0,)), ((), ()))
VMEM_LIMIT = 127 * 2**19


def dot(left, right, dims=NN):
    return lax.dot_general(left, right, dims, preferred_element_type=F32)


def frequencies():
    exponent = np.arange(0, HD, 2).astype(np.float32) / np.float32(HD)
    initial = np.float32(1.0) / np.float32(500000.0) ** exponent
    wavelength = np.float32(2.0 * math.pi) / initial
    smoothing = (np.float32(8192.0) / wavelength - np.float32(1.0)) / np.float32(3.0)
    low = initial / np.float32(32.0)
    blended = (np.float32(1.0) - smoothing) * low + smoothing * initial
    return np.where(wavelength < 2048.0, initial, np.where(wavelength > 8192.0, low, blended))


def aligned(index, size):
    return pl.ds(pl.multiple_of(index * size, size), size)


class Place:
    def __init__(self, dp, tensor):
        self.dp, self.tensor = dp, tensor
        self.bits = dp.bit_length() - 1
        self.p = lax.axis_index("dp")
        self.c = lax.axis_index("context")
        self.t = lax.axis_index("tensor")
        self.core = (self.p, 1 - self.c, self.t)
        self.low = lax.rem(lax.div(self.t * 2, tensor), 2)
        self.early = 1 - self.low
        self.late = self.low
        step = 1 - 2 * self.low
        self.inward = (self.p, self.c, self.t + step)
        self.outward = (self.p, self.c, self.t - step)
        edge = self.low * (tensor - 1 - self.t) + (1 - self.low) * self.t
        self.depth = edge
        self.at_end = edge == 0

    def flipped(self, mask):
        position = self.p
        for b in range(self.bits):
            if mask >> b & 1:
                bit = lax.rem(lax.div(self.p, 2**b), 2)
                position = position + (1 - 2 * bit) * 2**b
        return position

    def across(self, b):
        return (self.flipped(1 << b), self.c, self.t)

    def greet(self):
        barrier = pltpu.get_barrier_semaphore()
        for device in [self.core] + [self.across(b) for b in range(self.bits)] + [self.inward]:
            pl.semaphore_signal(barrier, inc=1, device_id=device, device_id_type=MESH)

        @pl.when(jnp.logical_not(self.at_end))
        def _():
            pl.semaphore_signal(barrier, inc=1, device_id=self.outward, device_id_type=MESH)

    def meet(self):
        barrier = pltpu.get_barrier_semaphore()

        @pl.when(self.at_end)
        def _():
            pl.semaphore_wait(barrier, 2 + self.bits)

        @pl.when(jnp.logical_not(self.at_end))
        def _():
            pl.semaphore_wait(barrier, 3 + self.bits)


def remote(source, target, send, receive, device):
    return pltpu.make_async_remote_copy(
        src_ref=source,
        dst_ref=target,
        send_sem=send,
        recv_sem=receive,
        device_id=device,
        device_id_type=MESH,
    )


def orders_of(bits, halves):
    forward = tuple(range(bits))
    return (forward, forward[::-1]) if halves == 2 else (forward,)


def phase_masks(order, phase):
    masks = [0]
    for b in order[:phase]:
        masks = masks + [m | 1 << b for m in masks]
    return [m | 1 << order[phase] for m in masks]


class Gather:
    def __init__(self, place, shard, full, axis, sems, halves=2):
        self.place, self.shard, self.full, self.axis = place, shard, full, axis
        self.halves = halves
        self.send, self.receive, self.core_send, self.core_receive, self.local = sems
        self.orders = orders_of(place.bits, halves)
        self.rows = shard.shape[0] // halves
        self.sends = []

    @staticmethod
    def semaphores(dp, halves=2):
        bits = dp.bit_length() - 1
        return [
            pltpu.SemaphoreType.DMA((halves, dp, max(bits, 1))),
            pltpu.SemaphoreType.DMA((halves, dp)),
            pltpu.SemaphoreType.DMA((halves, dp)),
            pltpu.SemaphoreType.DMA((halves, dp)),
            pltpu.SemaphoreType.DMA((1,)),
        ]

    def part(self, half):
        return self.shard.at[pl.ds(half * self.rows, self.rows)]

    def slot(self, position, core, half):
        index = position * 2 + core
        if self.axis == 0:
            rows = self.shard.shape[0]
            first = pl.multiple_of(index * rows + half * self.rows, self.rows)
            return self.full.at[pl.ds(first, self.rows)]
        return self.full.at[
            pl.ds(half * self.rows, self.rows), aligned(index, self.shard.shape[1])
        ]

    def _forward(self, half, mask, source):
        place = self.place
        order = self.orders[half]
        last = max([order.index(b) for b in order if mask >> b & 1], default=-1)
        target = self.slot(place.flipped(mask), place.c, half)
        for j in range(last + 1, place.bits):
            copy = remote(
                source,
                target,
                self.send.at[half, mask, j],
                self.receive.at[half, mask | 1 << order[j]],
                place.across(order[j]),
            )
            copy.start()
            self.sends.append(copy)
        copy = remote(
            source,
            target,
            self.core_send.at[half, mask],
            self.core_receive.at[half, mask],
            place.core,
        )
        copy.start()
        self.sends.append(copy)

    def start(self):
        place = self.place
        for half in range(self.halves):
            self._forward(half, 0, self.part(half))
        index = place.p * 2 + place.c
        if self.axis == 0:
            own = self.full.at[aligned(index, self.shard.shape[0])]
        else:
            own = self.full.at[:, aligned(index, self.shard.shape[1])]
        self.own = pltpu.make_async_copy(self.shard, own, self.local.at[0])
        self.own.start()

    def pass_on(self, phase):
        place = self.place
        for half in range(self.halves):
            for mask in phase_masks(self.orders[half], phase):
                source = self.slot(place.flipped(mask), place.c, half)
                remote(
                    source,
                    source,
                    self.send.at[half, mask, 0],
                    self.receive.at[half, mask],
                    place.core,
                ).wait_recv()
                self._forward(half, mask, source)

    def finish(self):
        place = self.place
        self.own.wait()
        for half in range(self.halves):
            for mask in range(place.dp):
                target = self.slot(place.flipped(mask), 1 - place.c, half)
                remote(
                    target,
                    target,
                    self.core_send.at[half, mask],
                    self.core_receive.at[half, mask],
                    place.core,
                ).wait_recv()

    def drain(self):
        for copy in self.sends:
            copy.wait_send()
        self.sends = []


class LineSum:
    lags = (0, 3, 5, 7)

    def __init__(self, place, part, inbox, result, sems, pieces, root):
        self.place, self.part, self.inbox, self.result = place, part, inbox, result
        self.sum_send, self.sum_receive, self.back_send, self.back_receive = sems
        self.pieces = pieces
        self.rows = part.shape[1] // pieces
        self.rounds = pieces + self.lags[-1]
        self.root = root

    @staticmethod
    def semaphores(pieces):
        return [pltpu.SemaphoreType.DMA((2, pieces))] * 4

    def _copy(self, kind, flow, i, device):
        rows = aligned(i, self.rows)
        if kind == "sum":
            return remote(
                self.part.at[flow, rows],
                self.inbox.at[flow, rows],
                self.sum_send.at[flow, i],
                self.sum_receive.at[flow, i],
                device,
            )
        return remote(
            self.result.at[flow, rows],
            self.result.at[flow, rows],
            self.back_send.at[flow, i],
            self.back_receive.at[flow, i],
            device,
        )

    def _add(self, flow, i):
        rows = aligned(i, self.rows)
        total = self.part[flow, rows].astype(F32) + self.inbox[flow, rows].astype(F32)
        self.part[flow, rows] = total.astype(BF16)

    def early_start(self):
        @pl.when(self.place.at_end)
        def _():
            def one(i, carry):
                self._copy("sum", self.place.early, i, self.place.inward).start()
                return carry

            lax.fori_loop(0, self.pieces, one, 0)

    def early_sum(self, i):
        place = self.place

        @pl.when(jnp.logical_not(place.at_end))
        def _():
            copy = self._copy("sum", place.early, i, place.inward)
            copy.wait_recv()
            self._add(place.early, i)
            copy.start()

    def late_sum(self, i):
        place = self.place
        copy = self._copy("sum", place.late, i, place.outward)
        copy.wait_recv()

        @pl.when(jnp.logical_not(place.at_end))
        def _():
            self._add(place.late, i)
            copy.start()

        @pl.when(place.at_end)
        def _():
            rows = aligned(i, self.rows)
            total = self.part[place.late, rows].astype(F32)
            total = total + self.inbox[place.late, rows].astype(F32)
            self.root(i, rows, total)
            self._copy("back", place.late, i, place.inward).start()

    def late_back(self, i):
        place = self.place

        @pl.when(jnp.logical_not(place.at_end))
        def _():
            copy = self._copy("back", place.late, i, place.inward)
            copy.wait_recv()
            copy.start()

    def early_back(self, i):
        place = self.place
        copy = self._copy("back", place.early, i, place.outward)
        copy.wait_recv()

        @pl.when(jnp.logical_not(place.at_end))
        def _():
            copy.start()

    def round(self, n):
        for lag, kind in zip(self.lags, ("early_sum", "late_sum", "late_back", "early_back")):
            i = n - lag
            if isinstance(i, int):
                if 0 <= i < self.pieces:
                    getattr(self, kind)(i)
            else:

                @pl.when((i >= 0) & (i < self.pieces))
                def _(kind=kind, i=i):
                    getattr(self, kind)(i)

    def run(self, first, last):
        def one(n, carry):
            self.round(n)
            return carry

        lax.fori_loop(first, last, one, 0)

    def drain(self):
        place = self.place

        def one(i, carry):
            self._copy("sum", place.early, i, place.inward).wait_send()
            self._copy("back", place.late, i, place.inward).wait_send()

            @pl.when(jnp.logical_not(place.at_end))
            def _():
                self._copy("sum", place.late, i, place.outward).wait_send()
                self._copy("back", place.early, i, place.outward).wait_send()

            return carry

        lax.fori_loop(0, self.pieces, one, 0)


class Scatter:
    def __init__(self, place, part, inbox, out, axis, sems):
        self.place, self.part, self.inbox, self.out, self.axis = place, part, inbox, out, axis
        self.send, self.receive, self.local = sems
        self.orders = orders_of(place.bits, 2)
        self.rows = out.shape[1] // 2
        self.sends = []

    @staticmethod
    def semaphores(dp):
        return [
            pltpu.SemaphoreType.DMA((2, dp)),
            pltpu.SemaphoreType.DMA((2, dp)),
            pltpu.SemaphoreType.DMA((1,)),
        ]

    @staticmethod
    def inbox_shape(dp, rows, columns):
        slots = sum(2**phase - 1 for phase in range(1, dp.bit_length() - 1))
        return (2, max(slots, 1), rows // 2, columns)

    def slot(self, position, half):
        if self.axis == 0:
            rows = self.out.shape[1]
            first = pl.multiple_of(position * rows + half * self.rows, self.rows)
            return self.part.at[pl.ds(first, self.rows)]
        return self.part.at[
            pl.ds(half * self.rows, self.rows), aligned(position, self.out.shape[2])
        ]

    def landing(self, half, phase, mask):
        if mask == 0:
            return self.out.at[1 + phase, pl.ds(half * self.rows, self.rows)]
        return self.inbox.at[half, self.code(half, phase, mask)]

    def code(self, half, phase, mask):
        order = self.orders[half]
        number = 0
        for later in range(self.place.bits - 1, phase, -1):
            number += 2**later - 1
        inside = [m for m in range(1, self.place.dp) if all(b in order[:phase] for b in bits_of(m))]
        return number + inside.index(mask)

    def _copies(self, half, phase):
        order = self.orders[half]
        b = order[phase]
        for mask in phase_masks(order, phase):
            yield remote(
                self.slot(self.place.flipped(mask), half),
                self.landing(half, phase, mask & ~(1 << b)),
                self.send.at[half, mask],
                self.receive.at[half, mask],
                self.place.across(b),
            )

    def start(self):
        place = self.place
        index = place.p
        if self.axis == 0:
            own = self.part.at[aligned(index, self.out.shape[1])]
        else:
            own = self.part.at[:, aligned(index, self.out.shape[2])]
        self.own = pltpu.make_async_copy(own, self.out.at[0], self.local.at[0])
        self.own.start()
        if place.bits:
            self._send(place.bits - 1)

    def _send(self, phase):
        for half in range(2):
            for copy in self._copies(half, phase):
                copy.start()
                self.sends.append(copy)

    def pass_on(self, phase):
        for half in range(2):
            order = self.orders[half]
            for copy, mask in zip(self._copies(half, phase), phase_masks(order, phase)):
                rest = mask & ~(1 << order[phase])
                if rest:
                    copy.wait_recv()
                    target = self.slot(self.place.flipped(rest), half)
                    source = self.landing(half, phase, rest)
                    pieces = max(1, self.rows // 64)
                    size = self.rows // pieces

                    def add(i, carry, target=target, source=source, size=size):
                        rows = aligned(i, size)
                        total = target[rows].astype(F32) + source[rows].astype(F32)
                        target[rows] = total.astype(BF16)
                        return carry

                    lax.fori_loop(0, pieces, add, 0)
        self._send(phase - 1)

    def finish(self):
        self.own.wait()
        for phase in range(self.place.bits):
            for half in range(2):
                order = self.orders[half]
                for copy, mask in zip(self._copies(half, phase), phase_masks(order, phase)):
                    if not mask & ~(1 << order[phase]):
                        copy.wait_recv()
        for copy in self.sends:
            copy.wait_send()
        self.sends = []


def bits_of(mask):
    return [b for b in range(mask.bit_length()) if mask >> b & 1]


def turned(z):
    width = z.shape[-1]
    half = HD // 2
    if width == 2 * HD:
        lane = lax.broadcasted_iota(jnp.int32, z.shape, 1)
        return jnp.where(lax.rem(lane, HD) < half, pltpu.roll(z, width - half, 1), pltpu.roll(z, half, 1))
    pieces = []
    for h in range(width // HD):
        pieces += [z[:, h * HD + half : (h + 1) * HD], z[:, h * HD : h * HD + half]]
    return jnp.concatenate(pieces, -1)


def document_starts(lengths, rows):
    starts = jnp.zeros(rows.shape, jnp.int32)
    end = lengths[0, 0]
    for k in range(lengths.shape[1]):
        starts = jnp.where(rows >= end, end, starts)
        if k + 1 < lengths.shape[1]:
            end = end + lengths[0, k + 1]
    return starts


def tables(place, lengths, freq, cosine, sine, tokens):
    rows = lax.broadcasted_iota(jnp.int32, (tokens, 128), 0) + place.c * tokens
    angle = (rows - document_starts(lengths, rows)).astype(F32) * freq[0:1, :]
    lane = lax.broadcasted_iota(jnp.int32, (tokens, 128), 1)
    cosine[...] = jnp.cos(angle)
    turned_sine = jnp.sin(angle)
    sine[...] = jnp.where(lax.rem(lane, HD) < HD // 2, -turned_sine, turned_sine)


def fill_bias(place, lengths, bias, tokens):
    keys = bias.shape[1]
    for b in range(tokens // QROWS):
        shape = (keys, QROWS)
        query = lax.broadcasted_iota(jnp.int32, shape, 1) + (place.c * tokens + b * QROWS)
        key = lax.broadcasted_iota(jnp.int32, shape, 0) + place.c * b * QROWS
        row = lax.broadcasted_iota(jnp.int32, (8, QROWS), 1) + (place.c * tokens + b * QROWS)
        starts = document_starts(lengths, row)[0:1, :]
        bias[b] = jnp.where((key >= starts) & (key <= query), 0.0, NEGATIVE)


def softmax_of(key, query, bias):
    scores = dot(key, query, NT) + bias
    highest = jnp.max(scores, 0, keepdims=True)
    raw = jnp.exp(scores - highest)
    return raw * (1.0 / jnp.sum(raw, 0, keepdims=True))


def forward_kernel(cfg, *refs):
    (
        x_in, dy_in, lengths, freq, gain_a_in, gain_m_in, wq_in, wk_in, wv_in, wo_in, wg_in, wu_in, wd_in,
        gu_full, wd_full,
        qkv_out, wo_out, gains_out, normed_out, q_out, k_out, v_out, mixed_out, hidden_out,
        n2_all, dy_all, act_all, dgu_all, dn2_out, terms_out,
        x, wq, wk, wv, wo, wraw, wd, gain_a, gain_m,
        sqkv, swo, sgu, swd, sgains,
        wqkv, wout, gains, normed, rscale, cosine, sine, bias,
        qh, kh, vh, kv, kv_in, mixed, part, inbox, result, hidden,
        gu_buffer, wd_buffer, act, dgu, dn2_sum, terms_sum, backs,
        load, store, kv_send, kv_receive, fill, spill, swap_send, swap_receive,
        chunk_send, chunk_receive, *sems,
    ) = refs
    place = Place(cfg.dp, cfg.tensor)
    tokens, width = x.shape
    heads, groups = cfg.heads, cfg.groups
    query_width, key_width = cfg.query_width, cfg.key_width
    units, chunks = cfg.hidden_units, len(cfg.chunks)
    block, owners = cfg.block, cfg.dp
    loads = []

    def fetch(source, target):
        copy = pltpu.make_async_copy(source, target, load.at[len(loads)])
        copy.start()
        loads.append(copy)
        return copy

    small = [
        fetch(source, target)
        for source, target in (
            (gain_a_in, gain_a), (gain_m_in, gain_m), (wq_in, wq), (wk_in, wk), (wv_in, wv)
        )
    ]
    load_x, load_wo = fetch(x_in, x), fetch(wo_in, wo)
    load_wg, load_wd = fetch(wg_in, wraw), fetch(wd_in, wd)
    place.greet()
    n_sems = 5
    gathers = []

    def gather(shard, full, axis, halves=2):
        at = n_sems * len(gathers)
        gathers.append(Gather(place, shard, full, axis, sems[at : at + n_sems], halves))
        return gathers[-1]

    g_gains = gather(sgains, gains, 1, 1)
    g_qkv = gather(sqkv, wqkv, 0)
    g_wo = gather(swo, wout, 1)
    g_gu, g_wd = [], []
    for start, count in cfg.chunks:
        columns = pl.ds(2 * start, 2 * count)
        g_gu.append(gather(sgu.at[:, columns], gu_full.at[:, columns], 0))
        rows = pl.ds(start, count)
        g_wd.append(gather(swd.at[rows], wd_full.at[rows], 1))
    line_sems = sems[n_sems * len(gathers) :]
    for copy in small:
        copy.wait()
    sgains[...] = jnp.zeros_like(sgains)
    sgains[0:1] = gain_a[...].astype(BF16)
    sgains[1:2] = gain_m[...].astype(BF16)
    sqkv[:, :query_width] = wq[...].astype(BF16)
    sqkv[:, query_width : query_width + key_width] = wk[...].astype(BF16)
    sqkv[:, query_width + key_width :] = wv[...].astype(BF16)
    place.meet()
    g_gains.start()
    g_qkv.start()
    load_wo.wait()
    swo[...] = wo[...].astype(BF16)

    def stage(second):
        for start, count in cfg.chunks:
            first = 2 * start + second * count
            sgu[:, first : first + count] = wraw[:, start : start + count].astype(BF16)

    load_wg.wait()
    stage(0)
    load_wu = fetch(wu_in, wraw)
    for phase in range(place.bits):
        g_gains.pass_on(phase)
        g_qkv.pass_on(phase)
        if phase == 0:
            g_wo.start()
            load_x.wait()
            rows_at = 64

            def scale(i, carry):
                rows = aligned(i, rows_at)
                wide = x[rows].astype(F32)
                mean = jnp.sum(wide * wide, -1, keepdims=True) * (1.0 / width)
                rscale[rows] = lax.rsqrt(mean + EPSILON)
                return carry

            lax.fori_loop(0, tokens // rows_at, scale, 0)
            tables(place, lengths, freq, cosine, sine, tokens)
            fill_bias(place, lengths, bias, tokens)
            load_wu.wait()
            stage(1)
            load_wd.wait()
            for start, count in cfg.chunks:
                rows = pl.ds(start, count)
                swd[rows] = wd[rows].astype(BF16)
    g_gains.finish()

    def norm(i, carry):
        rows = aligned(i, 64)
        scaled = x[rows].astype(F32) * rscale[rows]
        normed[rows] = (scaled * gains[0:1, :].astype(F32)).astype(BF16)
        return carry

    lax.fori_loop(0, tokens // 64, norm, 0)
    stores = []

    def keep(source, target):
        copy = pltpu.make_async_copy(source, target, store.at[len(stores)])
        copy.start()
        stores.append(copy)
        return copy

    normed_kept = keep(normed, normed_out)
    keep(gains, gains_out)
    g_qkv.finish()
    keep(wqkv, qkv_out)

    def begin(i):
        g_gu[i].start()
        g_wd[i].start()

    def advance(i, phase):
        g_gu[i].pass_on(phase)
        g_wd[i].pass_on(phase)

    for b in range(tokens // QROWS):
        rows = pl.ds(b * QROWS, QROWS)
        product = dot(normed[rows], wqkv[...])
        if b == 0:
            if place.bits:
                g_wo.pass_on(0)
            begin(0)
            begin(1)
        table_c, table_s = cosine[rows], sine[rows]
        for column in range(query_width // 128):
            z = product[:, column * 128 : (column + 1) * 128]
            z = (z * table_c + turned(z) * table_s) * HD**-0.5
            for h in range(2):
                qh[2 * column + h, rows] = z[:, h * HD : (h + 1) * HD].astype(BF16)
        z = product[:, query_width : query_width + key_width]
        if key_width % 128 == 0:
            wide = key_width // 128
            table_c = jnp.concatenate([table_c] * wide, -1)
            table_s = jnp.concatenate([table_s] * wide, -1)
        else:
            table_c, table_s = table_c[:, :key_width], table_s[:, :key_width]
        z = z * table_c + turned(z) * table_s
        kv[rows, :key_width] = z.astype(BF16)
        kv[rows, key_width:] = product[:, query_width + key_width :].astype(BF16)
    pass_kv = remote(kv, kv_in, kv_send.at[0], kv_receive.at[0], place.core)

    @pl.when(place.c == 0)
    def _():
        pass_kv.start()
        for g in range(groups):
            kh[g, tokens:] = jnp.zeros((tokens, HD), BF16)
            vh[g, tokens:] = jnp.zeros((tokens, HD), BF16)

    own_rows = aligned(place.c, tokens)
    for g in range(groups):
        kh[g, own_rows] = kv[:, g * HD : (g + 1) * HD]
        vh[g, own_rows] = kv[:, key_width + g * HD : key_width + (g + 1) * HD]

    @pl.when(place.c == 1)
    def _():
        pass_kv.wait_recv()
        for g in range(groups):
            kh[g, :tokens] = kv_in[:, g * HD : (g + 1) * HD]
            vh[g, :tokens] = kv_in[:, key_width + g * HD : key_width + (g + 1) * HD]

    keep(qh, q_out)
    keep(kh, k_out)
    keep(vh, v_out)
    normed_kept.wait()
    dy = normed
    load_dy = fetch(dy_in, dy)

    def attend(b):
        rows = aligned(b, QROWS)
        window = pl.ds(pl.multiple_of(place.c * b * QROWS, QROWS), bias.shape[1])

        def pair(j, carry):
            outs = []
            for h in range(2):
                head = 2 * j + h
                g = lax.div(head, heads // groups)
                weights = softmax_of(kh[g, window], qh[head, rows], bias[b]).astype(BF16)
                outs.append(dot(vh[g, window], weights, TN))
            mixed[rows, aligned(j, 128)] = jnp.concatenate(outs, 0).T.astype(BF16)
            return carry

        lax.fori_loop(0, heads // 2, pair, 0)

    def project(b):
        rows = aligned(b, QROWS)
        part[b] = dot(mixed[rows], wout[...]).astype(BF16)

    def root(i, rows, total):
        local = pl.ds(pl.multiple_of(place.late * QROWS + i * line.rows, line.rows), line.rows)
        total = total + x[local].astype(F32)
        hidden[rows] = total
        r = lax.rsqrt(jnp.sum(total * total, -1, keepdims=True) * (1.0 / width) + EPSILON)
        result[place.late, rows] = (total * r * gains[1:2, :].astype(F32)).astype(BF16)

    line = LineSum(place, part, inbox, result, line_sems, cfg.pieces, root)
    attend(place.early)
    for phase in range(1, place.bits):
        g_wo.pass_on(phase)
    g_wo.finish()
    keep(wout, wo_out)
    project(place.early)
    line.early_start()
    attend(place.late)
    project(place.late)
    keep(mixed, mixed_out)

    swaps, owns = [], []

    def swap(source, target, k, q, target_rows, sub):
        columns = pl.ds(q * block, block)
        copy = remote(
            source.at[:, aligned(2 * q + 1 - place.c, block)],
            target.at[pl.ds(tokens + sub, target_rows), columns],
            swap_send.at[k, q],
            swap_receive.at[k, q],
            place.core,
        )
        copy.start()
        swaps.append(copy)
        copy = pltpu.make_async_copy(
            source.at[:, aligned(2 * q + place.c, block)],
            target.at[pl.ds(sub, target_rows), columns],
            fill.at[k, q],
        )
        copy.start()
        owns.append(copy)

    load_dy.wait()
    for q in range(owners):
        swap(dy, dy_all, 0, q, tokens, 0)

    def chunk_load(i):
        slot = i % 2
        start, count = cfg.chunks[i]
        return [
            pltpu.make_async_copy(
                gu_full.at[:, pl.ds(2 * start, 2 * count)],
                gu_buffer.at[slot, :, pl.ds(0, 2 * count)],
                spill.at[slot, 0],
            ),
            pltpu.make_async_copy(
                wd_full.at[pl.ds(start, count)],
                wd_buffer.at[slot, pl.ds(0, count)],
                spill.at[slot, 1],
            ),
        ]

    def take(i):
        g_gu[i].finish()
        g_wd[i].finish()
        for copy in chunk_load(i):
            copy.start()

    def from_output(i):
        for copy in chunk_load(i):
            copy.wait()
        return dot(dy[...], wd_buffer[i % 2, : cfg.chunks[i][1]], NT)

    def from_output_early(i):
        backs[i] = from_output(i)

    later = range(1, place.bits)
    agenda = []
    if place.bits:
        agenda.append((2, advance, 0, 0))
    agenda.append((2, begin, 2))
    if place.bits:
        agenda.append((cfg.marks[0], advance, 1, 0))
    agenda += [(cfg.marks[0], begin, 3), (cfg.marks[0], begin, 4)]
    agenda += [(cfg.marks[1], advance, 0, phase) for phase in later]
    agenda += [(cfg.marks[1], take, 0), (cfg.marks[2], from_output_early, 0)]
    agenda += [(cfg.marks[3], advance, 1, phase) for phase in later]
    agenda += [(cfg.marks[3], take, 1)]
    at = 0
    for mark, action, *rest in agenda:
        line.run(at, mark)
        action(*rest)
        at = mark
    line.run(at, line.rounds)
    if place.bits:
        advance(2, 0)
    for b in range(2):
        for q in range(owners):
            swap(result.at[b], n2_all, 1 + b, q, QROWS, b * QROWS)
    keep(hidden, hidden_out)

    def give(i):
        slot = i % 2
        start, count = cfg.chunks[i]
        copies = []
        for k, (source, target, first, wide) in enumerate(
            ((act, act_all, start, count), (dgu, dgu_all, 2 * start, 2 * count))
        ):
            source, columns = source.at[slot, :, pl.ds(0, wide)], pl.ds(first, wide)
            copies.append(
                pltpu.make_async_copy(
                    source, target.at[pl.ds(0, tokens), columns], spill.at[slot, 2 + k]
                )
            )
            copies.append(
                remote(
                    source,
                    target.at[pl.ds(tokens, tokens), columns],
                    chunk_send.at[i, k],
                    chunk_receive.at[i, k],
                    place.core,
                )
            )
        return copies

    tile = width // 4
    for i in range(chunks):
        slot = i % 2
        count = cfg.chunks[i][1]
        if i >= 2:
            own_act, sent_act, own_dgu, sent_dgu = give(i - 2)
            own_act.wait()
            own_dgu.wait()
            sent_act.wait_send()
            sent_dgu.wait_send()
        n2 = result[...].reshape(tokens, width)
        back = backs[0] if i == 0 else from_output(i)
        both = dot(n2, gu_buffer[slot, :, : 2 * count])
        gate, upward = both[:, :count], both[:, count:]
        sigmoid = 1.0 / (1.0 + jnp.exp(-gate))
        swish = gate * sigmoid
        act[slot, :, :count] = (swish * upward).astype(BF16)
        dgu[slot, :, :count] = (
            back * upward * sigmoid * (1.0 + gate * (1.0 - sigmoid))
        ).astype(BF16)
        dgu[slot, :, count : 2 * count] = (back * swish).astype(BF16)
        for copy in give(i):
            copy.start()

        def add(n, carry, i=i, slot=slot, count=count):
            columns = aligned(n, tile)
            more = dot(dgu[slot, :, : 2 * count], gu_buffer[slot, columns, : 2 * count], NT)
            terms = dot(act[slot, :, :count], wd_buffer[slot, :count, columns])
            if i:
                more = more + dn2_sum[:, columns]
                terms = terms + terms_sum[:, columns]
            if i + 1 < chunks:
                dn2_sum[:, columns] = more
                terms_sum[:, columns] = terms
            else:
                for b in range(2):
                    part[b, :, columns] = more[b * QROWS : (b + 1) * QROWS].astype(BF16)
                    inbox[b, :, columns] = terms[b * QROWS : (b + 1) * QROWS].astype(BF16)
            return carry

        if i + 1 == chunks:
            line.drain()
        lax.fori_loop(0, 4, add, 0)
        if i == 0 and place.bits:
            advance(3, 0)
        if i == 1 and place.bits:
            advance(4, 0)
        if 2 <= i + 1 < chunks:
            for phase in later:
                advance(i + 1, phase)
            take(i + 1)
    keep(part, dn2_out)
    keep(inbox, terms_out)
    for i in range(max(chunks - 2, 0), chunks):
        own_act, sent_act, own_dgu, sent_dgu = give(i)
        own_act.wait()
        own_dgu.wait()
        sent_act.wait_send()
        sent_dgu.wait_send()
    for i in range(chunks):
        own_act, sent_act, own_dgu, sent_dgu = give(i)
        sent_act.wait_recv()
        sent_dgu.wait_recv()
    for g in gathers:
        g.drain()
    for copy in owns:
        copy.wait()
    for copy in swaps:
        copy.wait_recv()
        copy.wait_send()

    @pl.when(place.c == 0)
    def _():
        pass_kv.wait_send()

    for copy in stores[1:]:
        copy.wait()


class Config:
    def __init__(self, dp, tensor, tokens, width, heads, groups, hidden_units):
        self.dp, self.tensor, self.tokens, self.width = dp, tensor, tokens, width
        self.heads, self.groups, self.hidden_units = heads, groups, hidden_units
        self.pieces = 8
        eighth = hidden_units // 8
        self.chunks = [(2 * n * eighth, 2 * eighth) for n in range(3)]
        self.chunks += [(6 * eighth, eighth), (7 * eighth, eighth)]
        self.behind = 12
        self.marks = (7, 10, 12, 13)
        self.query_width, self.key_width = heads * HD, groups * HD
        self.qkv_width = self.query_width + 2 * self.key_width
        self.blocks = dp * 2
        self.block = width // self.blocks
        self.window = WINDOW + QROWS


def forward_call(cfg, x, dy, lengths, freq, gain_a, gain_m, wq, wk, wv, wo, wg, wu, wd):
    tokens, width, units = cfg.tokens, cfg.width, cfg.hidden_units
    any_spec = pl.BlockSpec(memory_space=pl.ANY)
    shape = jax.ShapeDtypeStruct
    mine = cfg.dp * cfg.block
    chunk = max(count for _, count in cfg.chunks)
    outs = [
        shape((width, 2 * units), BF16),
        shape((units, width), BF16),
        shape((width, cfg.qkv_width), BF16),
        shape((cfg.query_width, width), BF16),
        shape((16, width), BF16),
        shape((tokens, width), BF16),
        shape((cfg.heads, tokens, HD), BF16),
        shape((cfg.groups, 2 * tokens, HD), BF16),
        shape((cfg.groups, 2 * tokens, HD), BF16),
        shape((tokens, cfg.query_width), BF16),
        shape((QROWS, width), F32),
        shape((2 * tokens, mine), BF16),
        shape((2 * tokens, mine), BF16),
        shape((2 * tokens, units), BF16),
        shape((2 * tokens, 2 * units), BF16),
        shape((2, QROWS, width), BF16),
        shape((2, QROWS, width), BF16),
    ]
    scratch = [pltpu.VMEM(x.shape, BF16)]
    scratch += [pltpu.VMEM(w.shape, F32) for w in (wq, wk, wv, wo, wg, wd, gain_a, gain_m)]
    scratch += [pltpu.VMEM((wq.shape[0], cfg.qkv_width), BF16)]
    scratch += [pltpu.VMEM(wo.shape, BF16)]
    scratch += [pltpu.VMEM((wg.shape[0], 2 * units), BF16)]
    scratch += [pltpu.VMEM(wd.shape, BF16)]
    scratch += [pltpu.VMEM((16, gain_a.shape[1]), BF16)]
    scratch += [
        pltpu.VMEM((width, cfg.qkv_width), BF16),
        pltpu.VMEM((cfg.query_width, width), BF16),
        pltpu.VMEM((16, width), BF16),
        pltpu.VMEM((tokens, width), BF16),
        pltpu.VMEM((tokens, 1), F32),
        pltpu.VMEM((tokens, 128), F32),
        pltpu.VMEM((tokens, 128), F32),
        pltpu.VMEM((2, cfg.window, QROWS), F32),
        pltpu.VMEM((cfg.heads, tokens, HD), BF16),
        pltpu.VMEM((cfg.groups, 2 * tokens, HD), BF16),
        pltpu.VMEM((cfg.groups, 2 * tokens, HD), BF16),
        pltpu.VMEM((tokens, 2 * cfg.key_width), BF16),
        pltpu.VMEM((tokens, 2 * cfg.key_width), BF16),
        pltpu.VMEM((tokens, cfg.query_width), BF16),
        pltpu.VMEM((2, QROWS, width), BF16),
        pltpu.VMEM((2, QROWS, width), BF16),
        pltpu.VMEM((2, QROWS, width), BF16),
        pltpu.VMEM((QROWS, width), F32),
        pltpu.VMEM((2, width, 2 * chunk), BF16),
        pltpu.VMEM((2, chunk, width), BF16),
        pltpu.VMEM((2, tokens, chunk), BF16),
        pltpu.VMEM((2, tokens, 2 * chunk), BF16),
        pltpu.VMEM((tokens, width), F32),
        pltpu.VMEM((tokens, width), F32),
        pltpu.VMEM((1, tokens, chunk), F32),
        pltpu.SemaphoreType.DMA((11,)),
        pltpu.SemaphoreType.DMA((14,)),
        pltpu.SemaphoreType.DMA((1,)),
        pltpu.SemaphoreType.DMA((1,)),
        pltpu.SemaphoreType.DMA((3, cfg.dp)),
        pltpu.SemaphoreType.DMA((2, 4)),
        pltpu.SemaphoreType.DMA((3, cfg.dp)),
        pltpu.SemaphoreType.DMA((3, cfg.dp)),
        pltpu.SemaphoreType.DMA((len(cfg.chunks), 2)),
        pltpu.SemaphoreType.DMA((len(cfg.chunks), 2)),
    ]
    for halves in [1] + [2] * (2 + 2 * len(cfg.chunks)):
        scratch += Gather.semaphores(cfg.dp, halves)
    scratch += LineSum.semaphores(cfg.pieces)
    return pl.pallas_call(
        functools.partial(forward_kernel, cfg),
        out_shape=outs,
        in_specs=[
            any_spec,
            any_spec,
            pl.BlockSpec(memory_space=pltpu.SMEM),
            pl.BlockSpec(memory_space=pltpu.VMEM),
        ]
        + [any_spec] * 9,
        out_specs=[any_spec] * len(outs),
        scratch_shapes=scratch,
        compiler_params=pltpu.CompilerParams(
            collective_id=1, has_side_effects=True, vmem_limit_bytes=VMEM_LIMIT
        ),
        name="attention_forward",
    )(x, dy, lengths, freq, gain_a, gain_m, wq, wk, wv, wo, wg, wu, wd)


def backward_kernel(cfg, *refs):
    (
        dn2_in, n2_in, dy_all_in, act_in, dgu_in, dy_in, hidden_in, terms_in,
        mixed_in, wo_in, qkv_in, q_in, k_in, v_in, normed_in, x_in, gains_in, lengths, freq,
        activations_out, grad_out, down_out, gu_out, qkv_out, out_out, gain_out,
        dy, hidden, dh, gains, n2_all, dy_all, act, dgu, gu_rows, down,
        part, inbox, result, terms, inbox_two, final,
        relay_down, relay_gu, relay_qkv, relay_out, qh, kh, vh,
        dmixed, dk, dv, dkv, dkv_in, cosine, sine, bias,
        gain_two, gain_one, gain_rows, gain_box, gain_line,
        load, store, own_sem, swap_send, swap_receive, dkv_send, dkv_receive,
        gain_send, gain_receive, last_send, last_receive, ready, *sems,
    ) = refs
    place = Place(cfg.dp, cfg.tensor)
    tokens, width = dy.shape
    heads, groups = cfg.heads, cfg.groups
    query_width, key_width, qkv_width = cfg.query_width, cfg.key_width, cfg.qkv_width
    units = act.shape[1]
    chunk = units // 4
    block, owners = cfg.block, cfg.dp
    mine = owners * block
    spare = list(sems[3 * 4 + 4 * 3 :])
    at = 0

    def carve(array, rows, columns, first_row=0, first_column=0):
        if array.shape[0] >= first_row + rows and array.shape[1] >= first_column + columns:
            return array.at[pl.ds(first_row, rows), pl.ds(first_column, columns)]
        return spare.pop(0)

    views = []
    for columns in (mine, mine, qkv_width, qkv_width, query_width):
        views.append(carve(dgu, 2 * tokens, columns, 0, at))
        at += columns
    normed_all, db_all, dqkv, qkv_rows, mixed_all = views
    x = carve(act, tokens, width)
    wo = carve(act, query_width, width, tokens)
    wqkv = carve(down, width, qkv_width)
    out_columns = carve(n2_all, query_width, mine)
    loads = []

    def fetch(source, target):
        copy = pltpu.make_async_copy(source, target, load.at[len(loads)])
        copy.start()
        loads.append(copy)
        return copy

    load_part = fetch(dn2_in, part)
    first = [
        fetch(dy_in, dy),
        fetch(hidden_in, hidden),
        fetch(gains_in, gains),
        fetch(act_in, act),
        fetch(dy_all_in, dy_all),
    ]
    second = [fetch(n2_in, n2_all), fetch(dgu_in, dgu)]
    third = [fetch(terms_in, terms), fetch(q_in, qh), fetch(k_in, kh), fetch(v_in, vh)]
    barrier = pltpu.get_barrier_semaphore()
    greeted = [place.core]
    for mask in range(1, cfg.dp):
        greeted += [(place.flipped(mask), place.c, place.t), (place.flipped(mask), 1 - place.c, place.t)]
    for step in range(1, cfg.tensor):
        greeted.append((place.p, place.c, lax.rem(place.t + step, cfg.tensor)))
    for device in greeted:
        pl.semaphore_signal(barrier, inc=1, device_id=device, device_id_type=MESH)
    gain_two[...] = jnp.zeros_like(gain_two)
    gain_one[...] = jnp.zeros_like(gain_one)
    pl.semaphore_wait(barrier, len(greeted))
    n_line, n_scatter = 4, 3
    scatters = []
    for i, (rows, relay, out, axis) in enumerate(
        [
            (down, relay_down, down_out, 1),
            (gu_rows, relay_gu, gu_out, 0),
            (out_columns, relay_out, out_out, 1),
            (qkv_rows, relay_qkv, qkv_out, 0),
        ]
    ):
        at = 3 * n_line + n_scatter * i
        scatters.append(Scatter(place, rows, relay, out, axis, sems[at : at + n_scatter]))
    s_down, s_gu, s_out, s_qkv = scatters

    def local_rows(i):
        rows = QROWS // cfg.pieces
        return pl.ds(pl.multiple_of(place.late * QROWS + i * rows, rows), rows)

    def norm_back(source, total, gain, gain_sum):
        r = lax.rsqrt(jnp.sum(source * source, -1, keepdims=True) * (1.0 / width) + EPSILON)
        scaled = source * r
        gain_sum[...] += jnp.sum((total * scaled).reshape(-1, 8, width), 0)
        e = total * gain
        mean = jnp.sum(e * scaled, -1, keepdims=True) * (1.0 / width)
        return r * (e - scaled * mean)

    def root_three(i, rows, total):
        back = norm_back(hidden[rows], total, gains[1:2, :].astype(F32), gain_two)
        grad = dy[local_rows(i)].astype(F32) + back
        dh[rows] = grad
        result[place.late, rows] = grad.astype(BF16)

    def root_two(i, rows, total):
        final[place.late, rows] = (hidden[rows] + total).astype(BF16)

    def root_one(i, rows, total):
        source = x[local_rows(i)].astype(F32)
        back = norm_back(source, total, gains[0:1, :].astype(F32), gain_one)
        result[place.late, rows] = (dh[rows] + back).astype(BF16)

    line_three = LineSum(place, part, inbox, result, sems[:n_line], cfg.pieces, root_three)
    line_two = LineSum(
        place, terms, inbox_two, final, sems[n_line : 2 * n_line], cfg.pieces, root_two
    )
    line_one = LineSum(
        place, part, inbox, result, sems[2 * n_line : 3 * n_line], cfg.pieces, root_one
    )
    load_part.wait()
    line_three.early_start()

    def grad_down(i):
        rows = aligned(i, units // 4)
        down[rows] = dot(act[:, rows], dy_all[...], TN).astype(BF16)

    def grad_gate_up(i):
        product = dot(n2_all[...], dgu[:, aligned(i, chunk)], TN).astype(BF16)

        @pl.when(i < 6)
        def _():
            gu_rows[:, aligned(lax.rem(i, 2) * 4 + lax.div(i, 2), chunk)] = product

        @pl.when(i >= 6)
        def _():
            gu_rows[:, aligned(i, chunk // 2)] = product[:, : chunk // 2]
            gu_rows[:, aligned(8 + i, chunk // 2)] = product[:, chunk // 2 :]

    def lines(n):
        line_three.round(n)
        line_two.round(n - cfg.behind)

    def between(fill, rounds, fills):
        def one(i, carry):
            lines(rounds + i)
            fill(fills + i)
            return carry

        lax.fori_loop(0, 4, one, 0)

    for copy in first:
        copy.wait()
    between(grad_down, 0, 0)
    s_down.start()
    tables(place, lengths, freq, cosine, sine, tokens)
    fill_bias(place, lengths, bias, tokens)
    for copy in second + third:
        copy.wait()
    between(grad_gate_up, 4, 0)
    between(grad_gate_up, 8, 4)
    line_two.early_start()
    pl.semaphore_signal(ready, inc=1, device_id=place.core, device_id_type=MESH)
    rest = [
        fetch(wo_in, wo),
        fetch(x_in, x),
        fetch(mixed_in, mixed_all.at[pl.ds(0, tokens)]),
    ]
    for phase in range(place.bits - 1, 0, -1):
        s_down.pass_on(phase)
    s_gu.start()
    lines(12)
    pl.semaphore_wait(ready, 1)
    swaps, owns, db_swaps, db_owns = [], [], [], []

    def swap(source, target, k, q, kept):
        copy = remote(source, target, swap_send.at[k, q], swap_receive.at[k, q], place.core)
        copy.start()
        kept.append(copy)

    def own(source, target, k, q, kept):
        copy = pltpu.make_async_copy(source, target, own_sem.at[k, q])
        copy.start()
        kept.append(copy)

    def shares(q):
        return pl.ds(q * block, block), aligned(2 * q + 1 - place.c, block), aligned(2 * q + place.c, block)

    for q in range(owners):
        columns, theirs, ours = shares(q)
        swap(normed_in.at[:, theirs], normed_all.at[pl.ds(tokens, tokens), columns], 0, q, swaps)
        own(normed_in.at[:, ours], normed_all.at[pl.ds(0, tokens), columns], 0, q, owns)
    swap(mixed_in, mixed_all.at[pl.ds(tokens, tokens)], 3, 0, swaps)
    lines(13)
    lines(14)
    db = result
    for b in range(2):
        for q in range(owners):
            columns, theirs, ours = shares(q)
            target = pl.ds(tokens + b * QROWS, QROWS)
            swap(db.at[b, :, theirs], db_all.at[target, columns], 1 + b, q, db_swaps)
            target = pl.ds(b * QROWS, QROWS)
            own(db.at[b, :, ours], db_all.at[target, columns], 1 + b, q, db_owns)
    for copy in rest:
        copy.wait()

    def back_out(b, carry):
        product = dot(db[b], wo[...], NT)
        rows = aligned(b, QROWS)
        for h in range(heads):
            dmixed[h, rows] = product[:, h * HD : (h + 1) * HD].astype(BF16)
        return carry

    lax.fori_loop(0, 2, back_out, 0)
    dk[...] = jnp.zeros_like(dk)
    dv[...] = jnp.zeros_like(dv)

    def attend_back(b, rounds):
        rows = aligned(b, QROWS)
        window = pl.ds(pl.multiple_of(place.c * b * QROWS, QROWS), bias.shape[1])

        def pair(j, carry):
            outs = []
            for h in range(2):
                head = 2 * j + h
                g = lax.div(head, heads // groups)
                key, value = kh[g, window], vh[g, window]
                query, grad = qh[head, rows], dmixed[head, rows]
                weights = softmax_of(key, query, bias[b])
                dprobs = dot(value, grad, NT)
                delta = jnp.sum(weights * dprobs, 0, keepdims=True)
                dscores = (weights * (dprobs - delta)).astype(BF16)
                dv[g, window] += dot(weights.astype(BF16), grad)
                dk[g, window] += dot(dscores, query)
                outs.append(dot(key, dscores, TN))
            z = jnp.concatenate(outs, 0).T * HD**-0.5
            z = z * cosine[rows] - turned(z) * sine[rows]
            dqkv[rows, aligned(j, 128)] = z.astype(BF16)
            line_two.round(rounds + j)
            return carry

        lax.fori_loop(0, heads // 2, pair, 0)

    done = line_three.rounds - cfg.behind
    attend_back(place.early, done)
    for copy in db_owns + owns:
        copy.wait()
    for copy in db_swaps + swaps:
        copy.wait_recv()
        copy.wait_send()
    s_down.finish()
    load_qkv = fetch(qkv_in, wqkv)
    out_columns[...] = dot(mixed_all[...], db_all[...], TN).astype(BF16)
    s_out.start()
    attend_back(place.late, done + heads // 2)
    done = done + heads
    stores = []

    def keep(source, target):
        copy = pltpu.make_async_copy(source, target, store.at[len(stores)])
        copy.start()
        stores.append(copy)

    pass_back = remote(dkv, dkv_in, dkv_send.at[0], dkv_receive.at[0], place.core)

    def packed(rows):
        return jnp.concatenate(
            [dk[g, rows] for g in range(groups)] + [dv[g, rows] for g in range(groups)], -1
        )

    @pl.when(place.c == 1)
    def _():
        dkv[...] = packed(pl.ds(0, tokens))
        pass_back.start()

    own_rows = aligned(place.c, tokens)
    z = packed(own_rows)

    @pl.when(place.c == 0)
    def _():
        pass_back.wait_recv()
        dkv[...] = z + dkv_in[...]

    @pl.when(place.c == 1)
    def _():
        pass_back.wait_send()
        dkv[...] = z

    dkeys = dkv[:, :key_width]
    if key_width % 128 == 0:
        wide_by = key_width // 128
        table_c = jnp.concatenate([cosine[...]] * wide_by, -1)
        table_s = jnp.concatenate([sine[...]] * wide_by, -1)
    else:
        table_c, table_s = cosine[:, :key_width], sine[:, :key_width]
    dkeys = dkeys * table_c - turned(dkeys) * table_s
    dqkv[:tokens, query_width : query_width + key_width] = dkeys.astype(BF16)
    dqkv[:tokens, query_width + key_width :] = dkv[:, key_width:].astype(BF16)
    late_swaps = []
    swap(dqkv.at[pl.ds(0, tokens)], dqkv.at[pl.ds(tokens, tokens)], 3, 1, late_swaps)
    load_qkv.wait()
    columns_at = width // 4

    def back_through(b):
        def one(i, carry):
            rows, columns = aligned(b, QROWS), aligned(i, columns_at)
            part[b, :, columns] = dot(dqkv[rows], wqkv[columns], NT).astype(BF16)
            return carry

        lax.fori_loop(0, 4, one, 0)

    def run_lines(start, stop):
        def one(n, carry):
            line_one.round(n)
            line_two.round(done + n)
            return carry

        lax.fori_loop(start, stop, one, 0)

    line_three.drain()
    back_through(place.early)
    line_one.early_start()
    back_through(place.late)
    run_lines(0, 1)
    for copy in late_swaps:
        copy.wait_recv()
    qkv_rows[...] = dot(normed_all[...], dqkv[...], TN).astype(BF16)
    s_qkv.start()
    run_lines(1, 4)
    agenda = []
    for phase in range(place.bits - 1, 0, -1):
        for s in (s_gu, s_out, s_qkv):
            agenda.append(functools.partial(s.pass_on, phase))
    last_sum = cfg.pieces + line_one.lags[1]
    marks = [4 + (last_sum - 4) * (k + 1) // (len(agenda) + 1) for k in range(len(agenda))]
    at = 4
    for mark, item in zip(marks, agenda):
        run_lines(at, mark)
        item()
        at = mark
    run_lines(at, last_sum)

    ends = (0, cfg.tensor - 1)
    mine = place.p * 2 + place.c

    def gain_copy(mask, core):
        index = place.flipped(mask) * 2 + core
        return remote(
            gain_rows.at[:, aligned(index, block)],
            gain_box.at[mine],
            gain_send.at[mask, lax.rem(core + place.c, 2)],
            gain_receive.at[mask, lax.rem(core + place.c, 2)],
            (place.flipped(mask), core, place.t),
        )

    others = [(mask, core) for mask in range(cfg.dp) for core in range(2)]

    @pl.when(place.at_end)
    def _():
        gain_rows[0:1, :] = jnp.sum(gain_one[...], 0, keepdims=True)
        gain_rows[1:2, :] = jnp.sum(gain_two[...], 0, keepdims=True)
        gain_rows[2:, :] = jnp.zeros((6, width), F32)
        for mask in range(cfg.dp):
            for apart in range(2):
                if mask or apart:
                    core = place.c if apart == 0 else 1 - place.c
                    gain_copy(mask, core).start()
        gain_box[mine] = gain_rows[:, aligned(mine, block)]

    run_lines(last_sum, line_one.rounds - 2)

    def line_copy(step, end):
        return remote(
            gain_line.at[end],
            gain_line.at[end],
            last_send.at[step],
            last_receive.at[end],
            (place.p, place.c, lax.rem(place.t + step, cfg.tensor)),
        )

    for end, at_t in enumerate(ends):

        @pl.when(place.t == at_t)
        def _(end=end):
            for mask in range(cfg.dp):
                for apart in range(2):
                    if mask or apart:
                        core = place.c if apart == 0 else 1 - place.c
                        gain_copy(mask, core).wait_recv()
            gain_line[end] = jnp.sum(gain_box[...], 0)
            for step in range(1, cfg.tensor):
                line_copy(step, end).start()

    run_lines(line_one.rounds - 2, line_one.rounds)
    keep(result, grad_out)
    line_two.run(done + line_one.rounds, line_two.rounds)
    keep(final, activations_out)
    for end, at_t in enumerate(ends):

        @pl.when(place.t != at_t)
        def _(end=end):
            line_copy(1, end).wait_recv()

    gain_one[:, :block] = gain_line[0] + gain_line[1]
    keep(gain_one.at[:, pl.ds(0, block)], gain_out)
    for s in scatters[1:]:
        s.finish()

    @pl.when(place.at_end)
    def _():
        for mask in range(cfg.dp):
            for apart in range(2):
                if mask or apart:
                    core = place.c if apart == 0 else 1 - place.c
                    gain_copy(mask, core).wait_send()
        for step in range(1, cfg.tensor):
            line_copy(step, 0).wait_send()

    for copy in late_swaps:
        copy.wait_send()
    line_two.drain()
    line_one.drain()
    for copy in stores:
        copy.wait()


def backward_call(cfg, *operands):
    tokens, width, units = cfg.tokens, cfg.width, cfg.hidden_units
    any_spec = pl.BlockSpec(memory_space=pl.ANY)
    shape = jax.ShapeDtypeStruct
    bits = cfg.dp.bit_length() - 1
    mine = cfg.dp * cfg.block
    heads, groups, qkv_width = cfg.heads, cfg.groups, cfg.qkv_width
    outs = [
        shape((2, QROWS, width), BF16),
        shape((2, QROWS, width), BF16),
        shape((1 + bits, units, cfg.block), BF16),
        shape((1 + bits, cfg.block, 2 * units), BF16),
        shape((1 + bits, cfg.block, qkv_width), BF16),
        shape((1 + bits, cfg.query_width, cfg.block), BF16),
        shape((8, cfg.block), F32),
    ]
    halves = (2, QROWS, width)
    scratch = [
        pltpu.VMEM((tokens, width), BF16),
        pltpu.VMEM((QROWS, width), F32),
        pltpu.VMEM((QROWS, width), F32),
        pltpu.VMEM((16, width), BF16),
        pltpu.VMEM((2 * tokens, mine), BF16),
        pltpu.VMEM((2 * tokens, mine), BF16),
        pltpu.VMEM((2 * tokens, units), BF16),
        pltpu.VMEM((2 * tokens, 2 * units), BF16),
        pltpu.VMEM((mine, 2 * units), BF16),
        pltpu.VMEM((units, mine), BF16),
    ]
    scratch += [pltpu.VMEM(halves, BF16)] * 6
    scratch += [
        pltpu.VMEM(Scatter.inbox_shape(cfg.dp, units, cfg.block), BF16),
        pltpu.VMEM(Scatter.inbox_shape(cfg.dp, cfg.block, 2 * units), BF16),
        pltpu.VMEM(Scatter.inbox_shape(cfg.dp, cfg.block, qkv_width), BF16),
        pltpu.VMEM(Scatter.inbox_shape(cfg.dp, cfg.query_width, cfg.block), BF16),
        pltpu.VMEM((heads, tokens, HD), BF16),
        pltpu.VMEM((groups, 2 * tokens, HD), BF16),
        pltpu.VMEM((groups, 2 * tokens, HD), BF16),
        pltpu.VMEM((heads, tokens, HD), BF16),
        pltpu.VMEM((groups, 2 * tokens, HD), F32),
        pltpu.VMEM((groups, 2 * tokens, HD), F32),
        pltpu.VMEM((tokens, 2 * cfg.key_width), F32),
        pltpu.VMEM((tokens, 2 * cfg.key_width), F32),
        pltpu.VMEM((tokens, 128), F32),
        pltpu.VMEM((tokens, 128), F32),
        pltpu.VMEM((2, cfg.window, QROWS), F32),
        pltpu.VMEM((8, width), F32),
        pltpu.VMEM((8, width), F32),
        pltpu.VMEM((8, width), F32),
        pltpu.VMEM((2 * cfg.dp, 8, cfg.block), F32),
        pltpu.VMEM((2, 8, cfg.block), F32),
        pltpu.SemaphoreType.DMA((16,)),
        pltpu.SemaphoreType.DMA((3,)),
        pltpu.SemaphoreType.DMA((3, cfg.dp)),
        pltpu.SemaphoreType.DMA((4, max(cfg.dp, 2))),
        pltpu.SemaphoreType.DMA((4, max(cfg.dp, 2))),
        pltpu.SemaphoreType.DMA((1,)),
        pltpu.SemaphoreType.DMA((1,)),
        pltpu.SemaphoreType.DMA((cfg.dp, 2)),
        pltpu.SemaphoreType.DMA((cfg.dp, 2)),
        pltpu.SemaphoreType.DMA((cfg.tensor,)),
        pltpu.SemaphoreType.DMA((2,)),
        pltpu.SemaphoreType.REGULAR,
    ]
    scratch += LineSum.semaphores(cfg.pieces) * 3
    scratch += Scatter.semaphores(cfg.dp) * 4
    at = 0
    for columns in (mine, mine, qkv_width, qkv_width, cfg.query_width):
        if 2 * units < at + columns:
            scratch.append(pltpu.VMEM((2 * tokens, columns), BF16))
        at += columns
    if units < width:
        scratch.append(pltpu.VMEM((tokens, width), BF16))
    if units < width or 2 * tokens < tokens + cfg.query_width:
        scratch.append(pltpu.VMEM((cfg.query_width, width), BF16))
    if units < width or mine < qkv_width:
        scratch.append(pltpu.VMEM((width, qkv_width), BF16))
    if 2 * tokens < cfg.query_width:
        scratch.append(pltpu.VMEM((cfg.query_width, mine), BF16))
    in_specs = [any_spec] * 17 + [
        pl.BlockSpec(memory_space=pltpu.SMEM),
        pl.BlockSpec(memory_space=pltpu.VMEM),
    ]
    return pl.pallas_call(
        functools.partial(backward_kernel, cfg),
        out_shape=outs,
        in_specs=in_specs,
        out_specs=[any_spec] * len(outs),
        scratch_shapes=scratch,
        compiler_params=pltpu.CompilerParams(
            collective_id=3, has_side_effects=True, vmem_limit_bytes=VMEM_LIMIT
        ),
        name="backward",
    )(*operands)


def solution(mesh):
    dp, tensor = mesh.shape["dp"], mesh.shape["tensor"]

    def shards(
        inputs, cotangent, doc_lengths, gain_attn, w_query, w_key, w_value, w_out, gain_mlp,
        w_gate, w_up, w_down,
    ):
        tokens, width = inputs.shape
        cfg = Config(
            dp,
            tensor,
            tokens,
            width,
            w_query.shape[1] // HD,
            w_key.shape[1] // HD,
            w_gate.shape[1],
        )
        freq = jnp.asarray(np.tile(frequencies(), (8, 4)), F32)
        gains = (gain_attn.reshape(1, -1), gain_mlp.reshape(1, -1))
        (
            _, _, wqkv, wo, gains_full, normed, q, k, v, mixed, hidden,
            n2_all, dy_all, act_all, dgu_all, dn2, terms,
        ) = forward_call(
            cfg, inputs, cotangent, doc_lengths, freq, *gains,
            w_query, w_key, w_value, w_out, w_gate, w_up, w_down,
        )
        (
            activations, input_grad, down_terms, gu_terms, qkv_terms, out_terms, gain_sums,
        ) = backward_call(
            cfg, dn2, n2_all, dy_all, act_all, dgu_all, cotangent, hidden, terms,
            mixed, wo, wqkv, q, k, v, normed, inputs, gains_full, doc_lengths, freq,
        )

        def total(pieces):
            return jnp.sum(pieces.astype(F32), 0)

        qkv_grad = total(qkv_terms)
        units = cfg.hidden_units
        query_width, key_width = cfg.query_width, cfg.key_width
        return (
            activations.reshape(tokens, width),
            input_grad.reshape(tokens, width).astype(F32),
            gain_sums[0],
            qkv_grad[:, :query_width],
            qkv_grad[:, query_width : query_width + key_width],
            qkv_grad[:, query_width + key_width :],
            total(out_terms),
            gain_sums[1],
            total(gu_terms[:, :, :units]),
            total(gu_terms[:, :, units:]),
            total(down_terms),
        )

    rows, columns, gain = P(("dp", "context"), "tensor"), P("tensor", ("dp", "context")), P(("dp", "context"))
    tokens = P(("dp", "context"), None)
    return jax.shard_map(
        shards,
        mesh=mesh,
        in_specs=(tokens, tokens, P("dp", None), gain, rows, rows, rows, columns, gain, rows, rows, columns),
        out_specs=(tokens, tokens, gain, rows, rows, rows, columns, gain, rows, rows, columns),
        check_vma=False,
    )
```

```python
import functools
import math

import jax
import jax.numpy as jnp
import numpy as np
from jax import lax
from jax.experimental import pallas as pl
from jax.experimental.pallas import tpu as pltpu
from jax.sharding import PartitionSpec as P

HD = 64
WINDOW = 512
QROWS = 256
EPSILON = 1e-05
NEGATIVE = -1e30
MESH = pl.DeviceIdType.MESH
F32 = jnp.float32
BF16 = jnp.bfloat16
NN = (((1,), (0,)), ((), ()))
NT = (((1,), (1,)), ((), ()))
TN = (((0,), (0,)), ((), ()))
VMEM_LIMIT = 127 * 2**19


def dot(left, right, dims=NN):
    return lax.dot_general(left, right, dims, preferred_element_type=F32)


def frequencies():
    exponent = np.arange(0, HD, 2).astype(np.float32) / np.float32(HD)
    initial = np.float32(1.0) / np.float32(500000.0) ** exponent
    wavelength = np.float32(2.0 * math.pi) / initial
    smoothing = (np.float32(8192.0) / wavelength - np.float32(1.0)) / np.float32(3.0)
    low = initial / np.float32(32.0)
    blended = (np.float32(1.0) - smoothing) * low + smoothing * initial
    return np.where(wavelength < 2048.0, initial, np.where(wavelength > 8192.0, low, blended))


def aligned(index, size):
    return pl.ds(pl.multiple_of(index * size, size), size)


class Place:
    def __init__(self, dp, tensor):
        self.dp, self.tensor = dp, tensor
        self.bits = dp.bit_length() - 1
        self.p = lax.axis_index("dp")
        self.c = lax.axis_index("context")
        self.t = lax.axis_index("tensor")
        self.core = (self.p, 1 - self.c, self.t)
        self.low = lax.rem(lax.div(self.t * 2, tensor), 2)
        self.early = 1 - self.low
        self.late = self.low
        step = 1 - 2 * self.low
        self.inward = (self.p, self.c, self.t + step)
        self.outward = (self.p, self.c, self.t - step)
        edge = self.low * (tensor - 1 - self.t) + (1 - self.low) * self.t
        self.depth = edge
        self.at_end = edge == 0

    def flipped(self, mask):
        position = self.p
        for b in range(self.bits):
            if mask >> b & 1:
                bit = lax.rem(lax.div(self.p, 2**b), 2)
                position = position + (1 - 2 * bit) * 2**b
        return position

    def across(self, b):
        return (self.flipped(1 << b), self.c, self.t)

    def greet(self):
        barrier = pltpu.get_barrier_semaphore()
        for device in [self.core] + [self.across(b) for b in range(self.bits)] + [self.inward]:
            pl.semaphore_signal(barrier, inc=1, device_id=device, device_id_type=MESH)

        @pl.when(jnp.logical_not(self.at_end))
        def _():
            pl.semaphore_signal(barrier, inc=1, device_id=self.outward, device_id_type=MESH)

    def meet(self):
        barrier = pltpu.get_barrier_semaphore()

        @pl.when(self.at_end)
        def _():
            pl.semaphore_wait(barrier, 2 + self.bits)

        @pl.when(jnp.logical_not(self.at_end))
        def _():
            pl.semaphore_wait(barrier, 3 + self.bits)


def remote(source, target, send, receive, device):
    return pltpu.make_async_remote_copy(
        src_ref=source,
        dst_ref=target,
        send_sem=send,
        recv_sem=receive,
        device_id=device,
        device_id_type=MESH,
    )


def orders_of(bits, halves):
    forward = tuple(range(bits))
    return (forward, forward[::-1]) if halves == 2 else (forward,)


def phase_masks(order, phase):
    masks = [0]
    for b in order[:phase]:
        masks = masks + [m | 1 << b for m in masks]
    return [m | 1 << order[phase] for m in masks]


class Gather:
    def __init__(self, place, shard, full, axis, sems, halves=2):
        self.place, self.shard, self.full, self.axis = place, shard, full, axis
        self.halves = halves
        self.send, self.receive, self.core_send, self.core_receive, self.local = sems
        self.orders = orders_of(place.bits, halves)
        self.rows = shard.shape[0] // halves
        self.sends = []

    @staticmethod
    def semaphores(dp, halves=2):
        bits = dp.bit_length() - 1
        return [
            pltpu.SemaphoreType.DMA((halves, dp, max(bits, 1))),
            pltpu.SemaphoreType.DMA((halves, dp)),
            pltpu.SemaphoreType.DMA((halves, dp)),
            pltpu.SemaphoreType.DMA((halves, dp)),
            pltpu.SemaphoreType.DMA((1,)),
        ]

    def part(self, half):
        return self.shard.at[pl.ds(half * self.rows, self.rows)]

    def slot(self, position, core, half):
        index = position * 2 + core
        if self.axis == 0:
            rows = self.shard.shape[0]
            first = pl.multiple_of(index * rows + half * self.rows, self.rows)
            return self.full.at[pl.ds(first, self.rows)]
        return self.full.at[
            pl.ds(half * self.rows, self.rows), aligned(index, self.shard.shape[1])
        ]

    def _forward(self, half, mask, source):
        place = self.place
        order = self.orders[half]
        last = max([order.index(b) for b in order if mask >> b & 1], default=-1)
        target = self.slot(place.flipped(mask), place.c, half)
        for j in range(last + 1, place.bits):
            copy = remote(
                source,
                target,
                self.send.at[half, mask, j],
                self.receive.at[half, mask | 1 << order[j]],
                place.across(order[j]),
            )
            copy.start()
            self.sends.append(copy)
        copy = remote(
            source,
            target,
            self.core_send.at[half, mask],
            self.core_receive.at[half, mask],
            place.core,
        )
        copy.start()
        self.sends.append(copy)

    def start(self):
        place = self.place
        for half in range(self.halves):
            self._forward(half, 0, self.part(half))
        index = place.p * 2 + place.c
        if self.axis == 0:
            own = self.full.at[aligned(index, self.shard.shape[0])]
        else:
            own = self.full.at[:, aligned(index, self.shard.shape[1])]
        self.own = pltpu.make_async_copy(self.shard, own, self.local.at[0])
        self.own.start()

    def pass_on(self, phase):
        place = self.place
        for half in range(self.halves):
            for mask in phase_masks(self.orders[half], phase):
                source = self.slot(place.flipped(mask), place.c, half)
                remote(
                    source,
                    source,
                    self.send.at[half, mask, 0],
                    self.receive.at[half, mask],
                    place.core,
                ).wait_recv()
                self._forward(half, mask, source)

    def finish(self):
        place = self.place
        self.own.wait()
        for half in range(self.halves):
            for mask in range(place.dp):
                target = self.slot(place.flipped(mask), 1 - place.c, half)
                remote(
                    target,
                    target,
                    self.core_send.at[half, mask],
                    self.core_receive.at[half, mask],
                    place.core,
                ).wait_recv()

    def drain(self):
        for copy in self.sends:
            copy.wait_send()
        self.sends = []


class LineSum:
    lags = (0, 3, 5, 7)

    def __init__(self, place, part, inbox, result, sems, pieces, root):
        self.place, self.part, self.inbox, self.result = place, part, inbox, result
        self.sum_send, self.sum_receive, self.back_send, self.back_receive = sems
        self.pieces = pieces
        self.rows = part.shape[1] // pieces
        self.rounds = pieces + self.lags[-1]
        self.root = root

    @staticmethod
    def semaphores(pieces):
        return [pltpu.SemaphoreType.DMA((2, pieces))] * 4

    def _copy(self, kind, flow, i, device):
        rows = aligned(i, self.rows)
        if kind == "sum":
            return remote(
                self.part.at[flow, rows],
                self.inbox.at[flow, rows],
                self.sum_send.at[flow, i],
                self.sum_receive.at[flow, i],
                device,
            )
        return remote(
            self.result.at[flow, rows],
            self.result.at[flow, rows],
            self.back_send.at[flow, i],
            self.back_receive.at[flow, i],
            device,
        )

    def _add(self, flow, i):
        rows = aligned(i, self.rows)
        total = self.part[flow, rows].astype(F32) + self.inbox[flow, rows].astype(F32)
        self.part[flow, rows] = total.astype(BF16)

    def early_start(self):
        @pl.when(self.place.at_end)
        def _():
            def one(i, carry):
                self._copy("sum", self.place.early, i, self.place.inward).start()
                return carry

            lax.fori_loop(0, self.pieces, one, 0)

    def early_sum(self, i):
        place = self.place

        @pl.when(jnp.logical_not(place.at_end))
        def _():
            copy = self._copy("sum", place.early, i, place.inward)
            copy.wait_recv()
            self._add(place.early, i)
            copy.start()

    def late_sum(self, i):
        place = self.place
        copy = self._copy("sum", place.late, i, place.outward)
        copy.wait_recv()

        @pl.when(jnp.logical_not(place.at_end))
        def _():
            self._add(place.late, i)
            copy.start()

        @pl.when(place.at_end)
        def _():
            rows = aligned(i, self.rows)
            total = self.part[place.late, rows].astype(F32)
            total = total + self.inbox[place.late, rows].astype(F32)
            self.root(i, rows, total)
            self._copy("back", place.late, i, place.inward).start()

    def late_back(self, i):
        place = self.place

        @pl.when(jnp.logical_not(place.at_end))
        def _():
            copy = self._copy("back", place.late, i, place.inward)
            copy.wait_recv()
            copy.start()

    def early_back(self, i):
        place = self.place
        copy = self._copy("back", place.early, i, place.outward)
        copy.wait_recv()

        @pl.when(jnp.logical_not(place.at_end))
        def _():
            copy.start()

    def round(self, n):
        for lag, kind in zip(self.lags, ("early_sum", "late_sum", "late_back", "early_back")):
            i = n - lag
            if isinstance(i, int):
                if 0 <= i < self.pieces:
                    getattr(self, kind)(i)
            else:

                @pl.when((i >= 0) & (i < self.pieces))
                def _(kind=kind, i=i):
                    getattr(self, kind)(i)

    def run(self, first, last):
        def one(n, carry):
            self.round(n)
            return carry

        lax.fori_loop(first, last, one, 0)

    def drain(self):
        place = self.place

        def one(i, carry):
            self._copy("sum", place.early, i, place.inward).wait_send()
            self._copy("back", place.late, i, place.inward).wait_send()

            @pl.when(jnp.logical_not(place.at_end))
            def _():
                self._copy("sum", place.late, i, place.outward).wait_send()
                self._copy("back", place.early, i, place.outward).wait_send()

            return carry

        lax.fori_loop(0, self.pieces, one, 0)


class Scatter:
    def __init__(self, place, part, inbox, out, axis, sems):
        self.place, self.part, self.inbox, self.out, self.axis = place, part, inbox, out, axis
        self.send, self.receive, self.local = sems
        self.orders = orders_of(place.bits, 2)
        self.rows = out.shape[1] // 2
        self.sends = []

    @staticmethod
    def semaphores(dp):
        return [
            pltpu.SemaphoreType.DMA((2, dp)),
            pltpu.SemaphoreType.DMA((2, dp)),
            pltpu.SemaphoreType.DMA((1,)),
        ]

    @staticmethod
    def inbox_shape(dp, rows, columns):
        slots = sum(2**phase - 1 for phase in range(1, dp.bit_length() - 1))
        return (2, max(slots, 1), rows // 2, columns)

    def slot(self, position, half):
        if self.axis == 0:
            rows = self.out.shape[1]
            first = pl.multiple_of(position * rows + half * self.rows, self.rows)
            return self.part.at[pl.ds(first, self.rows)]
        return self.part.at[
            pl.ds(half * self.rows, self.rows), aligned(position, self.out.shape[2])
        ]

    def landing(self, half, phase, mask):
        if mask == 0:
            return self.out.at[1 + phase, pl.ds(half * self.rows, self.rows)]
        return self.inbox.at[half, self.code(half, phase, mask)]

    def code(self, half, phase, mask):
        order = self.orders[half]
        number = 0
        for later in range(self.place.bits - 1, phase, -1):
            number += 2**later - 1
        inside = [m for m in range(1, self.place.dp) if all(b in order[:phase] for b in bits_of(m))]
        return number + inside.index(mask)

    def _copies(self, half, phase):
        order = self.orders[half]
        b = order[phase]
        for mask in phase_masks(order, phase):
            yield remote(
                self.slot(self.place.flipped(mask), half),
                self.landing(half, phase, mask & ~(1 << b)),
                self.send.at[half, mask],
                self.receive.at[half, mask],
                self.place.across(b),
            )

    def start(self):
        place = self.place
        index = place.p
        if self.axis == 0:
            own = self.part.at[aligned(index, self.out.shape[1])]
        else:
            own = self.part.at[:, aligned(index, self.out.shape[2])]
        self.own = pltpu.make_async_copy(own, self.out.at[0], self.local.at[0])
        self.own.start()
        if place.bits:
            self._send(place.bits - 1)

    def _send(self, phase):
        for half in range(2):
            for copy in self._copies(half, phase):
                copy.start()
                self.sends.append(copy)

    def pass_on(self, phase):
        for half in range(2):
            order = self.orders[half]
            for copy, mask in zip(self._copies(half, phase), phase_masks(order, phase)):
                rest = mask & ~(1 << order[phase])
                if rest:
                    copy.wait_recv()
                    target = self.slot(self.place.flipped(rest), half)
                    source = self.landing(half, phase, rest)
                    pieces = max(1, self.rows // 64)
                    size = self.rows // pieces

                    def add(i, carry, target=target, source=source, size=size):
                        rows = aligned(i, size)
                        total = target[rows].astype(F32) + source[rows].astype(F32)
                        target[rows] = total.astype(BF16)
                        return carry

                    lax.fori_loop(0, pieces, add, 0)
        self._send(phase - 1)

    def finish(self):
        self.own.wait()
        for phase in range(self.place.bits):
            for half in range(2):
                order = self.orders[half]
                for copy, mask in zip(self._copies(half, phase), phase_masks(order, phase)):
                    if not mask & ~(1 << order[phase]):
                        copy.wait_recv()
        for copy in self.sends:
            copy.wait_send()
        self.sends = []


def bits_of(mask):
    return [b for b in range(mask.bit_length()) if mask >> b & 1]


def turned(z):
    width = z.shape[-1]
    half = HD // 2
    if width == 2 * HD:
        lane = lax.broadcasted_iota(jnp.int32, z.shape, 1)
        return jnp.where(lax.rem(lane, HD) < half, pltpu.roll(z, width - half, 1), pltpu.roll(z, half, 1))
    pieces = []
    for h in range(width // HD):
        pieces += [z[:, h * HD + half : (h + 1) * HD], z[:, h * HD : h * HD + half]]
    return jnp.concatenate(pieces, -1)


def document_starts(lengths, rows):
    starts = jnp.zeros(rows.shape, jnp.int32)
    end = lengths[0, 0]
    for k in range(lengths.shape[1]):
        starts = jnp.where(rows >= end, end, starts)
        if k + 1 < lengths.shape[1]:
            end = end + lengths[0, k + 1]
    return starts


def tables(place, lengths, freq, cosine, sine, tokens):
    rows = lax.broadcasted_iota(jnp.int32, (tokens, 128), 0) + place.c * tokens
    angle = (rows - document_starts(lengths, rows)).astype(F32) * freq[0:1, :]
    lane = lax.broadcasted_iota(jnp.int32, (tokens, 128), 1)
    cosine[...] = jnp.cos(angle)
    turned_sine = jnp.sin(angle)
    sine[...] = jnp.where(lax.rem(lane, HD) < HD // 2, -turned_sine, turned_sine)


def fill_bias(place, lengths, bias, tokens):
    keys = bias.shape[1]
    for b in range(tokens // QROWS):
        shape = (keys, QROWS)
        query = lax.broadcasted_iota(jnp.int32, shape, 1) + (place.c * tokens + b * QROWS)
        key = lax.broadcasted_iota(jnp.int32, shape, 0) + place.c * b * QROWS
        row = lax.broadcasted_iota(jnp.int32, (8, QROWS), 1) + (place.c * tokens + b * QROWS)
        starts = document_starts(lengths, row)[0:1, :]
        bias[b] = jnp.where((key >= starts) & (key <= query), 0.0, NEGATIVE)


def softmax_of(key, query, bias):
    scores = dot(key, query, NT) + bias
    highest = jnp.max(scores, 0, keepdims=True)
    raw = jnp.exp(scores - highest)
    return raw * (1.0 / jnp.sum(raw, 0, keepdims=True))


def forward_kernel(cfg, *refs):
    (
        x_in, dy_in, lengths, freq, gain_a_in, gain_m_in, wq_in, wk_in, wv_in, wo_in, wg_in, wu_in, wd_in,
        gu_full, wd_full,
        qkv_out, wo_out, gains_out, normed_out, q_out, k_out, v_out, mixed_out, hidden_out,
        n2_all, dy_all, act_all, dgu_all, dn2_out, terms_out,
        x, wq, wk, wv, wo, wraw, wd, gain_a, gain_m,
        sqkv, swo, sgu, swd, sgains,
        wqkv, wout, gains, normed, rscale, cosine, sine, bias,
        qh, kh, vh, kv, kv_in, mixed, part, inbox, result, hidden,
        gu_buffer, wd_buffer, act, dgu, dn2_sum, terms_sum, backs,
        load, store, kv_send, kv_receive, fill, spill, swap_send, swap_receive,
        chunk_send, chunk_receive, *sems,
    ) = refs
    place = Place(cfg.dp, cfg.tensor)
    tokens, width = x.shape
    heads, groups = cfg.heads, cfg.groups
    query_width, key_width = cfg.query_width, cfg.key_width
    units, chunks = cfg.hidden_units, len(cfg.chunks)
    block, owners = cfg.block, cfg.dp
    loads = []

    def fetch(source, target):
        copy = pltpu.make_async_copy(source, target, load.at[len(loads)])
        copy.start()
        loads.append(copy)
        return copy

    small = [
        fetch(source, target)
        for source, target in (
            (gain_a_in, gain_a), (gain_m_in, gain_m), (wq_in, wq), (wk_in, wk), (wv_in, wv)
        )
    ]
    load_x, load_wo = fetch(x_in, x), fetch(wo_in, wo)
    load_wg, load_wd = fetch(wg_in, wraw), fetch(wd_in, wd)
    place.greet()
    n_sems = 5
    gathers = []

    def gather(shard, full, axis, halves=2):
        at = n_sems * len(gathers)
        gathers.append(Gather(place, shard, full, axis, sems[at : at + n_sems], halves))
        return gathers[-1]

    g_gains = gather(sgains, gains, 1, 1)
    g_qkv = gather(sqkv, wqkv, 0)
    g_wo = gather(swo, wout, 1)
    g_gu, g_wd = [], []
    for start, count in cfg.chunks:
        columns = pl.ds(2 * start, 2 * count)
        g_gu.append(gather(sgu.at[:, columns], gu_full.at[:, columns], 0))
        rows = pl.ds(start, count)
        g_wd.append(gather(swd.at[rows], wd_full.at[rows], 1))
    line_sems = sems[n_sems * len(gathers) :]
    for copy in small:
        copy.wait()
    sgains[...] = jnp.zeros_like(sgains)
    sgains[0:1] = gain_a[...].astype(BF16)
    sgains[1:2] = gain_m[...].astype(BF16)
    sqkv[:, :query_width] = wq[...].astype(BF16)
    sqkv[:, query_width : query_width + key_width] = wk[...].astype(BF16)
    sqkv[:, query_width + key_width :] = wv[...].astype(BF16)
    place.meet()
    g_gains.start()
    g_qkv.start()
    load_wo.wait()
    swo[...] = wo[...].astype(BF16)

    def stage(second):
        for start, count in cfg.chunks:
            first = 2 * start + second * count
            sgu[:, first : first + count] = wraw[:, start : start + count].astype(BF16)

    load_wg.wait()
    stage(0)
    load_wu = fetch(wu_in, wraw)
    for phase in range(place.bits):
        g_gains.pass_on(phase)
        g_qkv.pass_on(phase)
        if phase == 0:
            g_wo.start()
            load_x.wait()
            rows_at = 64

            def scale(i, carry):
                rows = aligned(i, rows_at)
                wide = x[rows].astype(F32)
                mean = jnp.sum(wide * wide, -1, keepdims=True) * (1.0 / width)
                rscale[rows] = lax.rsqrt(mean + EPSILON)
                return carry

            lax.fori_loop(0, tokens // rows_at, scale, 0)
            tables(place, lengths, freq, cosine, sine, tokens)
            fill_bias(place, lengths, bias, tokens)
            load_wu.wait()
            stage(1)
            load_wd.wait()
            for start, count in cfg.chunks:
                rows = pl.ds(start, count)
                swd[rows] = wd[rows].astype(BF16)
    g_gains.finish()

    def norm(i, carry):
        rows = aligned(i, 64)
        scaled = x[rows].astype(F32) * rscale[rows]
        normed[rows] = (scaled * gains[0:1, :].astype(F32)).astype(BF16)
        return carry

    lax.fori_loop(0, tokens // 64, norm, 0)
    stores = []

    def keep(source, target):
        copy = pltpu.make_async_copy(source, target, store.at[len(stores)])
        copy.start()
        stores.append(copy)
        return copy

    normed_kept = keep(normed, normed_out)
    keep(gains, gains_out)
    g_qkv.finish()
    keep(wqkv, qkv_out)

    def begin(i):
        g_gu[i].start()
        g_wd[i].start()

    def advance(i, phase):
        g_gu[i].pass_on(phase)
        g_wd[i].pass_on(phase)

    for b in range(tokens // QROWS):
        rows = pl.ds(b * QROWS, QROWS)
        product = dot(normed[rows], wqkv[...])
        if b == 0:
            if place.bits:
                g_wo.pass_on(0)
            begin(0)
            begin(1)
        table_c, table_s = cosine[rows], sine[rows]
        for column in range(query_width // 128):
            z = product[:, column * 128 : (column + 1) * 128]
            z = (z * table_c + turned(z) * table_s) * HD**-0.5
            for h in range(2):
                qh[2 * column + h, rows] = z[:, h * HD : (h + 1) * HD].astype(BF16)
        z = product[:, query_width : query_width + key_width]
        if key_width % 128 == 0:
            wide = key_width // 128
            table_c = jnp.concatenate([table_c] * wide, -1)
            table_s = jnp.concatenate([table_s] * wide, -1)
        else:
            table_c, table_s = table_c[:, :key_width], table_s[:, :key_width]
        z = z * table_c + turned(z) * table_s
        kv[rows, :key_width] = z.astype(BF16)
        kv[rows, key_width:] = product[:, query_width + key_width :].astype(BF16)
    pass_kv = remote(kv, kv_in, kv_send.at[0], kv_receive.at[0], place.core)

    @pl.when(place.c == 0)
    def _():
        pass_kv.start()
        for g in range(groups):
            kh[g, tokens:] = jnp.zeros((tokens, HD), BF16)
            vh[g, tokens:] = jnp.zeros((tokens, HD), BF16)

    own_rows = aligned(place.c, tokens)
    for g in range(groups):
        kh[g, own_rows] = kv[:, g * HD : (g + 1) * HD]
        vh[g, own_rows] = kv[:, key_width + g * HD : key_width + (g + 1) * HD]

    @pl.when(place.c == 1)
    def _():
        pass_kv.wait_recv()
        for g in range(groups):
            kh[g, :tokens] = kv_in[:, g * HD : (g + 1) * HD]
            vh[g, :tokens] = kv_in[:, key_width + g * HD : key_width + (g + 1) * HD]

    keep(qh, q_out)
    keep(kh, k_out)
    keep(vh, v_out)
    normed_kept.wait()
    dy = normed
    load_dy = fetch(dy_in, dy)

    def attend(b):
        rows = aligned(b, QROWS)
        window = pl.ds(pl.multiple_of(place.c * b * QROWS, QROWS), bias.shape[1])

        def pair(j, carry):
            outs = []
            for h in range(2):
                head = 2 * j + h
                g = lax.div(head, heads // groups)
                weights = softmax_of(kh[g, window], qh[head, rows], bias[b]).astype(BF16)
                outs.append(dot(vh[g, window], weights, TN))
            mixed[rows, aligned(j, 128)] = jnp.concatenate(outs, 0).T.astype(BF16)
            return carry

        lax.fori_loop(0, heads // 2, pair, 0)

    def project(b):
        rows = aligned(b, QROWS)
        part[b] = dot(mixed[rows], wout[...]).astype(BF16)

    def root(i, rows, total):
        local = pl.ds(pl.multiple_of(place.late * QROWS + i * line.rows, line.rows), line.rows)
        total = total + x[local].astype(F32)
        hidden[rows] = total
        r = lax.rsqrt(jnp.sum(total * total, -1, keepdims=True) * (1.0 / width) + EPSILON)
        result[place.late, rows] = (total * r * gains[1:2, :].astype(F32)).astype(BF16)

    line = LineSum(place, part, inbox, result, line_sems, cfg.pieces, root)
    attend(place.early)
    for phase in range(1, place.bits):
        g_wo.pass_on(phase)
    g_wo.finish()
    keep(wout, wo_out)
    project(place.early)
    line.early_start()
    attend(place.late)
    project(place.late)
    keep(mixed, mixed_out)

    swaps, owns = [], []

    def swap(source, target, k, q, target_rows, sub):
        columns = pl.ds(q * block, block)
        copy = remote(
            source.at[:, aligned(2 * q + 1 - place.c, block)],
            target.at[pl.ds(tokens + sub, target_rows), columns],
            swap_send.at[k, q],
            swap_receive.at[k, q],
            place.core,
        )
        copy.start()
        swaps.append(copy)
        copy = pltpu.make_async_copy(
            source.at[:, aligned(2 * q + place.c, block)],
            target.at[pl.ds(sub, target_rows), columns],
            fill.at[k, q],
        )
        copy.start()
        owns.append(copy)

    load_dy.wait()
    for q in range(owners):
        swap(dy, dy_all, 0, q, tokens, 0)

    def chunk_load(i):
        slot = i % 2
        start, count = cfg.chunks[i]
        return [
            pltpu.make_async_copy(
                gu_full.at[:, pl.ds(2 * start, 2 * count)],
                gu_buffer.at[slot, :, pl.ds(0, 2 * count)],
                spill.at[slot, 0],
            ),
            pltpu.make_async_copy(
                wd_full.at[pl.ds(start, count)],
                wd_buffer.at[slot, pl.ds(0, count)],
                spill.at[slot, 1],
            ),
        ]

    def take(i):
        g_gu[i].finish()
        g_wd[i].finish()
        for copy in chunk_load(i):
            copy.start()

    def from_output(i):
        for copy in chunk_load(i):
            copy.wait()
        return dot(dy[...], wd_buffer[i % 2, : cfg.chunks[i][1]], NT)

    def from_output_early(i):
        backs[i] = from_output(i)

    later = range(1, place.bits)
    agenda = []
    if place.bits:
        agenda.append((2, advance, 0, 0))
    agenda.append((2, begin, 2))
    if place.bits:
        agenda.append((cfg.marks[0], advance, 1, 0))
    agenda += [(cfg.marks[0], begin, 3), (cfg.marks[0], begin, 4)]
    agenda += [(cfg.marks[1], advance, 0, phase) for phase in later]
    agenda += [(cfg.marks[1], take, 0), (cfg.marks[2], from_output_early, 0)]
    agenda += [(cfg.marks[3], advance, 1, phase) for phase in later]
    agenda += [(cfg.marks[3], take, 1)]
    at = 0
    for mark, action, *rest in agenda:
        line.run(at, mark)
        action(*rest)
        at = mark
    line.run(at, line.rounds)
    if place.bits:
        advance(2, 0)
    for b in range(2):
        for q in range(owners):
            swap(result.at[b], n2_all, 1 + b, q, QROWS, b * QROWS)
    keep(hidden, hidden_out)

    def give(i):
        slot = i % 2
        start, count = cfg.chunks[i]
        copies = []
        for k, (source, target, first, wide) in enumerate(
            ((act, act_all, start, count), (dgu, dgu_all, 2 * start, 2 * count))
        ):
            source, columns = source.at[slot, :, pl.ds(0, wide)], pl.ds(first, wide)
            copies.append(
                pltpu.make_async_copy(
                    source, target.at[pl.ds(0, tokens), columns], spill.at[slot, 2 + k]
                )
            )
            copies.append(
                remote(
                    source,
                    target.at[pl.ds(tokens, tokens), columns],
                    chunk_send.at[i, k],
                    chunk_receive.at[i, k],
                    place.core,
                )
            )
        return copies

    tile = width // 4
    for i in range(chunks):
        slot = i % 2
        count = cfg.chunks[i][1]
        if i >= 2:
            own_act, sent_act, own_dgu, sent_dgu = give(i - 2)
            own_act.wait()
            own_dgu.wait()
            sent_act.wait_send()
            sent_dgu.wait_send()
        n2 = result[...].reshape(tokens, width)
        back = backs[0] if i == 0 else from_output(i)
        both = dot(n2, gu_buffer[slot, :, : 2 * count])
        gate, upward = both[:, :count], both[:, count:]
        sigmoid = 1.0 / (1.0 + jnp.exp(-gate))
        swish = gate * sigmoid
        act[slot, :, :count] = (swish * upward).astype(BF16)
        dgu[slot, :, :count] = (
            back * upward * sigmoid * (1.0 + gate * (1.0 - sigmoid))
        ).astype(BF16)
        dgu[slot, :, count : 2 * count] = (back * swish).astype(BF16)
        for copy in give(i):
            copy.start()

        def add(n, carry, i=i, slot=slot, count=count):
            columns = aligned(n, tile)
            more = dot(dgu[slot, :, : 2 * count], gu_buffer[slot, columns, : 2 * count], NT)
            terms = dot(act[slot, :, :count], wd_buffer[slot, :count, columns])
            if i:
                more = more + dn2_sum[:, columns]
                terms = terms + terms_sum[:, columns]
            if i + 1 < chunks:
                dn2_sum[:, columns] = more
                terms_sum[:, columns] = terms
            else:
                for b in range(2):
                    part[b, :, columns] = more[b * QROWS : (b + 1) * QROWS].astype(BF16)
                    inbox[b, :, columns] = terms[b * QROWS : (b + 1) * QROWS].astype(BF16)
            return carry

        if i + 1 == chunks:
            line.drain()
        lax.fori_loop(0, 4, add, 0)
        if i == 0 and place.bits:
            advance(3, 0)
        if i == 1 and place.bits:
            advance(4, 0)
        if 2 <= i + 1 < chunks:
            for phase in later:
                advance(i + 1, phase)
            take(i + 1)
    keep(part, dn2_out)
    keep(inbox, terms_out)
    for i in range(max(chunks - 2, 0), chunks):
        own_act, sent_act, own_dgu, sent_dgu = give(i)
        own_act.wait()
        own_dgu.wait()
        sent_act.wait_send()
        sent_dgu.wait_send()
    for i in range(chunks):
        own_act, sent_act, own_dgu, sent_dgu = give(i)
        sent_act.wait_recv()
        sent_dgu.wait_recv()
    for g in gathers:
        g.drain()
    for copy in owns:
        copy.wait()
    for copy in swaps:
        copy.wait_recv()
        copy.wait_send()

    @pl.when(place.c == 0)
    def _():
        pass_kv.wait_send()

    for copy in stores[1:]:
        copy.wait()


class Config:
    def __init__(self, dp, tensor, tokens, width, heads, groups, hidden_units):
        self.dp, self.tensor, self.tokens, self.width = dp, tensor, tokens, width
        self.heads, self.groups, self.hidden_units = heads, groups, hidden_units
        self.pieces = 8
        eighth = hidden_units // 8
        self.chunks = [(2 * n * eighth, 2 * eighth) for n in range(3)]
        self.chunks += [(6 * eighth, eighth), (7 * eighth, eighth)]
        self.behind = 12
        self.marks = (7, 10, 12, 13)
        self.query_width, self.key_width = heads * HD, groups * HD
        self.qkv_width = self.query_width + 2 * self.key_width
        self.blocks = dp * 2
        self.block = width // self.blocks
        self.window = WINDOW + QROWS


def forward_call(cfg, x, dy, lengths, freq, gain_a, gain_m, wq, wk, wv, wo, wg, wu, wd):
    tokens, width, units = cfg.tokens, cfg.width, cfg.hidden_units
    any_spec = pl.BlockSpec(memory_space=pl.ANY)
    shape = jax.ShapeDtypeStruct
    mine = cfg.dp * cfg.block
    chunk = max(count for _, count in cfg.chunks)
    outs = [
        shape((width, 2 * units), BF16),
        shape((units, width), BF16),
        shape((width, cfg.qkv_width), BF16),
        shape((cfg.query_width, width), BF16),
        shape((16, width), BF16),
        shape((tokens, width), BF16),
        shape((cfg.heads, tokens, HD), BF16),
        shape((cfg.groups, 2 * tokens, HD), BF16),
        shape((cfg.groups, 2 * tokens, HD), BF16),
        shape((tokens, cfg.query_width), BF16),
        shape((QROWS, width), F32),
        shape((2 * tokens, mine), BF16),
        shape((2 * tokens, mine), BF16),
        shape((2 * tokens, units), BF16),
        shape((2 * tokens, 2 * units), BF16),
        shape((2, QROWS, width), BF16),
        shape((2, QROWS, width), BF16),
    ]
    scratch = [pltpu.VMEM(x.shape, BF16)]
    scratch += [pltpu.VMEM(w.shape, F32) for w in (wq, wk, wv, wo, wg, wd, gain_a, gain_m)]
    scratch += [pltpu.VMEM((wq.shape[0], cfg.qkv_width), BF16)]
    scratch += [pltpu.VMEM(wo.shape, BF16)]
    scratch += [pltpu.VMEM((wg.shape[0], 2 * units), BF16)]
    scratch += [pltpu.VMEM(wd.shape, BF16)]
    scratch += [pltpu.VMEM((16, gain_a.shape[1]), BF16)]
    scratch += [
        pltpu.VMEM((width, cfg.qkv_width), BF16),
        pltpu.VMEM((cfg.query_width, width), BF16),
        pltpu.VMEM((16, width), BF16),
        pltpu.VMEM((tokens, width), BF16),
        pltpu.VMEM((tokens, 1), F32),
        pltpu.VMEM((tokens, 128), F32),
        pltpu.VMEM((tokens, 128), F32),
        pltpu.VMEM((2, cfg.window, QROWS), F32),
        pltpu.VMEM((cfg.heads, tokens, HD), BF16),
        pltpu.VMEM((cfg.groups, 2 * tokens, HD), BF16),
        pltpu.VMEM((cfg.groups, 2 * tokens, HD), BF16),
        pltpu.VMEM((tokens, 2 * cfg.key_width), BF16),
        pltpu.VMEM((tokens, 2 * cfg.key_width), BF16),
        pltpu.VMEM((tokens, cfg.query_width), BF16),
        pltpu.VMEM((2, QROWS, width), BF16),
        pltpu.VMEM((2, QROWS, width), BF16),
        pltpu.VMEM((2, QROWS, width), BF16),
        pltpu.VMEM((QROWS, width), F32),
        pltpu.VMEM((2, width, 2 * chunk), BF16),
        pltpu.VMEM((2, chunk, width), BF16),
        pltpu.VMEM((2, tokens, chunk), BF16),
        pltpu.VMEM((2, tokens, 2 * chunk), BF16),
        pltpu.VMEM((tokens, width), F32),
        pltpu.VMEM((tokens, width), F32),
        pltpu.VMEM((1, tokens, chunk), F32),
        pltpu.SemaphoreType.DMA((11,)),
        pltpu.SemaphoreType.DMA((14,)),
        pltpu.SemaphoreType.DMA((1,)),
        pltpu.SemaphoreType.DMA((1,)),
        pltpu.SemaphoreType.DMA((3, cfg.dp)),
        pltpu.SemaphoreType.DMA((2, 4)),
        pltpu.SemaphoreType.DMA((3, cfg.dp)),
        pltpu.SemaphoreType.DMA((3, cfg.dp)),
        pltpu.SemaphoreType.DMA((len(cfg.chunks), 2)),
        pltpu.SemaphoreType.DMA((len(cfg.chunks), 2)),
    ]
    for halves in [1] + [2] * (2 + 2 * len(cfg.chunks)):
        scratch += Gather.semaphores(cfg.dp, halves)
    scratch += LineSum.semaphores(cfg.pieces)
    return pl.pallas_call(
        functools.partial(forward_kernel, cfg),
        out_shape=outs,
        in_specs=[
            any_spec,
            any_spec,
            pl.BlockSpec(memory_space=pltpu.SMEM),
            pl.BlockSpec(memory_space=pltpu.VMEM),
        ]
        + [any_spec] * 9,
        out_specs=[any_spec] * len(outs),
        scratch_shapes=scratch,
        compiler_params=pltpu.CompilerParams(
            collective_id=1, has_side_effects=True, vmem_limit_bytes=VMEM_LIMIT
        ),
        name="attention_forward",
    )(x, dy, lengths, freq, gain_a, gain_m, wq, wk, wv, wo, wg, wu, wd)


def backward_kernel(cfg, *refs):
    (
        dn2_in, n2_in, dy_all_in, act_in, dgu_in, dy_in, hidden_in, terms_in,
        mixed_in, wo_in, qkv_in, q_in, k_in, v_in, normed_in, x_in, gains_in, lengths, freq,
        activations_out, grad_out, down_out, gu_out, qkv_out, out_out, gain_out,
        dy, hidden, dh, gains, n2_all, dy_all, act, dgu, gu_rows, down,
        part, inbox, result, terms, inbox_two, final,
        relay_down, relay_gu, relay_qkv, relay_out, qh, kh, vh,
        dmixed, dk, dv, dkv, dkv_in, cosine, sine, bias,
        gain_two, gain_one, gain_rows, gain_box, gain_line,
        load, store, own_sem, swap_send, swap_receive, dkv_send, dkv_receive,
        gain_send, gain_receive, last_send, last_receive, ready, *sems,
    ) = refs
    place = Place(cfg.dp, cfg.tensor)
    tokens, width = dy.shape
    heads, groups = cfg.heads, cfg.groups
    query_width, key_width, qkv_width = cfg.query_width, cfg.key_width, cfg.qkv_width
    units = act.shape[1]
    chunk = units // 4
    block, owners = cfg.block, cfg.dp
    mine = owners * block
    spare = list(sems[3 * 4 + 4 * 3 :])
    at = 0

    def carve(array, rows, columns, first_row=0, first_column=0):
        if array.shape[0] >= first_row + rows and array.shape[1] >= first_column + columns:
            return array.at[pl.ds(first_row, rows), pl.ds(first_column, columns)]
        return spare.pop(0)

    views = []
    for columns in (mine, mine, qkv_width, qkv_width, query_width):
        views.append(carve(dgu, 2 * tokens, columns, 0, at))
        at += columns
    normed_all, db_all, dqkv, qkv_rows, mixed_all = views
    x = carve(act, tokens, width)
    wo = carve(act, query_width, width, tokens)
    wqkv = carve(down, width, qkv_width)
    out_columns = carve(n2_all, query_width, mine)
    loads = []

    def fetch(source, target):
        copy = pltpu.make_async_copy(source, target, load.at[len(loads)])
        copy.start()
        loads.append(copy)
        return copy

    load_part = fetch(dn2_in, part)
    first = [
        fetch(dy_in, dy),
        fetch(hidden_in, hidden),
        fetch(gains_in, gains),
        fetch(act_in, act),
        fetch(dy_all_in, dy_all),
    ]
    second = [fetch(n2_in, n2_all), fetch(dgu_in, dgu)]
    third = [fetch(terms_in, terms), fetch(q_in, qh), fetch(k_in, kh), fetch(v_in, vh)]
    barrier = pltpu.get_barrier_semaphore()
    greeted = [place.core]
    for mask in range(1, cfg.dp):
        greeted += [(place.flipped(mask), place.c, place.t), (place.flipped(mask), 1 - place.c, place.t)]
    for step in range(1, cfg.tensor):
        greeted.append((place.p, place.c, lax.rem(place.t + step, cfg.tensor)))
    for device in greeted:
        pl.semaphore_signal(barrier, inc=1, device_id=device, device_id_type=MESH)
    gain_two[...] = jnp.zeros_like(gain_two)
    gain_one[...] = jnp.zeros_like(gain_one)
    pl.semaphore_wait(barrier, len(greeted))
    n_line, n_scatter = 4, 3
    scatters = []
    for i, (rows, relay, out, axis) in enumerate(
        [
            (down, relay_down, down_out, 1),
            (gu_rows, relay_gu, gu_out, 0),
            (out_columns, relay_out, out_out, 1),
            (qkv_rows, relay_qkv, qkv_out, 0),
        ]
    ):
        at = 3 * n_line + n_scatter * i
        scatters.append(Scatter(place, rows, relay, out, axis, sems[at : at + n_scatter]))
    s_down, s_gu, s_out, s_qkv = scatters

    def local_rows(i):
        rows = QROWS // cfg.pieces
        return pl.ds(pl.multiple_of(place.late * QROWS + i * rows, rows), rows)

    def norm_back(source, total, gain, gain_sum):
        r = lax.rsqrt(jnp.sum(source * source, -1, keepdims=True) * (1.0 / width) + EPSILON)
        scaled = source * r
        gain_sum[...] += jnp.sum((total * scaled).reshape(-1, 8, width), 0)
        e = total * gain
        mean = jnp.sum(e * scaled, -1, keepdims=True) * (1.0 / width)
        return r * (e - scaled * mean)

    def root_three(i, rows, total):
        back = norm_back(hidden[rows], total, gains[1:2, :].astype(F32), gain_two)
        grad = dy[local_rows(i)].astype(F32) + back
        dh[rows] = grad
        result[place.late, rows] = grad.astype(BF16)

    def root_two(i, rows, total):
        final[place.late, rows] = (hidden[rows] + total).astype(BF16)

    def root_one(i, rows, total):
        source = x[local_rows(i)].astype(F32)
        back = norm_back(source, total, gains[0:1, :].astype(F32), gain_one)
        result[place.late, rows] = (dh[rows] + back).astype(BF16)

    line_three = LineSum(place, part, inbox, result, sems[:n_line], cfg.pieces, root_three)
    line_two = LineSum(
        place, terms, inbox_two, final, sems[n_line : 2 * n_line], cfg.pieces, root_two
    )
    line_one = LineSum(
        place, part, inbox, result, sems[2 * n_line : 3 * n_line], cfg.pieces, root_one
    )
    load_part.wait()
    line_three.early_start()

    def grad_down(i):
        rows = aligned(i, units // 4)
        down[rows] = dot(act[:, rows], dy_all[...], TN).astype(BF16)

    def grad_gate_up(i):
        product = dot(n2_all[...], dgu[:, aligned(i, chunk)], TN).astype(BF16)

        @pl.when(i < 6)
        def _():
            gu_rows[:, aligned(lax.rem(i, 2) * 4 + lax.div(i, 2), chunk)] = product

        @pl.when(i >= 6)
        def _():
            gu_rows[:, aligned(i, chunk // 2)] = product[:, : chunk // 2]
            gu_rows[:, aligned(8 + i, chunk // 2)] = product[:, chunk // 2 :]

    def lines(n):
        line_three.round(n)
        line_two.round(n - cfg.behind)

    def between(fill, rounds, fills, count=4):
        def one(i, carry):
            lines(rounds + i)
            fill(fills + i)
            return carry

        lax.fori_loop(0, count, one, 0)

    for copy in first:
        copy.wait()
    between(grad_down, 0, 0)
    s_down.start()
    tables(place, lengths, freq, cosine, sine, tokens)
    fill_bias(place, lengths, bias, tokens)
    for copy in second + third:
        copy.wait()
    between(grad_gate_up, 4, 0)
    between(grad_gate_up, 8, 4, 3)
    line_two.early_start()
    between(grad_gate_up, 11, 7, 1)
    pl.semaphore_signal(ready, inc=1, device_id=place.core, device_id_type=MESH)
    rest = [
        fetch(wo_in, wo),
        fetch(x_in, x),
        fetch(mixed_in, mixed_all.at[pl.ds(0, tokens)]),
    ]
    for phase in range(place.bits - 1, 0, -1):
        s_down.pass_on(phase)
    s_gu.start()
    lines(12)
    pl.semaphore_wait(ready, 1)
    swaps, owns, db_swaps, db_owns = [], [], [], []

    def swap(source, target, k, q, kept):
        copy = remote(source, target, swap_send.at[k, q], swap_receive.at[k, q], place.core)
        copy.start()
        kept.append(copy)

    def own(source, target, k, q, kept):
        copy = pltpu.make_async_copy(source, target, own_sem.at[k, q])
        copy.start()
        kept.append(copy)

    def shares(q):
        return pl.ds(q * block, block), aligned(2 * q + 1 - place.c, block), aligned(2 * q + place.c, block)

    for q in range(owners):
        columns, theirs, ours = shares(q)
        swap(normed_in.at[:, theirs], normed_all.at[pl.ds(tokens, tokens), columns], 0, q, swaps)
        own(normed_in.at[:, ours], normed_all.at[pl.ds(0, tokens), columns], 0, q, owns)
    swap(mixed_in, mixed_all.at[pl.ds(tokens, tokens)], 3, 0, swaps)
    lines(13)
    lines(14)
    db = result
    for b in range(2):
        for q in range(owners):
            columns, theirs, ours = shares(q)
            target = pl.ds(tokens + b * QROWS, QROWS)
            swap(db.at[b, :, theirs], db_all.at[target, columns], 1 + b, q, db_swaps)
            target = pl.ds(b * QROWS, QROWS)
            own(db.at[b, :, ours], db_all.at[target, columns], 1 + b, q, db_owns)
    for copy in rest:
        copy.wait()

    def back_out(b, carry):
        product = dot(db[b], wo[...], NT)
        rows = aligned(b, QROWS)
        for h in range(heads):
            dmixed[h, rows] = product[:, h * HD : (h + 1) * HD].astype(BF16)
        return carry

    lax.fori_loop(0, 2, back_out, 0)
    dk[...] = jnp.zeros_like(dk)
    dv[...] = jnp.zeros_like(dv)

    def attend_back(b, rounds):
        rows = aligned(b, QROWS)
        window = pl.ds(pl.multiple_of(place.c * b * QROWS, QROWS), bias.shape[1])

        def pair(j, carry):
            outs = []
            for h in range(2):
                head = 2 * j + h
                g = lax.div(head, heads // groups)
                key, value = kh[g, window], vh[g, window]
                query, grad = qh[head, rows], dmixed[head, rows]
                weights = softmax_of(key, query, bias[b])
                dprobs = dot(value, grad, NT)
                delta = jnp.sum(weights * dprobs, 0, keepdims=True)
                dscores = (weights * (dprobs - delta)).astype(BF16)
                dv[g, window] += dot(weights.astype(BF16), grad)
                dk[g, window] += dot(dscores, query)
                outs.append(dot(key, dscores, TN))
            z = jnp.concatenate(outs, 0).T * HD**-0.5
            z = z * cosine[rows] - turned(z) * sine[rows]
            dqkv[rows, aligned(j, 128)] = z.astype(BF16)
            line_two.round(rounds + j)
            return carry

        lax.fori_loop(0, heads // 2, pair, 0)

    done = line_three.rounds - cfg.behind
    attend_back(place.early, done)
    for copy in db_owns + owns:
        copy.wait()
    for copy in db_swaps + swaps:
        copy.wait_recv()
        copy.wait_send()
    s_down.finish()
    load_qkv = fetch(qkv_in, wqkv)
    out_columns[...] = dot(mixed_all[...], db_all[...], TN).astype(BF16)
    s_out.start()
    attend_back(place.late, done + heads // 2)
    done = done + heads
    stores = []

    def keep(source, target):
        copy = pltpu.make_async_copy(source, target, store.at[len(stores)])
        copy.start()
        stores.append(copy)

    pass_back = remote(dkv, dkv_in, dkv_send.at[0], dkv_receive.at[0], place.core)

    def packed(rows):
        return jnp.concatenate(
            [dk[g, rows] for g in range(groups)] + [dv[g, rows] for g in range(groups)], -1
        )

    @pl.when(place.c == 1)
    def _():
        dkv[...] = packed(pl.ds(0, tokens))
        pass_back.start()

    own_rows = aligned(place.c, tokens)
    z = packed(own_rows)

    @pl.when(place.c == 0)
    def _():
        pass_back.wait_recv()
        dkv[...] = z + dkv_in[...]

    @pl.when(place.c == 1)
    def _():
        pass_back.wait_send()
        dkv[...] = z

    dkeys = dkv[:, :key_width]
    if key_width % 128 == 0:
        wide_by = key_width // 128
        table_c = jnp.concatenate([cosine[...]] * wide_by, -1)
        table_s = jnp.concatenate([sine[...]] * wide_by, -1)
    else:
        table_c, table_s = cosine[:, :key_width], sine[:, :key_width]
    dkeys = dkeys * table_c - turned(dkeys) * table_s
    dqkv[:tokens, query_width : query_width + key_width] = dkeys.astype(BF16)
    dqkv[:tokens, query_width + key_width :] = dkv[:, key_width:].astype(BF16)
    late_swaps = []
    swap(dqkv.at[pl.ds(0, tokens)], dqkv.at[pl.ds(tokens, tokens)], 3, 1, late_swaps)
    load_qkv.wait()
    columns_at = width // 4

    def back_through(b):
        def one(i, carry):
            rows, columns = aligned(b, QROWS), aligned(i, columns_at)
            part[b, :, columns] = dot(dqkv[rows], wqkv[columns], NT).astype(BF16)
            return carry

        lax.fori_loop(0, 4, one, 0)

    def run_lines(start, stop):
        def one(n, carry):
            line_one.round(n)
            line_two.round(done + n)
            return carry

        lax.fori_loop(start, stop, one, 0)

    line_three.drain()
    back_through(place.early)
    line_one.early_start()
    back_through(place.late)
    run_lines(0, 1)
    for copy in late_swaps:
        copy.wait_recv()
    qkv_rows[...] = dot(normed_all[...], dqkv[...], TN).astype(BF16)
    s_qkv.start()
    run_lines(1, 4)
    agenda = []
    for phase in range(place.bits - 1, 0, -1):
        for s in (s_gu, s_out, s_qkv):
            agenda.append(functools.partial(s.pass_on, phase))
    last_sum = cfg.pieces + line_one.lags[1]
    marks = [4 + (last_sum - 4) * (k + 1) // (len(agenda) + 1) for k in range(len(agenda))]
    at = 4
    for mark, item in zip(marks, agenda):
        run_lines(at, mark)
        item()
        at = mark
    run_lines(at, last_sum)

    ends = (0, cfg.tensor - 1)
    mine = place.p * 2 + place.c

    def gain_copy(mask, core):
        index = place.flipped(mask) * 2 + core
        return remote(
            gain_rows.at[:, aligned(index, block)],
            gain_box.at[mine],
            gain_send.at[mask, lax.rem(core + place.c, 2)],
            gain_receive.at[mask, lax.rem(core + place.c, 2)],
            (place.flipped(mask), core, place.t),
        )

    others = [(mask, core) for mask in range(cfg.dp) for core in range(2)]

    @pl.when(place.at_end)
    def _():
        gain_rows[0:1, :] = jnp.sum(gain_one[...], 0, keepdims=True)
        gain_rows[1:2, :] = jnp.sum(gain_two[...], 0, keepdims=True)
        gain_rows[2:, :] = jnp.zeros((6, width), F32)
        for mask in range(cfg.dp):
            for apart in range(2):
                if mask or apart:
                    core = place.c if apart == 0 else 1 - place.c
                    gain_copy(mask, core).start()
        gain_box[mine] = gain_rows[:, aligned(mine, block)]

    run_lines(last_sum, line_one.rounds - 2)

    def line_copy(step, end):
        return remote(
            gain_line.at[end],
            gain_line.at[end],
            last_send.at[step],
            last_receive.at[end],
            (place.p, place.c, lax.rem(place.t + step, cfg.tensor)),
        )

    for end, at_t in enumerate(ends):

        @pl.when(place.t == at_t)
        def _(end=end):
            for mask in range(cfg.dp):
                for apart in range(2):
                    if mask or apart:
                        core = place.c if apart == 0 else 1 - place.c
                        gain_copy(mask, core).wait_recv()
            gain_line[end] = jnp.sum(gain_box[...], 0)
            for step in range(1, cfg.tensor):
                line_copy(step, end).start()

    run_lines(line_one.rounds - 2, line_one.rounds)
    keep(result, grad_out)
    line_two.run(done + line_one.rounds, line_two.rounds)
    keep(final, activations_out)
    for end, at_t in enumerate(ends):

        @pl.when(place.t != at_t)
        def _(end=end):
            line_copy(1, end).wait_recv()

    gain_one[:, :block] = gain_line[0] + gain_line[1]
    keep(gain_one.at[:, pl.ds(0, block)], gain_out)
    for s in scatters[1:]:
        s.finish()

    @pl.when(place.at_end)
    def _():
        for mask in range(cfg.dp):
            for apart in range(2):
                if mask or apart:
                    core = place.c if apart == 0 else 1 - place.c
                    gain_copy(mask, core).wait_send()
        for step in range(1, cfg.tensor):
            line_copy(step, 0).wait_send()

    for copy in late_swaps:
        copy.wait_send()
    line_two.drain()
    line_one.drain()
    for copy in stores:
        copy.wait()


def backward_call(cfg, *operands):
    tokens, width, units = cfg.tokens, cfg.width, cfg.hidden_units
    any_spec = pl.BlockSpec(memory_space=pl.ANY)
    shape = jax.ShapeDtypeStruct
    bits = cfg.dp.bit_length() - 1
    mine = cfg.dp * cfg.block
    heads, groups, qkv_width = cfg.heads, cfg.groups, cfg.qkv_width
    outs = [
        shape((2, QROWS, width), BF16),
        shape((2, QROWS, width), BF16),
        shape((1 + bits, units, cfg.block), BF16),
        shape((1 + bits, cfg.block, 2 * units), BF16),
        shape((1 + bits, cfg.block, qkv_width), BF16),
        shape((1 + bits, cfg.query_width, cfg.block), BF16),
        shape((8, cfg.block), F32),
    ]
    halves = (2, QROWS, width)
    scratch = [
        pltpu.VMEM((tokens, width), BF16),
        pltpu.VMEM((QROWS, width), F32),
        pltpu.VMEM((QROWS, width), F32),
        pltpu.VMEM((16, width), BF16),
        pltpu.VMEM((2 * tokens, mine), BF16),
        pltpu.VMEM((2 * tokens, mine), BF16),
        pltpu.VMEM((2 * tokens, units), BF16),
        pltpu.VMEM((2 * tokens, 2 * units), BF16),
        pltpu.VMEM((mine, 2 * units), BF16),
        pltpu.VMEM((units, mine), BF16),
    ]
    scratch += [pltpu.VMEM(halves, BF16)] * 6
    scratch += [
        pltpu.VMEM(Scatter.inbox_shape(cfg.dp, units, cfg.block), BF16),
        pltpu.VMEM(Scatter.inbox_shape(cfg.dp, cfg.block, 2 * units), BF16),
        pltpu.VMEM(Scatter.inbox_shape(cfg.dp, cfg.block, qkv_width), BF16),
        pltpu.VMEM(Scatter.inbox_shape(cfg.dp, cfg.query_width, cfg.block), BF16),
        pltpu.VMEM((heads, tokens, HD), BF16),
        pltpu.VMEM((groups, 2 * tokens, HD), BF16),
        pltpu.VMEM((groups, 2 * tokens, HD), BF16),
        pltpu.VMEM((heads, tokens, HD), BF16),
        pltpu.VMEM((groups, 2 * tokens, HD), F32),
        pltpu.VMEM((groups, 2 * tokens, HD), F32),
        pltpu.VMEM((tokens, 2 * cfg.key_width), F32),
        pltpu.VMEM((tokens, 2 * cfg.key_width), F32),
        pltpu.VMEM((tokens, 128), F32),
        pltpu.VMEM((tokens, 128), F32),
        pltpu.VMEM((2, cfg.window, QROWS), F32),
        pltpu.VMEM((8, width), F32),
        pltpu.VMEM((8, width), F32),
        pltpu.VMEM((8, width), F32),
        pltpu.VMEM((2 * cfg.dp, 8, cfg.block), F32),
        pltpu.VMEM((2, 8, cfg.block), F32),
        pltpu.SemaphoreType.DMA((16,)),
        pltpu.SemaphoreType.DMA((3,)),
        pltpu.SemaphoreType.DMA((3, cfg.dp)),
        pltpu.SemaphoreType.DMA((4, max(cfg.dp, 2))),
        pltpu.SemaphoreType.DMA((4, max(cfg.dp, 2))),
        pltpu.SemaphoreType.DMA((1,)),
        pltpu.SemaphoreType.DMA((1,)),
        pltpu.SemaphoreType.DMA((cfg.dp, 2)),
        pltpu.SemaphoreType.DMA((cfg.dp, 2)),
        pltpu.SemaphoreType.DMA((cfg.tensor,)),
        pltpu.SemaphoreType.DMA((2,)),
        pltpu.SemaphoreType.REGULAR,
    ]
    scratch += LineSum.semaphores(cfg.pieces) * 3
    scratch += Scatter.semaphores(cfg.dp) * 4
    at = 0
    for columns in (mine, mine, qkv_width, qkv_width, cfg.query_width):
        if 2 * units < at + columns:
            scratch.append(pltpu.VMEM((2 * tokens, columns), BF16))
        at += columns
    if units < width:
        scratch.append(pltpu.VMEM((tokens, width), BF16))
    if units < width or 2 * tokens < tokens + cfg.query_width:
        scratch.append(pltpu.VMEM((cfg.query_width, width), BF16))
    if units < width or mine < qkv_width:
        scratch.append(pltpu.VMEM((width, qkv_width), BF16))
    if 2 * tokens < cfg.query_width:
        scratch.append(pltpu.VMEM((cfg.query_width, mine), BF16))
    in_specs = [any_spec] * 17 + [
        pl.BlockSpec(memory_space=pltpu.SMEM),
        pl.BlockSpec(memory_space=pltpu.VMEM),
    ]
    return pl.pallas_call(
        functools.partial(backward_kernel, cfg),
        out_shape=outs,
        in_specs=in_specs,
        out_specs=[any_spec] * len(outs),
        scratch_shapes=scratch,
        compiler_params=pltpu.CompilerParams(
            collective_id=3, has_side_effects=True, vmem_limit_bytes=VMEM_LIMIT
        ),
        name="backward",
    )(*operands)


def solution(mesh):
    dp, tensor = mesh.shape["dp"], mesh.shape["tensor"]

    def shards(
        inputs, cotangent, doc_lengths, gain_attn, w_query, w_key, w_value, w_out, gain_mlp,
        w_gate, w_up, w_down,
    ):
        tokens, width = inputs.shape
        cfg = Config(
            dp,
            tensor,
            tokens,
            width,
            w_query.shape[1] // HD,
            w_key.shape[1] // HD,
            w_gate.shape[1],
        )
        freq = jnp.asarray(np.tile(frequencies(), (8, 4)), F32)
        gains = (gain_attn.reshape(1, -1), gain_mlp.reshape(1, -1))
        (
            _, _, wqkv, wo, gains_full, normed, q, k, v, mixed, hidden,
            n2_all, dy_all, act_all, dgu_all, dn2, terms,
        ) = forward_call(
            cfg, inputs, cotangent, doc_lengths, freq, *gains,
            w_query, w_key, w_value, w_out, w_gate, w_up, w_down,
        )
        (
            activations, input_grad, down_terms, gu_terms, qkv_terms, out_terms, gain_sums,
        ) = backward_call(
            cfg, dn2, n2_all, dy_all, act_all, dgu_all, cotangent, hidden, terms,
            mixed, wo, wqkv, q, k, v, normed, inputs, gains_full, doc_lengths, freq,
        )

        def total(pieces):
            return jnp.sum(pieces.astype(F32), 0)

        qkv_grad = total(qkv_terms)
        units = cfg.hidden_units
        query_width, key_width = cfg.query_width, cfg.key_width
        return (
            activations.reshape(tokens, width),
            input_grad.reshape(tokens, width).astype(F32),
            gain_sums[0],
            qkv_grad[:, :query_width],
            qkv_grad[:, query_width : query_width + key_width],
            qkv_grad[:, query_width + key_width :],
            total(out_terms),
            gain_sums[1],
            total(gu_terms[:, :, :units]),
            total(gu_terms[:, :, units:]),
            total(down_terms),
        )

    rows, columns, gain = P(("dp", "context"), "tensor"), P("tensor", ("dp", "context")), P(("dp", "context"))
    tokens = P(("dp", "context"), None)
    return jax.shard_map(
        shards,
        mesh=mesh,
        in_specs=(tokens, tokens, P("dp", None), gain, rows, rows, rows, columns, gain, rows, rows, columns),
        out_specs=(tokens, tokens, gain, rows, rows, rows, columns, gain, rows, rows, columns),
        check_vma=False,
    )
```
